128 devices in a mesh: row: 16 (over x_lo, z, core), col: 8 (over x_hi, y).
Axes of the slice: x: 4 (x_hi: 2, x_lo: 2; x = x_hi * 2 + x_lo), y: 4, z: 4, core: 2. Of those that a mesh axis runs over, the one named last changes fastest.
Arguments:
- matrix_tiles: float32 [5, 16, 128, 10, 8, 128], P(None, 'row', None, None, 'col'), may hold values from -60715.73 to 60715.73
Outputs:
- reduced: float32 [5, 16, 128, 10, 8, 128], P(None, 'row', None, None, 'col')
The draws below stay inside these ranges and needn't reach their ends.
All inputs are finite; a program needn't handle non-finite values.
Results may differ from the reference program's by a relative error of at most 0.0003.
Values sent between devices are 32-bit elements; how exact they have to be, the bound alone decides.
No kernel may reach another device: no remote copies, remote signals or barrier semaphores. Data moves between devices by JAX's collectives and lax.ppermute only.
A program may use at most 128 MiB of HBM per device.

```python
import jax
import jax.numpy as jnp
from jax import lax

ORDER = 10240
TILE = 128
BAND = 256
PANELS = 2
ROW_BLOCKS = 5
COL_BLOCKS = 10
N_ROW = 16
N_COL = 8


def draw_matrix_tiles(key, part):
    first_key = jax.random.fold_in(key, 11)
    common_key = jax.random.fold_in(key, 37)
    common = jax.random.uniform(common_key, (ORDER,), jnp.float32, -1.7320508, 1.7320508)
    base_values = jnp.clip(jax.random.normal(first_key, (ORDER, ORDER), jnp.float32), -6.0, 6.0)
    symmetric = (base_values + base_values.T) * 0.70710678
    symmetric = symmetric + 2.0 * common[:, None] * common[None, :]
    column_norms = jnp.sqrt(jnp.sum(symmetric * symmetric, axis=0))
    offsets = jnp.arange(BAND, dtype=jnp.int32)
    for panel_index in range(PANELS):
        start_col = panel_index * BAND
        start_row = start_col + BAND
        boost_values = 2.0 * column_norms[start_col + offsets]
        symmetric = symmetric.at[start_row + offsets, start_col + offsets].add(boost_values)
        symmetric = symmetric.at[start_col + offsets, start_row + offsets].add(boost_values)
    return symmetric.reshape(ROW_BLOCKS, N_ROW, TILE, COL_BLOCKS, N_COL, TILE)


def setup_inputs(seed: int = 0) -> dict:
    keys = jax.random.split(jax.random.key(seed), 2)
    matrix_tiles = draw_matrix_tiles(jax.random.fold_in(keys[1], 71), 0)
    return dict(matrix_tiles=matrix_tiles)


def multiply(first_matrix, second_matrix):
    return jnp.dot(first_matrix, second_matrix, precision=lax.Precision.HIGHEST, preferred_element_type=first_matrix.dtype)

def transposed_left(first_matrix, second_matrix):
    return lax.dot_general(first_matrix, second_matrix, (((0,), (0,)), ((), ())), precision=lax.Precision.HIGHEST, preferred_element_type=first_matrix.dtype)

def transposed_right(first_matrix, second_matrix):
    return lax.dot_general(first_matrix, second_matrix, (((1,), (1,)), ((), ())), precision=lax.Precision.HIGHEST, preferred_element_type=first_matrix.dtype)

def lower_inverse(matrix):
    factor = jnp.linalg.cholesky(matrix)
    identity = jnp.eye(matrix.shape[0], dtype=matrix.dtype)
    return lax.linalg.triangular_solve(factor, identity, left_side=True, lower=True)

def reflector_factors(gram_matrix, top_panel):
    inverse = lower_inverse(gram_matrix)
    top_basis = transposed_right(top_panel, inverse)
    sign_values = jnp.where(jnp.diagonal(top_basis) >= 0, -1.0, 1.0).astype(top_basis.dtype)
    shifted = top_basis - jnp.diag(sign_values)
    outer_inverse = lower_inverse(transposed_left(shifted, shifted))
    kernel = transposed_left(outer_inverse, outer_inverse)
    transform = -sign_values[:, None] * multiply(shifted, kernel)
    return (inverse, sign_values, transform)

def reference(matrix_tiles):
    tile_shape = matrix_tiles.shape
    order_size = tile_shape[0] * tile_shape[1] * tile_shape[2]
    matrix = matrix_tiles.reshape(order_size, order_size)
    for panel_index in range(PANELS):
        panel_start = panel_index * BAND
        below_start = panel_start + BAND
        panel_block = matrix[below_start:, panel_start:below_start]
        gram_matrix = transposed_left(panel_block, panel_block)
        inverse, sign_values, transform = reflector_factors(gram_matrix, panel_block[:BAND])
        basis_rows = transposed_right(panel_block, inverse)
        basis_rows = basis_rows.at[:BAND].add(-jnp.diag(sign_values))
        vectors = jnp.concatenate([jnp.zeros((below_start, BAND), matrix.dtype), basis_rows], 0)
        applied = multiply(multiply(matrix, vectors), transform)
        inner_term = multiply(transform.T, transposed_left(vectors, applied))
        updates = applied - 0.5 * multiply(vectors, inner_term)
        matrix = matrix - transposed_right(jnp.concatenate([vectors, updates], 1), jnp.concatenate([updates, vectors], 1))
    return matrix.reshape(tile_shape)
```

```python
import jax
import jax.numpy as jnp
from jax import lax
from jax.experimental import pallas as pl
from jax.experimental.pallas import tpu as pltpu
from jax.sharding import Mesh
from jax.sharding import PartitionSpec as P

PANELS = 2
PAIR = ("x_lo", "z")
CORE = "core"
ROW = ("x_lo", "z", "core")
COL = ("x_hi", "y")
HI = lax.Precision.HIGHEST

def mm(a, b):
    return lax.dot_general(a, b, (((1,), (0,)), ((), ())), precision=HI, preferred_element_type=jnp.float32)
def mm_nt(a, b):
    return lax.dot_general(a, b, (((1,), (1,)), ((), ())), precision=HI, preferred_element_type=jnp.float32)

STEP = 8

def entries(block):
    columns = [jnp.broadcast_to(block[:, j:j + 1], (STEP, 128)) for j in range(STEP)]
    return [[jnp.broadcast_to(columns[j][i:i + 1, :], (STEP, 128)) for j in range(STEP)] for i in range(STEP)]

def as_columns(x, sub):
    out = []
    for j in range(STEP):
        col = jnp.zeros((STEP, 128), jnp.float32)
        for i in range(STEP):
            if x[i][j] is not None:
                col = jnp.where(sub == i, x[i][j], col)
        out.append(col)
    return out

def apply(cols, rows):
    n = rows.shape[1]
    parts = []
    for c in range(0, n, 128):
        acc = None
        for j in range(STEP):
            t = cols[j] * rows[j:j + 1, c:c + 128]
            acc = t if acc is None else acc + t
        parts.append(acc)
    return jnp.concatenate(parts, 1)

def chol_inverse_8(e):
    x = [[None] * STEP for _ in range(STEP)]
    l = [[None] * STEP for _ in range(STEP)]
    a = [[e[i][j] for j in range(STEP)] for i in range(STEP)]
    inv = [None] * STEP
    for k in range(STEP):
        inv[k] = 1.0 / jnp.sqrt(a[k][k])
        for i in range(k + 1, STEP):
            l[i][k] = a[i][k] * inv[k]
        for j in range(k + 1, STEP):
            for i in range(j, STEP):
                a[i][j] = a[i][j] - l[i][k] * l[j][k]
        x[k][k] = inv[k]
        for j in range(k):
            s = None
            for q in range(j, k):
                t = l[k][q] * x[q][j]
                s = t if s is None else s + t
            x[k][j] = -s * inv[k]
    return x

def inverse_8(e):
    a = [[e[i][j] for j in range(STEP)] for i in range(STEP)]
    for k in range(STEP):
        p = 1.0 / a[k][k]
        a[k] = [a[k][j] * p if j != k else p for j in range(STEP)]
        for i in range(STEP):
            if i == k:
                continue
            f = a[i][k]
            a[i] = [a[i][j] - f * a[k][j] if j != k else -f * p for j in range(STEP)]
    return a

def eliminate(m_ref, n, symmetric):
    lanes8 = lax.broadcasted_iota(jnp.int32, (STEP, n), 1)
    subs8 = lax.broadcasted_iota(jnp.int32, (STEP, n), 0)
    sub = lax.broadcasted_iota(jnp.int32, (STEP, 128), 0)
    lanes = lax.broadcasted_iota(jnp.int32, (n, n), 1)
    rows_of = lax.broadcasted_iota(jnp.int32, (n, n), 0)

    def body(k, _):
        at = pl.multiple_of(k * STEP, STEP)
        rows = m_ref[pl.ds(at, STEP), :]
        block = pltpu.roll(rows, n - at, 1)[:, :STEP]
        here = (lanes8 >= at) & (lanes8 < at + STEP)
        e = entries(block)
        unit = jnp.where(here, (lanes8 - at == subs8).astype(jnp.float32), rows)
        if symmetric:
            x = chol_inverse_8(e)
            kept = apply(as_columns(x, sub), unit)
            xt = [[x[j][i] for j in range(STEP)] for i in range(STEP)]
            spread = apply(as_columns(xt, sub), kept)
        else:
            spread = kept = apply(as_columns(inverse_8(e), sub), unit)
        m = m_ref[...]
        inside = (lanes >= at) & (lanes < at + STEP)
        other = (rows_of >= at + STEP) if symmetric else ((rows_of < at) | (rows_of >= at + STEP))
        left = jnp.where(inside & other, m, 0.0)
        full = jnp.concatenate([spread] * (n // STEP), 0)
        full = jnp.where((rows_of >= at) & (rows_of < at + STEP), full, 0.0)
        m_ref[...] = jnp.where(inside & other, 0.0, m) - mm(left, full)
        m_ref[pl.ds(at, STEP), :] = kept
        return 0

    lax.fori_loop(0, n // STEP, body, 0)

def factor_kernel(gram_ref, top_ref, inv_ref, sign_ref, tf_ref, m_ref):
    n = gram_ref.shape[0]
    r = lax.broadcasted_iota(jnp.int32, (n, n), 0)
    c = lax.broadcasted_iota(jnp.int32, (n, n), 1)
    m_ref[...] = gram_ref[...]
    eliminate(m_ref, n, True)
    inv = jnp.where(r >= c, m_ref[...], 0.0)
    inv_ref[...] = inv
    q1t = mm_nt(inv, top_ref[...])
    diag = jnp.sum(jnp.where(r == c, q1t, 0.0), axis=0, keepdims=True)
    sign = jnp.where(diag >= 0, -1.0, 1.0)
    sign_ref[...] = sign
    m_ref[...] = (r == c).astype(jnp.float32) - q1t * sign
    eliminate(m_ref, n, False)
    tf_ref[...] = m_ref[...]

def factors(gram, top):
    n = gram.shape[0]
    f32 = jnp.float32
    return pl.pallas_call(
        factor_kernel,
        out_shape=[jax.ShapeDtypeStruct((n, n), f32), jax.ShapeDtypeStruct((1, n), f32), jax.ShapeDtypeStruct((n, n), f32)],
        scratch_shapes=[pltpu.VMEM((n, n), f32)],
        compiler_params=pltpu.CompilerParams(vmem_limit_bytes=32 * 2**20),
        cost_estimate=pl.CostEstimate(flops=2 * 64 * n**3, bytes_accessed=20 * n * n, transcendentals=0),
    )(gram, top)


def mm_tn(a, b):
    return lax.dot_general(a, b, (((0,), (0,)), ((), ())), precision=HI, preferred_element_type=jnp.float32)


def swap(x, axis):
    return lax.all_to_all(x, axis, 0, 0, tiled=True)


def gathered(x, axis):
    return swap(jnp.broadcast_to(x[None], (lax.axis_size(axis), *x.shape)), axis)


def other_core(x):
    return lax.ppermute(x, CORE, [(0, 1), (1, 0)])


def in_core_order(mine, core, axis):
    theirs = other_core(mine)
    first = core == 0
    return jnp.stack([jnp.where(first, mine, theirs), jnp.where(first, theirs, mine)], axis)


def to_mirror(piece):
    rows, cols = lax.axis_size(ROW), lax.axis_size(COL)
    pairs = []
    for r in range(rows):
        for c in range(cols):
            to_row, to_col = r // cols * cols + c, r % cols
            pairs.append((r * cols + c, to_row * cols + to_col))
    return lax.ppermute(piece, ROW + COL, pairs)


def cut_rows(x, blocks, peers):
    width = x.shape[-1]
    return x.reshape(blocks, peers, -1, width).transpose(1, 0, 2, 3).reshape(peers, -1, width)


def joined_rows(slabs, blocks):
    peers, _, width = slabs.shape
    return slabs.reshape(peers, blocks, -1, width).transpose(1, 0, 2, 3).reshape(-1, width)


def mirror_rows(mine, core, blocks):
    far, near = lax.axis_size("x_lo"), lax.axis_size("z")
    width = mine.shape[-1]
    both = in_core_order(mine.reshape(far, near, blocks, -1, width), core, 2)
    return both.transpose(3, 0, 1, 2, 4, 5).reshape(-1, width)


def on_device(matrix_tiles):
    tile_shape = matrix_tiles.shape
    blocks, tile, wide = tile_shape[0], tile_shape[2], tile_shape[3]
    band = 2 * tile
    rows, cols = lax.axis_size(ROW), lax.axis_size(COL)
    r, c, core = lax.axis_index(ROW), lax.axis_index(COL), lax.axis_index(CORE)
    a = matrix_tiles.reshape(blocks * tile, wide * tile)
    slab = blocks * tile // cols
    part = band // cols

    def places(count, peers, me):
        at = jnp.arange(count, dtype=jnp.int32)
        return (at // tile * peers + me) * tile + at % tile

    row_of, col_of = places(blocks * tile, rows, r), places(wide * tile, cols, c)
    lane = jnp.arange(band, dtype=jnp.int32)
    for panel in range(PANELS):
        start, below = panel * band, (panel + 1) * band
        source = cut_rows(a[:, :tile], blocks, cols)
        source = swap(source, COL)
        first = start // tile
        piece = jnp.concatenate([source[first], source[first + 1]], 1)
        mirrored = to_mirror(piece)
        p_rows = joined_rows(gathered(piece, COL), blocks)
        p_cols = mirror_rows(gathered(mirrored, PAIR), core, blocks)
        p_rows = jnp.where((row_of >= below)[:, None], p_rows, 0.0)
        p_cols = jnp.where((col_of >= below)[:, None], p_cols, 0.0)

        gram = mm_tn(p_cols, p_cols).reshape(cols, part, band)
        top = jnp.concatenate(
            [jnp.where(c == below // tile + i, p_cols[:tile], 0.0) for i in range(2)], 0
        ).reshape(cols, part, band)
        summed = swap(jnp.concatenate([gram, top], 1), COL).sum(0)
        summed = gathered(summed, COL)
        gram, top = summed[:, :part].reshape(band, band), summed[:, part:].reshape(band, band)
        inverse, sign, tf = factors(gram, top)

        y_rows = mm_nt(p_rows, inverse) - jnp.where(row_of[:, None] - below == lane[None, :], sign, 0.0)
        y_cols = mm_nt(p_cols, inverse) - jnp.where(col_of[:, None] - below == lane[None, :], sign, 0.0)
        u = mm(a, y_cols)
        h = mm_tn(y_rows, u).reshape(cols, part, band)
        sent = jnp.concatenate([cut_rows(u, blocks, cols), h], 1)
        summed = swap(sent, COL).sum(0)
        piece, h = summed[:slab], summed[slab:]
        arrived = gathered(jnp.concatenate([to_mirror(piece), h], 0), PAIR)
        h = arrived[:, slab:].sum(0)
        h = h + other_core(h)
        u_cols = mirror_rows(arrived[:, :slab], core, blocks)
        arrived = gathered(jnp.concatenate([piece, h], 0), COL)
        u_rows = joined_rows(arrived[:, :slab], blocks)
        h = arrived[:, slab:].reshape(band, band)
        half_z = 0.5 * mm_tn(tf, mm(h, tf))
        w_rows = mm(u_rows, tf) - mm(y_rows, half_z)
        w_cols = mm(u_cols, tf) - mm(y_cols, half_z)
        a = a - mm_nt(jnp.concatenate([y_rows, w_rows], 1), jnp.concatenate([w_cols, y_cols], 1))
    return a.reshape(tile_shape)


def solution(mesh):
    finer = Mesh(mesh.devices.reshape(2, 4, 2, 2, 4), ("x_lo", "z", "core", "x_hi", "y"))
    spec = P(None, ROW, None, None, COL, None)
    return jax.shard_map(on_device, mesh=finer, in_specs=(spec,), out_specs=spec, check_vma=False)
```

```python
import functools

import jax
import jax.numpy as jnp
from jax import lax
from jax.experimental import pallas as pl
from jax.experimental.pallas import tpu as pltpu
from jax.sharding import Mesh
from jax.sharding import PartitionSpec as P

PANELS = 2
PAIR = ("x_lo", "z")
CORE = "core"
ROW = ("x_lo", "z", "core")
COL = ("x_hi", "y")
HI = lax.Precision.HIGHEST

def mm(a, b):
    return lax.dot_general(a, b, (((1,), (0,)), ((), ())), precision=HI, preferred_element_type=jnp.float32)
def mm_nt(a, b):
    return lax.dot_general(a, b, (((1,), (1,)), ((), ())), precision=HI, preferred_element_type=jnp.float32)

STEP = 8

def entries(block):
    columns = [jnp.broadcast_to(block[:, j:j + 1], (STEP, 128)) for j in range(STEP)]
    return [[jnp.broadcast_to(columns[j][i:i + 1, :], (STEP, 128)) for j in range(STEP)] for i in range(STEP)]

def as_columns(x, sub):
    out = []
    for j in range(STEP):
        col = jnp.zeros((STEP, 128), jnp.float32)
        for i in range(STEP):
            if x[i][j] is not None:
                col = jnp.where(sub == i, x[i][j], col)
        out.append(col)
    return out

def apply(cols, rows):
    n = rows.shape[1]
    parts = []
    for c in range(0, n, 128):
        acc = None
        for j in range(STEP):
            t = cols[j] * rows[j:j + 1, c:c + 128]
            acc = t if acc is None else acc + t
        parts.append(acc)
    return jnp.concatenate(parts, 1)

def chol_inverse_8(e):
    x = [[None] * STEP for _ in range(STEP)]
    l = [[None] * STEP for _ in range(STEP)]
    a = [[e[i][j] for j in range(STEP)] for i in range(STEP)]
    inv = [None] * STEP
    for k in range(STEP):
        inv[k] = 1.0 / jnp.sqrt(a[k][k])
        for i in range(k + 1, STEP):
            l[i][k] = a[i][k] * inv[k]
        for j in range(k + 1, STEP):
            for i in range(j, STEP):
                a[i][j] = a[i][j] - l[i][k] * l[j][k]
        x[k][k] = inv[k]
        for j in range(k):
            s = None
            for q in range(j, k):
                t = l[k][q] * x[q][j]
                s = t if s is None else s + t
            x[k][j] = -s * inv[k]
    return x

def inverse_8(e):
    a = [[e[i][j] for j in range(STEP)] for i in range(STEP)]
    for k in range(STEP):
        p = 1.0 / a[k][k]
        a[k] = [a[k][j] * p if j != k else p for j in range(STEP)]
        for i in range(STEP):
            if i == k:
                continue
            f = a[i][k]
            a[i] = [a[i][j] - f * a[k][j] if j != k else -f * p for j in range(STEP)]
    return a

def eliminate(m_ref, n, symmetric, steps):
    lanes8 = lax.broadcasted_iota(jnp.int32, (STEP, n), 1)
    subs8 = lax.broadcasted_iota(jnp.int32, (STEP, n), 0)
    sub = lax.broadcasted_iota(jnp.int32, (STEP, 128), 0)
    lanes = lax.broadcasted_iota(jnp.int32, (n, n), 1)
    rows_of = lax.broadcasted_iota(jnp.int32, (n, n), 0)

    def body(k, _):
        at = pl.multiple_of(k * STEP, STEP)
        rows = m_ref[pl.ds(at, STEP), :]
        block = pltpu.roll(rows, n - at, 1)[:, :STEP]
        here = (lanes8 >= at) & (lanes8 < at + STEP)
        e = entries(block)
        unit = jnp.where(here, (lanes8 - at == subs8).astype(jnp.float32), rows)
        if symmetric:
            x = chol_inverse_8(e)
            kept = apply(as_columns(x, sub), unit)
            xt = [[x[j][i] for j in range(STEP)] for i in range(STEP)]
            spread = apply(as_columns(xt, sub), kept)
        else:
            spread = kept = apply(as_columns(inverse_8(e), sub), unit)
        m = m_ref[...]
        inside = (lanes >= at) & (lanes < at + STEP)
        other = (rows_of >= at + STEP) if symmetric else ((rows_of < at) | (rows_of >= at + STEP))
        left = jnp.where(inside & other, m, 0.0)
        full = jnp.concatenate([spread] * (n // STEP), 0)
        full = jnp.where((rows_of >= at) & (rows_of < at + STEP), full, 0.0)
        m_ref[...] = jnp.where(inside & other, 0.0, m) - mm(left, full)
        m_ref[pl.ds(at, STEP), :] = kept
        return 0

    lax.fori_loop(*steps, body, 0)

def stage_kernel(symmetric, steps, m_ref, out_ref):
    out_ref[...] = m_ref[...]
    eliminate(out_ref, m_ref.shape[0], symmetric, steps)


def last_symmetric_kernel(steps, m_ref, top_ref, inv_ref, sign_ref, next_ref, work_ref):
    n = m_ref.shape[0]
    r = lax.broadcasted_iota(jnp.int32, (n, n), 0)
    c = lax.broadcasted_iota(jnp.int32, (n, n), 1)
    work_ref[...] = m_ref[...]
    eliminate(work_ref, n, True, steps)
    inv = jnp.where(r >= c, work_ref[...], 0.0)
    inv_ref[...] = inv
    q1t = mm_nt(inv, top_ref[...])
    diag = jnp.sum(jnp.where(r == c, q1t, 0.0), axis=0, keepdims=True)
    sign = jnp.where(diag >= 0, -1.0, 1.0)
    sign_ref[...] = sign
    next_ref[...] = (r == c).astype(jnp.float32) - q1t * sign


def cost(n, steps):
    return pl.CostEstimate(flops=STAGE_FLOPS, bytes_accessed=8 * n * n, transcendentals=0)


STAGE_FLOPS = 10**10


def stage(m, symmetric, first, last):
    n = m.shape[0]
    return pl.pallas_call(
        functools.partial(stage_kernel, symmetric, (first, last)),
        out_shape=jax.ShapeDtypeStruct((n, n), jnp.float32),
        compiler_params=pltpu.CompilerParams(vmem_limit_bytes=16 * 2**20),
        cost_estimate=cost(n, last - first),
    )(m)


def last_symmetric(m, top, first):
    n = m.shape[0]
    square = jax.ShapeDtypeStruct((n, n), jnp.float32)
    return pl.pallas_call(
        functools.partial(last_symmetric_kernel, (first, n // STEP)),
        out_shape=[square, jax.ShapeDtypeStruct((1, n), jnp.float32), square],
        scratch_shapes=[pltpu.VMEM((n, n), jnp.float32)],
        compiler_params=pltpu.CompilerParams(vmem_limit_bytes=16 * 2**20),
        cost_estimate=cost(n, n // STEP - first),
    )(m, top)


def mm_tn(a, b):
    return lax.dot_general(a, b, (((0,), (0,)), ((), ())), precision=HI, preferred_element_type=jnp.float32)


def swap(x, axis):
    return lax.all_to_all(x, axis, 0, 0, tiled=True)


def gathered(x, axis):
    return swap(jnp.broadcast_to(x[None], (lax.axis_size(axis), *x.shape)), axis)


def other_core(x):
    return lax.ppermute(x, CORE, [(0, 1), (1, 0)])


def in_core_order(mine, core, axis):
    theirs = other_core(mine)
    first = core == 0
    return jnp.stack([jnp.where(first, mine, theirs), jnp.where(first, theirs, mine)], axis)


def to_mirror(piece):
    rows, cols = lax.axis_size(ROW), lax.axis_size(COL)
    pairs = []
    for r in range(rows):
        for c in range(cols):
            to_row, to_col = r // cols * cols + c, r % cols
            pairs.append((r * cols + c, to_row * cols + to_col))
    return lax.ppermute(piece, ROW + COL, pairs)


def cut_rows(x, blocks, peers):
    width = x.shape[-1]
    return x.reshape(blocks, peers, -1, width).transpose(1, 0, 2, 3).reshape(peers, -1, width)


def joined_rows(slabs, blocks):
    peers, _, width = slabs.shape
    return slabs.reshape(peers, blocks, -1, width).transpose(1, 0, 2, 3).reshape(-1, width)


def mirror_rows(mine, core, blocks):
    far, near = lax.axis_size("x_lo"), lax.axis_size("z")
    width = mine.shape[-1]
    both = in_core_order(mine.reshape(far, near, blocks, -1, width), core, 2)
    return both.transpose(3, 0, 1, 2, 4, 5).reshape(-1, width)


def after(x, other):
    return lax.optimization_barrier((x, other))[0]


def on_device(matrix_tiles):
    tile_shape = matrix_tiles.shape
    blocks, tile, wide = tile_shape[0], tile_shape[2], tile_shape[3]
    band = 2 * tile
    half = band // STEP // 2
    rows, cols = lax.axis_size(ROW), lax.axis_size(COL)
    r, c, core = lax.axis_index(ROW), lax.axis_index(COL), lax.axis_index(CORE)
    a = matrix_tiles.reshape(blocks * tile, wide * tile)
    slab = blocks * tile // cols
    part = band // cols
    lane = jnp.arange(band, dtype=jnp.int32)

    def places(count, peers, me):
        at = jnp.arange(count, dtype=jnp.int32)
        return (at // tile * peers + me) * tile + at % tile

    def pair(source, first):
        return jnp.concatenate([source[first], source[first + 1]], 1)

    def cleared(x, at, below):
        return jnp.where((at >= below)[:, None], x, 0.0)

    row_of, col_of = places(blocks * tile, rows, r), places(wide * tile, cols, c)
    own = jnp.arange(slab, dtype=jnp.int32)
    own_of = (own // (tile // cols) * rows + r) * tile + c * (tile // cols) + own % (tile // cols)

    source = swap(cut_rows(a[:, :tile], blocks, cols), COL)
    p_own, next_own = pair(source, 0), pair(source, 2)
    p_cols = cleared(mirror_rows(gathered(to_mirror(p_own), PAIR), core, blocks), col_of, band)
    p_own = cleared(p_own, own_of, band)
    for panel in range(PANELS):
        below = (panel + 1) * band
        first = below // tile
        gram = mm_tn(p_cols, p_cols).reshape(cols, part, band)
        top = jnp.concatenate(
            [jnp.where(c == first + i, p_cols[:tile], 0.0) for i in range(2)], 0
        ).reshape(cols, part, band)
        summed = swap(jnp.concatenate([gram, top], 1), COL).sum(0)
        summed = gathered(summed, COL)
        gram, top = summed[:, :part].reshape(band, band), summed[:, part:].reshape(band, band)
        inverse, sign, shifted = last_symmetric(stage(gram, True, 0, half), top, half)

        u = cut_rows(mm(a, p_cols), blocks, cols)
        if panel:
            u = jnp.concatenate([u, cut_rows(a[:, :tile], blocks, cols)], 2)
        arrived = swap(after(u, gram), COL)
        u_own = arrived[:, :, :band].sum(0)
        edge_own = pair(arrived[:, :, band:], first) if panel else next_own
        if panel == 0:
            arrived = gathered(after(jnp.concatenate([p_own, next_own], 1), u_own), COL)
            joined = joined_rows(arrived, blocks)
            p_rows, next_rows = cleared(joined[:, :band], row_of, band), joined[:, band:]

        def signs_at(at):
            return jnp.where(at[:, None] - below == lane[None, :], sign, 0.0)

        u_own = mm_nt(u_own, inverse) - edge_own * sign
        y_rows = mm_nt(p_rows, inverse) - signs_at(row_of)
        y_cols = mm_nt(p_cols, inverse) - signs_at(col_of)
        mirrored = to_mirror(u_own)
        if panel == 0:
            next_mirrored = to_mirror(next_own)
        u_rows = joined_rows(gathered(u_own, COL), blocks)
        h = mm_tn(y_rows, u_rows)
        h = lax.dynamic_slice_in_dim(h, c * part, part, 0)
        held = tile // cols
        tops = [jnp.where(r == first + i, u_own[:held], 0.0) for i in range(0 if panel else 2)]
        arrived = gathered(jnp.concatenate([mirrored, h, *tops], 0), PAIR)
        u_cols = mirror_rows(arrived[:, :slab], core, blocks)
        small = arrived[:, slab:].sum(0)
        small = gathered(small + other_core(small), COL)
        h = small[:, :part].reshape(band, band)
        u_top = None if panel else small[:, part:].reshape(cols, 2, held, band).swapaxes(0, 1).reshape(band, band)
        if panel == 0:
            next_cols = mirror_rows(gathered(after(next_mirrored, u_cols), PAIR), core, blocks)

        tf = stage(stage(shifted, False, 0, half), False, half, 2 * half)
        half_z = 0.5 * mm_tn(tf, mm(h, tf))
        w_rows = mm(u_rows, tf) - mm(y_rows, half_z)
        w_cols = mm(u_cols, tf) - mm(y_cols, half_z)
        if panel == 0:
            y_top = mm_nt(top, inverse) - jnp.where(jnp.eye(band, dtype=bool), sign, 0.0)
            w_top = mm(u_top, tf) - mm(y_top, half_z)
            tops = jnp.concatenate([w_top, y_top], 1)
            p_cols = cleared(next_cols - mm_nt(jnp.concatenate([y_cols, w_cols], 1), tops), col_of, below + band)
            p_rows = cleared(next_rows - mm_nt(jnp.concatenate([y_rows, w_rows], 1), tops), row_of, below + band)
        a = a - mm_nt(jnp.concatenate([y_rows, w_rows], 1), jnp.concatenate([w_cols, y_cols], 1))
    return a.reshape(tile_shape)


def solution(mesh):
    finer = Mesh(mesh.devices.reshape(2, 4, 2, 2, 4), ("x_lo", "z", "core", "x_hi", "y"))
    spec = P(None, ROW, None, None, COL, None)
    return jax.shard_map(on_device, mesh=finer, in_specs=(spec,), out_specs=spec, check_vma=False)
```

```python
import functools

import jax
import jax.numpy as jnp
from jax import lax
from jax.experimental import pallas as pl
from jax.experimental.pallas import tpu as pltpu
from jax.sharding import Mesh
from jax.sharding import PartitionSpec as P

PANELS = 2
PAIR = ("x_lo", "z")
CORE = "core"
ROW = ("x_lo", "z", "core")
COL = ("x_hi", "y")
HI = lax.Precision.HIGHEST

def mm(a, b):
    return lax.dot_general(a, b, (((1,), (0,)), ((), ())), precision=HI, preferred_element_type=jnp.float32)
def mm_nt(a, b):
    return lax.dot_general(a, b, (((1,), (1,)), ((), ())), precision=HI, preferred_element_type=jnp.float32)

STEP = 8

def entries(block):
    columns = [jnp.broadcast_to(block[:, j:j + 1], (STEP, 128)) for j in range(STEP)]
    return [[jnp.broadcast_to(columns[j][i:i + 1, :], (STEP, 128)) for j in range(STEP)] for i in range(STEP)]

def as_columns(x, sub):
    out = []
    for j in range(STEP):
        col = jnp.zeros((STEP, 128), jnp.float32)
        for i in range(STEP):
            if x[i][j] is not None:
                col = jnp.where(sub == i, x[i][j], col)
        out.append(col)
    return out

def apply(cols, rows):
    n = rows.shape[1]
    parts = []
    for c in range(0, n, 128):
        acc = None
        for j in range(STEP):
            t = cols[j] * rows[j:j + 1, c:c + 128]
            acc = t if acc is None else acc + t
        parts.append(acc)
    return jnp.concatenate(parts, 1)

def chol_inverse_8(e):
    x = [[None] * STEP for _ in range(STEP)]
    l = [[None] * STEP for _ in range(STEP)]
    a = [[e[i][j] for j in range(STEP)] for i in range(STEP)]
    inv = [None] * STEP
    for k in range(STEP):
        inv[k] = 1.0 / jnp.sqrt(a[k][k])
        for i in range(k + 1, STEP):
            l[i][k] = a[i][k] * inv[k]
        for j in range(k + 1, STEP):
            for i in range(j, STEP):
                a[i][j] = a[i][j] - l[i][k] * l[j][k]
        x[k][k] = inv[k]
        for j in range(k):
            s = None
            for q in range(j, k):
                t = l[k][q] * x[q][j]
                s = t if s is None else s + t
            x[k][j] = -s * inv[k]
    return x

def inverse_8(e):
    a = [[e[i][j] for j in range(STEP)] for i in range(STEP)]
    for k in range(STEP):
        p = 1.0 / a[k][k]
        a[k] = [a[k][j] * p if j != k else p for j in range(STEP)]
        for i in range(STEP):
            if i == k:
                continue
            f = a[i][k]
            a[i] = [a[i][j] - f * a[k][j] if j != k else -f * p for j in range(STEP)]
    return a

def eliminate(m_ref, n, symmetric, steps):
    lanes8 = lax.broadcasted_iota(jnp.int32, (STEP, n), 1)
    subs8 = lax.broadcasted_iota(jnp.int32, (STEP, n), 0)
    sub = lax.broadcasted_iota(jnp.int32, (STEP, 128), 0)
    lanes = lax.broadcasted_iota(jnp.int32, (n, n), 1)
    rows_of = lax.broadcasted_iota(jnp.int32, (n, n), 0)

    def body(k, _):
        at = pl.multiple_of(k * STEP, STEP)
        rows = m_ref[pl.ds(at, STEP), :]
        block = pltpu.roll(rows, n - at, 1)[:, :STEP]
        here = (lanes8 >= at) & (lanes8 < at + STEP)
        e = entries(block)
        unit = jnp.where(here, (lanes8 - at == subs8).astype(jnp.float32), rows)
        if symmetric:
            x = chol_inverse_8(e)
            kept = apply(as_columns(x, sub), unit)
            xt = [[x[j][i] for j in range(STEP)] for i in range(STEP)]
            spread = apply(as_columns(xt, sub), kept)
        else:
            spread = kept = apply(as_columns(inverse_8(e), sub), unit)
        m = m_ref[...]
        inside = (lanes >= at) & (lanes < at + STEP)
        other = (rows_of >= at + STEP) if symmetric else ((rows_of < at) | (rows_of >= at + STEP))
        left = jnp.where(inside & other, m, 0.0)
        full = jnp.concatenate([spread] * (n // STEP), 0)
        full = jnp.where((rows_of >= at) & (rows_of < at + STEP), full, 0.0)
        m_ref[...] = jnp.where(inside & other, 0.0, m) - mm(left, full)
        m_ref[pl.ds(at, STEP), :] = kept
        return 0

    lax.fori_loop(*steps, body, 0)

def stage_kernel(symmetric, steps, m_ref, out_ref):
    out_ref[...] = m_ref[...]
    eliminate(out_ref, m_ref.shape[0], symmetric, steps)


def last_symmetric_kernel(steps, m_ref, top_ref, inv_ref, sign_ref, next_ref, work_ref):
    n = m_ref.shape[0]
    r = lax.broadcasted_iota(jnp.int32, (n, n), 0)
    c = lax.broadcasted_iota(jnp.int32, (n, n), 1)
    work_ref[...] = m_ref[...]
    eliminate(work_ref, n, True, steps)
    inv = jnp.where(r >= c, work_ref[...], 0.0)
    inv_ref[...] = inv
    q1t = mm_nt(inv, top_ref[...])
    diag = jnp.sum(jnp.where(r == c, q1t, 0.0), axis=0, keepdims=True)
    sign = jnp.where(diag >= 0, -1.0, 1.0)
    sign_ref[...] = sign
    next_ref[...] = (r == c).astype(jnp.float32) - q1t * sign


def cost(n, steps):
    return pl.CostEstimate(flops=STAGE_FLOPS, bytes_accessed=8 * n * n, transcendentals=0)


STAGE_FLOPS = 10**10


def stage(m, symmetric, first, last):
    n = m.shape[0]
    return pl.pallas_call(
        functools.partial(stage_kernel, symmetric, (first, last)),
        out_shape=jax.ShapeDtypeStruct((n, n), jnp.float32),
        compiler_params=pltpu.CompilerParams(vmem_limit_bytes=16 * 2**20),
        cost_estimate=cost(n, last - first),
    )(m)


def last_symmetric(m, top, first):
    n = m.shape[0]
    square = jax.ShapeDtypeStruct((n, n), jnp.float32)
    return pl.pallas_call(
        functools.partial(last_symmetric_kernel, (first, n // STEP)),
        out_shape=[square, jax.ShapeDtypeStruct((1, n), jnp.float32), square],
        scratch_shapes=[pltpu.VMEM((n, n), jnp.float32)],
        compiler_params=pltpu.CompilerParams(vmem_limit_bytes=16 * 2**20),
        cost_estimate=cost(n, n // STEP - first),
    )(m, top)


def mm_tn(a, b):
    return lax.dot_general(a, b, (((0,), (0,)), ((), ())), precision=HI, preferred_element_type=jnp.float32)


def swap(x, axis):
    return lax.all_to_all(x, axis, 0, 0, tiled=True)


def gathered(x, axis):
    return swap(jnp.broadcast_to(x[None], (lax.axis_size(axis), *x.shape)), axis)


def other_core(x):
    return lax.ppermute(x, CORE, [(0, 1), (1, 0)])


def in_core_order(mine, core, axis):
    theirs = other_core(mine)
    first = core == 0
    return jnp.stack([jnp.where(first, mine, theirs), jnp.where(first, theirs, mine)], axis)


def to_mirror(piece):
    rows, cols = lax.axis_size(ROW), lax.axis_size(COL)
    pairs = []
    for r in range(rows):
        for c in range(cols):
            to_row, to_col = r // cols * cols + c, r % cols
            pairs.append((r * cols + c, to_row * cols + to_col))
    return lax.ppermute(piece, ROW + COL, pairs)


def cut_rows(x, blocks, peers):
    width = x.shape[-1]
    return x.reshape(blocks, peers, -1, width).transpose(1, 0, 2, 3).reshape(peers, -1, width)


def joined_rows(slabs, blocks):
    peers, _, width = slabs.shape
    return slabs.reshape(peers, blocks, -1, width).transpose(1, 0, 2, 3).reshape(-1, width)


def mirror_rows(mine, core, blocks):
    far, near = lax.axis_size("x_lo"), lax.axis_size("z")
    width = mine.shape[-1]
    both = in_core_order(mine.reshape(far, near, blocks, -1, width), core, 2)
    return both.transpose(3, 0, 1, 2, 4, 5).reshape(-1, width)


def untile_kernel(wide, tiles_ref, a_ref):
    rows, lanes = a_ref.shape[0], tiles_ref.shape[1]
    for n in range(wide):
        a_ref[:, n * lanes:(n + 1) * lanes] = tiles_ref[pl.ds(n, rows, stride=wide), :]


def untiled(matrix_tiles):
    blocks, _, tile, wide, _, lanes = matrix_tiles.shape
    return pl.pallas_call(
        functools.partial(untile_kernel, wide),
        grid=(blocks,),
        in_specs=[pl.BlockSpec((tile * wide, lanes), lambda i: (i, 0))],
        out_specs=pl.BlockSpec((tile, wide * lanes), lambda i: (i, 0)),
        out_shape=jax.ShapeDtypeStruct((blocks * tile, wide * lanes), jnp.float32),
        compiler_params=pltpu.CompilerParams(vmem_limit_bytes=16 * 2**20),
    )(matrix_tiles.reshape(blocks * tile * wide, lanes))


def after(x, other):
    return lax.optimization_barrier((x, other))[0]


def on_device(matrix_tiles):
    tile_shape = matrix_tiles.shape
    blocks, tile, wide = tile_shape[0], tile_shape[2], tile_shape[3]
    band = 2 * tile
    half = band // STEP // 2
    rows, cols = lax.axis_size(ROW), lax.axis_size(COL)
    r, c, core = lax.axis_index(ROW), lax.axis_index(COL), lax.axis_index(CORE)
    a = untiled(matrix_tiles)
    slab = blocks * tile // cols
    part = band // cols
    lane = jnp.arange(band, dtype=jnp.int32)

    def places(count, peers, me):
        at = jnp.arange(count, dtype=jnp.int32)
        return (at // tile * peers + me) * tile + at % tile

    def pair(source, first):
        return jnp.concatenate([source[first], source[first + 1]], 1)

    def cleared(x, at, below):
        return jnp.where((at >= below)[:, None], x, 0.0)

    row_of, col_of = places(blocks * tile, rows, r), places(wide * tile, cols, c)
    own = jnp.arange(slab, dtype=jnp.int32)
    own_of = (own // (tile // cols) * rows + r) * tile + c * (tile // cols) + own % (tile // cols)

    source = swap(cut_rows(a[:, :tile], blocks, cols), COL)
    p_own, next_own = pair(source, 0), pair(source, 2)
    mirrored = to_mirror(jnp.concatenate([p_own, next_own], 1))
    arrived = gathered(p_own, COL)
    p_rows = cleared(joined_rows(arrived, blocks), row_of, band)
    mine = gathered(after(mirrored, arrived), PAIR)
    theirs = other_core(mine)
    far, near, held = lax.axis_size("x_lo"), lax.axis_size("z"), tile // cols
    shape = (far, near, blocks, held, 2 * band)
    mine, theirs = mine.reshape(shape), theirs.reshape(shape)
    gram, tops = 0.0, []
    for x, which in ((mine, core), (theirs, 1 - core)):
        i, z, m, t = (lax.broadcasted_iota(jnp.int32, shape[:4], d) for d in range(4))
        at = ((m * far + i) * cols + c) * tile + (2 * z + which) * held + t
        x = jnp.where((at >= band)[..., None], x[..., :band], 0.0)
        tops.append(x[0, :, 0])
        x = x.reshape(-1, band)
        gram = gram + mm_tn(x, x)
    top = jnp.stack([jnp.where(core == 0, tops[0], tops[1]), jnp.where(core == 0, tops[1], tops[0])], 1)
    top = top.reshape(tile, band)
    both = jnp.stack([jnp.where(core == 0, mine, theirs), jnp.where(core == 0, theirs, mine)], 2)
    both = both.transpose(3, 0, 1, 2, 4, 5).reshape(-1, 2 * band)
    p_cols, next_cols = cleared(both[:, :band], col_of, band), both[:, band:]
    for panel in range(PANELS):
        below = (panel + 1) * band
        first = below // tile
        if panel:
            gram, top = mm_tn(p_cols, p_cols), p_cols[:tile]
        gram = gram.reshape(cols, part, band)
        top = jnp.concatenate([jnp.where(c == first + i, top, 0.0) for i in range(2)], 0)
        summed = swap(jnp.concatenate([gram, top.reshape(cols, part, band)], 1), COL).sum(0)
        summed = gathered(summed, COL)
        gram, top = summed[:, :part].reshape(band, band), summed[:, part:].reshape(band, band)
        u = cut_rows(mm(a, p_cols), blocks, cols)
        if panel:
            u = jnp.concatenate([u, cut_rows(a[:, :tile], blocks, cols)], 2)
        arrived = swap(after(u, gram), COL)
        half_way = after(stage(gram, True, 0, half), arrived)
        inverse, sign, shifted = last_symmetric(half_way, top, half)
        u_own = arrived[:, :, :band].sum(0)
        edge_own = pair(arrived[:, :, band:], first) if panel else next_own
        if panel == 0:
            arrived = gathered(after(next_own, arrived), COL)
            next_rows = joined_rows(arrived, blocks)
            u_own, shifted = after((u_own, shifted), arrived)

        def signs_at(at):
            return jnp.where(at[:, None] - below == lane[None, :], sign, 0.0)

        u_own = mm_nt(u_own, inverse) - edge_own * sign
        y_rows = mm_nt(p_rows, inverse) - signs_at(row_of)
        y_cols = mm_nt(p_cols, inverse) - signs_at(col_of)
        mirrored = to_mirror(u_own)
        arrived = gathered(u_own, COL)
        u_rows = joined_rows(arrived, blocks)
        half_way = after(stage(shifted, False, 0, half), arrived)
        mirrored = after(mirrored, half_way)
        h = mm_tn(y_rows, u_rows)
        h = lax.dynamic_slice_in_dim(h, c * part, part, 0)
        tops = [jnp.where(r == first + i, u_own[:held], 0.0) for i in range(0 if panel else 2)]
        arrived = gathered(jnp.concatenate([mirrored, h, *tops], 0), PAIR)
        tf = stage(half_way, False, half, 2 * half)
        arrived = after(arrived, tf)
        u_cols = mirror_rows(arrived[:, :slab], core, blocks)
        small = arrived[:, slab:].sum(0)
        small = gathered(small + other_core(small), COL)
        h = small[:, :part].reshape(band, band)
        u_top = None if panel else small[:, part:].reshape(cols, 2, held, band).swapaxes(0, 1).reshape(band, band)
        half_z = 0.5 * mm_tn(tf, mm(h, tf))
        w_rows = mm(u_rows, tf) - mm(y_rows, half_z)
        w_cols = mm(u_cols, tf) - mm(y_cols, half_z)
        if panel == 0:
            y_top = mm_nt(top, inverse) - jnp.where(jnp.eye(band, dtype=bool), sign, 0.0)
            w_top = mm(u_top, tf) - mm(y_top, half_z)
            tops = jnp.concatenate([w_top, y_top], 1)
            p_cols = cleared(next_cols - mm_nt(jnp.concatenate([y_cols, w_cols], 1), tops), col_of, below + band)
            p_rows = cleared(next_rows - mm_nt(jnp.concatenate([y_rows, w_rows], 1), tops), row_of, below + band)
        a = a - mm_nt(jnp.concatenate([y_rows, w_rows], 1), jnp.concatenate([w_cols, y_cols], 1))
    return a.reshape(tile_shape)


def solution(mesh):
    finer = Mesh(mesh.devices.reshape(2, 4, 2, 2, 4), ("x_lo", "z", "core", "x_hi", "y"))
    spec = P(None, ROW, None, None, COL, None)
    return jax.shard_map(on_device, mesh=finer, in_specs=(spec,), out_specs=spec, check_vma=False)
```

```python
import functools

import jax
import jax.numpy as jnp
from jax import lax
from jax.experimental import pallas as pl
from jax.experimental.pallas import tpu as pltpu
from jax.sharding import Mesh
from jax.sharding import PartitionSpec as P

PANELS = 2
PAIR = ("x_lo", "z")
CORE = "core"
ROW = ("x_lo", "z", "core")
COL = ("x_hi", "y")
HI = lax.Precision.HIGHEST


def mm(a, b):
    return lax.dot_general(a, b, (((1,), (0,)), ((), ())), precision=HI, preferred_element_type=jnp.float32)


def mm_nt(a, b):
    return lax.dot_general(a, b, (((1,), (1,)), ((), ())), precision=HI, preferred_element_type=jnp.float32)


def mm_tn(a, b):
    return lax.dot_general(a, b, (((0,), (0,)), ((), ())), precision=HI, preferred_element_type=jnp.float32)


STEP = 8


def entries(block):
    columns = [jnp.broadcast_to(block[:, j:j + 1], (STEP, 128)) for j in range(STEP)]
    return [[jnp.broadcast_to(columns[j][i:i + 1, :], (STEP, 128)) if j <= i else None for j in range(STEP)] for i in range(STEP)]


def inverse_root(a):
    y = lax.rsqrt(a)
    return y * (1.5 - (0.5 * a) * (y * y))


def chol_inverse_8(a):
    a = [list(row) for row in a]
    x = [[None] * STEP for _ in range(STEP)]
    for k in range(STEP):
        x[k][k] = inverse_root(a[k][k])
        for i in range(k + 1, STEP):
            a[i][k] = a[i][k] * x[k][k]
        for j in range(k + 1, STEP):
            for i in range(j, STEP):
                a[i][j] = a[i][j] - a[i][k] * a[j][k]
    for k in range(STEP):
        for j in range(k):
            s = a[k][j] * x[j][j]
            for q in range(j + 1, k):
                s = s + a[k][q] * x[q][j]
            x[k][j] = -s * x[k][k]
    return x


def apply_lower(x, rows, sub):
    columns = []
    for j in range(STEP):
        col = x[STEP - 1][j]
        for i in range(STEP - 2, j - 1, -1):
            col = jnp.where(sub == i, x[i][j], col)
        columns.append(jnp.where(sub >= j, col, 0.0) if j else col)
    parts = []
    for c in range(0, rows.shape[1], 128):
        terms = [columns[j] * rows[j:j + 1, c:c + 128] for j in range(STEP)]
        while len(terms) > 1:
            terms = [terms[i] + terms[i + 1] for i in range(0, len(terms), 2)]
        parts.append(terms[0])
    return jnp.concatenate(parts, 1)


def three(x):
    hi = x.astype(jnp.bfloat16).astype(jnp.float32)
    rest = x - hi
    mid = rest.astype(jnp.bfloat16).astype(jnp.float32)
    return hi, mid, rest - mid


def outer(left, right):
    a, b, c = three(left)
    d, e, f = three(right)
    lefts = jnp.concatenate([a, a, b, a, c, b], 0).astype(jnp.bfloat16)
    rights = jnp.concatenate([d, e, d, f, d, e], 0).astype(jnp.bfloat16)
    return lax.dot_general(lefts, rights, (((0,), (0,)), ((), ())), preferred_element_type=jnp.float32)


def eliminate(m_ref, n, steps):
    lanes8 = lax.broadcasted_iota(jnp.int32, (STEP, n), 1)
    subs8 = lax.broadcasted_iota(jnp.int32, (STEP, n), 0)
    sub = lax.broadcasted_iota(jnp.int32, (STEP, 128), 0)
    low = steps[0] * STEP
    lanes = lax.broadcasted_iota(jnp.int32, (n - low, n), 1)
    rows_of = lax.broadcasted_iota(jnp.int32, (n - low, n), 0) + low

    def body(k, _):
        at = pl.multiple_of(k * STEP, STEP)
        rows = m_ref[pl.ds(at, STEP), :]
        block = pltpu.roll(rows, n - at, 1)[:, :STEP]
        here = (lanes8 >= at) & (lanes8 < at + STEP)
        unit = jnp.where(here, (lanes8 - at == subs8).astype(jnp.float32), rows)
        kept = apply_lower(chol_inverse_8(entries(block)), unit, sub)
        m_ref[pl.ds(at, STEP), :] = kept
        m = m_ref[low:, :]
        cleared = (lanes >= at) & (lanes < at + STEP) & (rows_of >= at + STEP)
        left = jnp.where(lanes8 >= at + STEP, kept, 0.0)
        m_ref[low:, :] = jnp.where(cleared, 0.0, m) - outer(left, kept)[low:, :]
        return 0

    lax.fori_loop(*steps, body, 0)


def square_places(n):
    return lax.broadcasted_iota(jnp.int32, (n, n), 0), lax.broadcasted_iota(jnp.int32, (n, n), 1)


def packed(m):
    h = m.shape[0] // 2
    r, c = square_places(h)
    low, high = m[:h, :h], m[h:, h:]
    diagonal = jnp.sum(jnp.where(r == c, high, 0.0), axis=0, keepdims=True)
    last = jnp.pad(diagonal, ((0, STEP - 1), (0, h)))
    return jnp.concatenate([jnp.concatenate([m[h:, :h], jnp.where(r >= c, low, high)], 1), last], 0)


def unpacked(p):
    h = p.shape[1] // 2
    r, c = square_places(h)
    corner, both, diagonal = p[:h, :h], p[:h, h:], p[h:h + 1, :h]
    flipped = both.T
    low = jnp.where(r >= c, both, flipped)
    high = jnp.where(r == c, diagonal, jnp.where(r < c, both, flipped))
    return jnp.concatenate(
        [jnp.concatenate([low, corner.T], 1), jnp.concatenate([corner, high], 1)], 0
    )


def call(kernel, shapes, *operands, flops=10**10):
    return pl.pallas_call(
        kernel,
        out_shape=[jax.ShapeDtypeStruct(s, jnp.float32) for s in shapes],
        compiler_params=pltpu.CompilerParams(vmem_limit_bytes=24 * 2**20),
        cost_estimate=pl.CostEstimate(flops=flops, bytes_accessed=2**20, transcendentals=0),
    )(*operands)


def first_kernel(steps, parts_ref, m_ref):
    total = parts_ref[0]
    for i in range(1, parts_ref.shape[0]):
        total = total + parts_ref[i]
    m_ref[...] = unpacked(total)
    eliminate(m_ref, m_ref.shape[0], steps)


def last_kernel(steps, m_ref, out_ref):
    n = m_ref.shape[0]
    r, c = square_places(n)
    out_ref[...] = m_ref[...]
    eliminate(out_ref, n, steps)
    out_ref[...] = jnp.where(r >= c, out_ref[...], 0.0)


def reflect_kernel(inverse_ref, top_ref, sign_ref, turned_ref):
    n = top_ref.shape[0]
    r, c = square_places(n)
    q1t = mm_nt(inverse_ref[...], top_ref[...])
    diagonal = jnp.sum(jnp.where(r == c, q1t, 0.0), axis=0, keepdims=True)
    sign = jnp.where(diagonal >= 0, -1.0, 1.0)
    sign_ref[...] = sign
    turned_ref[...] = jnp.where(r == c, q1t - sign, q1t)


def outer_first_kernel(steps, turned_ref, m_ref):
    m_ref[...] = mm_nt(turned_ref[...], turned_ref[...])
    eliminate(m_ref, m_ref.shape[0], steps)


def outer_last_kernel(steps, m_ref, turned_ref, sign_ref, tft_ref):
    n = m_ref.shape[0]
    r, c = square_places(n)
    tft_ref[...] = m_ref[...]
    eliminate(tft_ref, n, steps)
    root = jnp.where(r >= c, tft_ref[...], 0.0)
    tft_ref[...] = -mm(mm_tn(root, root), turned_ref[...]) * sign_ref[...]


def half_z_kernel(mine_ref, theirs_ref, tft_ref, z_ref):
    z_ref[...] = 0.5 * mm_nt(mm(tft_ref[...], unpacked(mine_ref[...] + theirs_ref[...])), tft_ref[...])


def swap(x, axis):
    return lax.all_to_all(x, axis, 0, 0, tiled=True)


def gathered(x, axis):
    return swap(jnp.broadcast_to(x[None], (lax.axis_size(axis), *x.shape)), axis)


def other_core(x):
    return lax.ppermute(x, CORE, [(0, 1), (1, 0)])


def in_core_order(mine, core, axis):
    theirs = other_core(mine)
    first = core == 0
    return jnp.stack([jnp.where(first, mine, theirs), jnp.where(first, theirs, mine)], axis)


def to_mirror(piece):
    rows, cols = lax.axis_size(ROW), lax.axis_size(COL)
    pairs = []
    for r in range(rows):
        for c in range(cols):
            to_row, to_col = r // cols * cols + c, r % cols
            pairs.append((r * cols + c, to_row * cols + to_col))
    return lax.ppermute(piece, ROW + COL, pairs)


def cut_rows(x, blocks, peers):
    width = x.shape[-1]
    return x.reshape(blocks, peers, -1, width).transpose(1, 0, 2, 3).reshape(peers, -1, width)


def joined_rows(slabs, blocks):
    peers, _, width = slabs.shape
    return slabs.reshape(peers, blocks, -1, width).transpose(1, 0, 2, 3).reshape(-1, width)


def mirror_rows(mine, core, blocks):
    far, near = lax.axis_size("x_lo"), lax.axis_size("z")
    width = mine.shape[-1]
    both = in_core_order(mine.reshape(far, near, blocks, -1, width), core, 2)
    return both.transpose(3, 0, 1, 2, 4, 5).reshape(-1, width)


def untile_kernel(wide, tiles_ref, a_ref):
    rows, lanes = a_ref.shape[0], tiles_ref.shape[1]
    for n in range(wide):
        a_ref[:, n * lanes:(n + 1) * lanes] = tiles_ref[pl.ds(n, rows, stride=wide), :]


def untiled(matrix_tiles):
    blocks, _, tile, wide, _, lanes = matrix_tiles.shape
    return pl.pallas_call(
        functools.partial(untile_kernel, wide),
        grid=(blocks,),
        in_specs=[pl.BlockSpec((tile * wide, lanes), lambda i: (i, 0))],
        out_specs=pl.BlockSpec((tile, wide * lanes), lambda i: (i, 0)),
        out_shape=jax.ShapeDtypeStruct((blocks * tile, wide * lanes), jnp.float32),
        compiler_params=pltpu.CompilerParams(vmem_limit_bytes=16 * 2**20),
    )(matrix_tiles.reshape(blocks * tile * wide, lanes))


def tile_kernel(wide, a_ref, tiles_ref):
    rows, lanes = a_ref.shape[0], tiles_ref.shape[1]
    for n in range(wide):
        tiles_ref[pl.ds(n, rows, stride=wide), :] = a_ref[:, n * lanes:(n + 1) * lanes]


def tiled(a, shape):
    blocks, _, tile, wide, _, lanes = shape
    return pl.pallas_call(
        functools.partial(tile_kernel, wide),
        grid=(blocks,),
        in_specs=[pl.BlockSpec((tile, wide * lanes), lambda i: (i, 0))],
        out_specs=pl.BlockSpec((tile * wide, lanes), lambda i: (i, 0)),
        out_shape=jax.ShapeDtypeStruct((blocks * tile * wide, lanes), jnp.float32),
        compiler_params=pltpu.CompilerParams(vmem_limit_bytes=16 * 2**20),
    )(a).reshape(shape)


def after(x, other):
    return lax.optimization_barrier((x, other))[0]


def on_device(matrix_tiles):
    tile_shape = matrix_tiles.shape
    blocks, tile, wide = tile_shape[0], tile_shape[2], tile_shape[3]
    band = 2 * tile
    half = band // STEP // 2
    rows, cols = lax.axis_size(ROW), lax.axis_size(COL)
    r, c, core = lax.axis_index(ROW), lax.axis_index(COL), lax.axis_index(CORE)
    a = untiled(matrix_tiles)
    slab = blocks * tile // cols
    part = band // cols
    lane = jnp.arange(band, dtype=jnp.int32)

    def places(count, peers, me):
        at = jnp.arange(count, dtype=jnp.int32)
        return (at // tile * peers + me) * tile + at % tile

    def pair(source, first):
        return jnp.concatenate([source[first], source[first + 1]], 1)

    def cleared(x, at, below):
        return jnp.where((at >= below)[:, None], x, 0.0)

    row_of, col_of = places(blocks * tile, rows, r), places(wide * tile, cols, c)
    own = jnp.arange(slab, dtype=jnp.int32)
    own_of = (own // (tile // cols) * rows + r) * tile + c * (tile // cols) + own % (tile // cols)

    source = swap(cut_rows(a[:, :tile], blocks, cols), COL)
    p_own, next_own = pair(source, 0), pair(source, 2)
    mirrored = to_mirror(jnp.concatenate([p_own, next_own], 1))
    arrived = gathered(p_own, COL)
    p_rows = cleared(joined_rows(arrived, blocks), row_of, band)
    mine = gathered(after(mirrored, arrived), PAIR)
    theirs = other_core(mine)
    far, near, held = lax.axis_size("x_lo"), lax.axis_size("z"), tile // cols
    shape = (far, near, blocks, held, 2 * band)
    mine, theirs = mine.reshape(shape), theirs.reshape(shape)
    gram, tops = 0.0, []
    for x, which in ((mine, core), (theirs, 1 - core)):
        i, z, m, t = (lax.broadcasted_iota(jnp.int32, shape[:4], d) for d in range(4))
        at = ((m * far + i) * cols + c) * tile + (2 * z + which) * held + t
        x = jnp.where((at >= band)[..., None], x[..., :band], 0.0)
        tops.append(x[0, :, 0])
        x = x.reshape(-1, band)
        gram = gram + mm_tn(x, x)
    top = jnp.stack([jnp.where(core == 0, tops[0], tops[1]), jnp.where(core == 0, tops[1], tops[0])], 1)
    top = top.reshape(tile, band)
    both = jnp.stack([jnp.where(core == 0, mine, theirs), jnp.where(core == 0, theirs, mine)], 2)
    both = both.transpose(3, 0, 1, 2, 4, 5).reshape(-1, 2 * band)
    p_cols, next_cols = cleared(both[:, :band], col_of, band), both[:, band:]
    half = band // STEP // 2
    square = (band, band)
    for panel in range(PANELS):
        below = (panel + 1) * band
        first = below // tile
        if panel:
            gram, top = mm_tn(p_cols, p_cols), p_cols[:tile]
        parts = gathered(packed(gram), COL)
        (half_way,) = call(functools.partial(first_kernel, (0, half)), [square], parts)

        top = jnp.concatenate([jnp.where(c == first + i, top, 0.0) for i in range(2)], 0)
        sent = [cut_rows(mm(a, p_cols), blocks, cols), top.reshape(cols, part, band)]
        if panel:
            edge = cut_rows(a[:, :tile], blocks, cols)
            sent.append(jnp.concatenate([edge[:, :slab // 2], edge[:, slab // 2:]], 2))
        arrived = swap(after(jnp.concatenate(sent, 1), parts), COL)
        half_way = after(half_way, arrived)
        (inverse,) = call(functools.partial(last_kernel, (half, 2 * half)), [square], half_way)
        summed = arrived[:, :slab + part].sum(0)
        u_own, top = summed[:slab], summed[slab:]
        if panel:
            edge = arrived[first:first + 2, slab + part:]
            edge = jnp.concatenate([edge[:, :, :tile], edge[:, :, tile:]], 1)
            edge_own = jnp.concatenate([edge[0], edge[1]], 1)
            arrived = gathered(top, COL)
        else:
            edge_own = next_own
            arrived = gathered(jnp.concatenate([top, next_own], 0), COL)
            next_rows = joined_rows(arrived[:, part:], blocks)
        top = arrived[:, :part].reshape(square)
        sign, turned = call(reflect_kernel, [(1, band), square], inverse, top, flops=10**9)

        def signs_at(at):
            return jnp.where(at[:, None] - below == lane[None, :], sign, 0.0)

        u_own = mm_nt(u_own, inverse) - edge_own * sign
        y_rows = mm_nt(p_rows, inverse) - signs_at(row_of)
        y_cols = mm_nt(p_cols, inverse) - signs_at(col_of)
        mirrored = to_mirror(u_own)
        arrived = gathered(u_own, COL)
        u_rows = joined_rows(arrived, blocks)
        (half_way,) = call(functools.partial(outer_first_kernel, (0, half)), [square], turned)
        mirrored, half_way = after((mirrored, half_way), arrived)
        sent = [mirrored, packed(mm_tn(y_rows, u_rows))]
        if panel == 0:
            sent.append(u_rows[:tile])
        arrived = gathered(after(jnp.concatenate(sent, 0), half_way), PAIR)
        (tft,) = call(functools.partial(outer_last_kernel, (half, 2 * half)), [square], half_way, turned, sign)
        arrived = after(arrived, tft)
        packs = band // 2 + STEP
        mine = arrived[:, slab:slab + packs].sum(0)
        if panel == 0:
            mine = jnp.concatenate([mine, arrived[first // 2, slab + packs:]], 0)
        theirs = other_core(mine)
        u_cols = mirror_rows(arrived[:, :slab], core, blocks)
        (half_z,) = call(half_z_kernel, [square], mine[:packs], theirs[:packs], tft, flops=10**9)
        w_rows = mm_nt(u_rows, tft) - mm(y_rows, half_z)
        w_cols = mm_nt(u_cols, tft) - mm(y_cols, half_z)
        if panel == 0:
            mine, theirs = mine[packs:], theirs[packs:]
            u_top = jnp.concatenate([jnp.where(core == 0, mine, theirs), jnp.where(core == 0, theirs, mine)], 0)
            y_top = mm_nt(top, inverse) - jnp.where(jnp.eye(band, dtype=bool), sign, 0.0)
            w_top = mm_nt(u_top, tft) - mm(y_top, half_z)
            tops = jnp.concatenate([w_top, y_top], 1)
            p_cols = cleared(next_cols - mm_nt(jnp.concatenate([y_cols, w_cols], 1), tops), col_of, below + band)
            p_rows = cleared(next_rows - mm_nt(jnp.concatenate([y_rows, w_rows], 1), tops), row_of, below + band)
        a = a - mm_nt(jnp.concatenate([y_rows, w_rows], 1), jnp.concatenate([w_cols, y_cols], 1))
    return tiled(a, tile_shape)


def solution(mesh):
    finer = Mesh(mesh.devices.reshape(2, 4, 2, 2, 4), ("x_lo", "z", "core", "x_hi", "y"))
    spec = P(None, ROW, None, None, COL, None)
    return jax.shard_map(on_device, mesh=finer, in_specs=(spec,), out_specs=spec, check_vma=False)
```

```python
import functools

import jax
import jax.numpy as jnp
from jax import lax
from jax.experimental import pallas as pl
from jax.experimental.pallas import tpu as pltpu
from jax.sharding import Mesh
from jax.sharding import PartitionSpec as P

PANELS = 2
PAIR = ("x_lo", "z")
CORE = "core"
ROW = ("x_lo", "z", "core")
COL = ("x_hi", "y")
HI = lax.Precision.HIGHEST


def mm(a, b):
    return lax.dot_general(a, b, (((1,), (0,)), ((), ())), precision=HI, preferred_element_type=jnp.float32)


def mm_nt(a, b):
    return lax.dot_general(a, b, (((1,), (1,)), ((), ())), precision=HI, preferred_element_type=jnp.float32)


def mm_tn(a, b):
    return lax.dot_general(a, b, (((0,), (0,)), ((), ())), precision=HI, preferred_element_type=jnp.float32)


STEP = 8


def entries(block):
    columns = [jnp.broadcast_to(block[:, j:j + 1], (STEP, 128)) for j in range(STEP)]
    return [[jnp.broadcast_to(columns[j][i:i + 1, :], (STEP, 128)) if j <= i else None for j in range(STEP)] for i in range(STEP)]


def inverse_root(a):
    y = lax.rsqrt(a)
    return y * (1.5 - (0.5 * a) * (y * y))


def chol_inverse_8(a):
    a = [list(row) for row in a]
    x = [[None] * STEP for _ in range(STEP)]
    for k in range(STEP):
        x[k][k] = inverse_root(a[k][k])
        for i in range(k + 1, STEP):
            a[i][k] = a[i][k] * x[k][k]
        for j in range(k + 1, STEP):
            for i in range(j, STEP):
                a[i][j] = a[i][j] - a[i][k] * a[j][k]
    for k in range(STEP):
        for j in range(k):
            s = a[k][j] * x[j][j]
            for q in range(j + 1, k):
                s = s + a[k][q] * x[q][j]
            x[k][j] = -s * x[k][k]
    return x


def apply_lower(x, rows, sub):
    columns = []
    for j in range(STEP):
        col = x[STEP - 1][j]
        for i in range(STEP - 2, j - 1, -1):
            col = jnp.where(sub == i, x[i][j], col)
        columns.append(jnp.where(sub >= j, col, 0.0) if j else col)
    parts = []
    for c in range(0, rows.shape[1], 128):
        terms = [columns[j] * rows[j:j + 1, c:c + 128] for j in range(STEP)]
        while len(terms) > 1:
            terms = [terms[i] + terms[i + 1] for i in range(0, len(terms), 2)]
        parts.append(terms[0])
    return jnp.concatenate(parts, 1)


def three(x):
    hi = x.astype(jnp.bfloat16).astype(jnp.float32)
    rest = x - hi
    mid = rest.astype(jnp.bfloat16).astype(jnp.float32)
    return hi, mid, rest - mid


def outer(left, right):
    a, b, c = three(left)
    d, e, f = three(right)
    lefts = jnp.concatenate([a, a, b, a, c, b], 0).astype(jnp.bfloat16)
    rights = jnp.concatenate([d, e, d, f, d, e], 0).astype(jnp.bfloat16)
    return lax.dot_general(lefts, rights, (((0,), (0,)), ((), ())), preferred_element_type=jnp.float32)


def eliminate(m_ref, n, steps):
    lanes8 = lax.broadcasted_iota(jnp.int32, (STEP, n), 1)
    subs8 = lax.broadcasted_iota(jnp.int32, (STEP, n), 0)
    sub = lax.broadcasted_iota(jnp.int32, (STEP, 128), 0)
    low = steps[0] * STEP
    lanes = lax.broadcasted_iota(jnp.int32, (n - low, n), 1)
    rows_of = lax.broadcasted_iota(jnp.int32, (n - low, n), 0) + low

    def body(k, _):
        at = pl.multiple_of(k * STEP, STEP)
        rows = m_ref[pl.ds(at, STEP), :]
        block = pltpu.roll(rows, n - at, 1)[:, :STEP]
        here = (lanes8 >= at) & (lanes8 < at + STEP)
        unit = jnp.where(here, (lanes8 - at == subs8).astype(jnp.float32), rows)
        kept = apply_lower(chol_inverse_8(entries(block)), unit, sub)
        m_ref[pl.ds(at, STEP), :] = kept
        m = m_ref[low:, :]
        cleared = (lanes >= at) & (lanes < at + STEP) & (rows_of >= at + STEP)
        left = jnp.where(lanes8 >= at + STEP, kept, 0.0)
        m_ref[low:, :] = jnp.where(cleared, 0.0, m) - outer(left, kept)[low:, :]
        return 0

    lax.fori_loop(*steps, body, 0)


def square_places(n):
    return lax.broadcasted_iota(jnp.int32, (n, n), 0), lax.broadcasted_iota(jnp.int32, (n, n), 1)


def packed(m):
    h = m.shape[0] // 2
    r, c = square_places(h)
    low, high = m[:h, :h], m[h:, h:]
    diagonal = jnp.sum(jnp.where(r == c, high, 0.0), axis=0, keepdims=True)
    last = jnp.pad(diagonal, ((0, STEP - 1), (0, h)))
    return jnp.concatenate([jnp.concatenate([m[h:, :h], jnp.where(r >= c, low, high)], 1), last], 0)


def unpacked(p):
    h = p.shape[1] // 2
    r, c = square_places(h)
    corner, both, diagonal = p[:h, :h], p[:h, h:], p[h:h + 1, :h]
    flipped = both.T
    low = jnp.where(r >= c, both, flipped)
    high = jnp.where(r == c, diagonal, jnp.where(r < c, both, flipped))
    return jnp.concatenate(
        [jnp.concatenate([low, corner.T], 1), jnp.concatenate([corner, high], 1)], 0
    )


def call(kernel, shapes, *operands, flops=10**10):
    return pl.pallas_call(
        kernel,
        out_shape=[jax.ShapeDtypeStruct(s, jnp.float32) for s in shapes],
        compiler_params=pltpu.CompilerParams(vmem_limit_bytes=24 * 2**20),
        cost_estimate=pl.CostEstimate(flops=flops, bytes_accessed=2**20, transcendentals=0),
    )(*operands)


def whole_kernel(parts_ref, out_ref):
    n = out_ref.shape[0]
    r, c = square_places(n)
    total = parts_ref[0]
    for i in range(1, parts_ref.shape[0]):
        total = total + parts_ref[i]
    out_ref[...] = unpacked(total)
    for i in range(0, n // STEP, 8):
        eliminate(out_ref, n, (i, i + 8))
    out_ref[...] = jnp.where(r >= c, out_ref[...], 0.0)


def middle_kernel(steps, m_ref, out_ref):
    out_ref[...] = m_ref[...]
    eliminate(out_ref, m_ref.shape[0], steps)


def reflect_kernel(inverse_ref, top_ref, sign_ref, turned_ref):
    n = top_ref.shape[0]
    r, c = square_places(n)
    q1t = mm_nt(inverse_ref[...], top_ref[...])
    diagonal = jnp.sum(jnp.where(r == c, q1t, 0.0), axis=0, keepdims=True)
    sign = jnp.where(diagonal >= 0, -1.0, 1.0)
    sign_ref[...] = sign
    turned_ref[...] = jnp.where(r == c, q1t - sign, q1t)


def outer_first_kernel(steps, turned_ref, m_ref):
    m_ref[...] = mm_nt(turned_ref[...], turned_ref[...])
    eliminate(m_ref, m_ref.shape[0], steps)


def outer_last_kernel(steps, m_ref, turned_ref, sign_ref, tft_ref):
    n = m_ref.shape[0]
    r, c = square_places(n)
    tft_ref[...] = m_ref[...]
    eliminate(tft_ref, n, steps)
    root = jnp.where(r >= c, tft_ref[...], 0.0)
    tft_ref[...] = -mm(mm_tn(root, root), turned_ref[...]) * sign_ref[...]


def half_z_kernel(mine_ref, theirs_ref, tft_ref, z_ref):
    z_ref[...] = 0.5 * mm_nt(mm(tft_ref[...], unpacked(mine_ref[...] + theirs_ref[...])), tft_ref[...])


def swap(x, axis):
    return lax.all_to_all(x, axis, 0, 0, tiled=True)


def gathered(x, axis):
    return swap(jnp.broadcast_to(x[None], (lax.axis_size(axis), *x.shape)), axis)


def other_core(x):
    return lax.ppermute(x, CORE, [(0, 1), (1, 0)])


def in_core_order(mine, core, axis):
    theirs = other_core(mine)
    first = core == 0
    return jnp.stack([jnp.where(first, mine, theirs), jnp.where(first, theirs, mine)], axis)


def to_mirror(piece):
    rows, cols = lax.axis_size(ROW), lax.axis_size(COL)
    pairs = []
    for r in range(rows):
        for c in range(cols):
            to_row, to_col = r // cols * cols + c, r % cols
            pairs.append((r * cols + c, to_row * cols + to_col))
    return lax.ppermute(piece, ROW + COL, pairs)


def cut_rows(x, blocks, peers):
    width = x.shape[-1]
    return x.reshape(blocks, peers, -1, width).transpose(1, 0, 2, 3).reshape(peers, -1, width)


def joined_rows(slabs, blocks):
    peers, _, width = slabs.shape
    return slabs.reshape(peers, blocks, -1, width).transpose(1, 0, 2, 3).reshape(-1, width)


def mirror_rows(mine, core, blocks):
    far, near = lax.axis_size("x_lo"), lax.axis_size("z")
    width = mine.shape[-1]
    both = in_core_order(mine.reshape(far, near, blocks, -1, width), core, 2)
    return both.transpose(3, 0, 1, 2, 4, 5).reshape(-1, width)


def untile_kernel(wide, tiles_ref, a_ref):
    rows, lanes = a_ref.shape[0], tiles_ref.shape[1]
    for n in range(wide):
        a_ref[:, n * lanes:(n + 1) * lanes] = tiles_ref[pl.ds(n, rows, stride=wide), :]


def untiled(matrix_tiles):
    blocks, _, tile, wide, _, lanes = matrix_tiles.shape
    return pl.pallas_call(
        functools.partial(untile_kernel, wide),
        grid=(blocks,),
        in_specs=[pl.BlockSpec((tile * wide, lanes), lambda i: (i, 0))],
        out_specs=pl.BlockSpec((tile, wide * lanes), lambda i: (i, 0)),
        out_shape=jax.ShapeDtypeStruct((blocks * tile, wide * lanes), jnp.float32),
        compiler_params=pltpu.CompilerParams(vmem_limit_bytes=16 * 2**20),
    )(matrix_tiles.reshape(blocks * tile * wide, lanes))


def tile_kernel(wide, a_ref, tiles_ref):
    rows, lanes = a_ref.shape[0], tiles_ref.shape[1]
    for n in range(wide):
        tiles_ref[pl.ds(n, rows, stride=wide), :] = a_ref[:, n * lanes:(n + 1) * lanes]


def tiled(a, shape):
    blocks, _, tile, wide, _, lanes = shape
    return pl.pallas_call(
        functools.partial(tile_kernel, wide),
        grid=(blocks,),
        in_specs=[pl.BlockSpec((tile, wide * lanes), lambda i: (i, 0))],
        out_specs=pl.BlockSpec((tile * wide, lanes), lambda i: (i, 0)),
        out_shape=jax.ShapeDtypeStruct((blocks * tile * wide, lanes), jnp.float32),
        compiler_params=pltpu.CompilerParams(vmem_limit_bytes=16 * 2**20),
    )(a).reshape(shape)


def after(x, other):
    return lax.optimization_barrier((x, other))[0]


def on_device(matrix_tiles):
    tile_shape = matrix_tiles.shape
    blocks, tile, wide = tile_shape[0], tile_shape[2], tile_shape[3]
    band = 2 * tile
    rows, cols = lax.axis_size(ROW), lax.axis_size(COL)
    r, c, core = lax.axis_index(ROW), lax.axis_index(COL), lax.axis_index(CORE)
    a = untiled(matrix_tiles)
    slab = blocks * tile // cols
    part = band // cols
    lane = jnp.arange(band, dtype=jnp.int32)

    def places(count, peers, me):
        at = jnp.arange(count, dtype=jnp.int32)
        return (at // tile * peers + me) * tile + at % tile

    def pair(source, first):
        return jnp.concatenate([source[first], source[first + 1]], 1)

    def cleared(x, at, below):
        return jnp.where((at >= below)[:, None], x, 0.0)

    row_of, col_of = places(blocks * tile, rows, r), places(wide * tile, cols, c)
    own = jnp.arange(slab, dtype=jnp.int32)
    own_of = (own // (tile // cols) * rows + r) * tile + c * (tile // cols) + own % (tile // cols)

    source = swap(cut_rows(a[:, :tile], blocks, cols), COL)
    p_own, next_own = pair(source, 0), pair(source, 2)
    both_own = jnp.concatenate([p_own, next_own], 1)
    mirrored = to_mirror(both_own)
    arrived = gathered(both_own, COL)
    joined = joined_rows(arrived, blocks)
    p_rows, next_rows = cleared(joined[:, :band], row_of, band), joined[:, band:]
    mine = gathered(after(mirrored, arrived), PAIR)
    theirs = other_core(mine)
    far, near, held = lax.axis_size("x_lo"), lax.axis_size("z"), tile // cols
    shape = (far, near, blocks, held, 2 * band)
    mine, theirs = mine.reshape(shape), theirs.reshape(shape)
    gram, tops = 0.0, []
    for x, which in ((mine, core), (theirs, 1 - core)):
        i, z, m, t = (lax.broadcasted_iota(jnp.int32, shape[:4], d) for d in range(4))
        at = ((m * far + i) * cols + c) * tile + (2 * z + which) * held + t
        x = jnp.where((at >= band)[..., None], x[..., :band], 0.0)
        tops.append(x[0, :, 0])
        x = x.reshape(-1, band)
        gram = gram + mm_tn(x, x)
    top = jnp.stack([jnp.where(core == 0, tops[0], tops[1]), jnp.where(core == 0, tops[1], tops[0])], 1)
    top = top.reshape(tile, band)
    both = jnp.stack([jnp.where(core == 0, mine, theirs), jnp.where(core == 0, theirs, mine)], 2)
    both = both.transpose(3, 0, 1, 2, 4, 5).reshape(-1, 2 * band)
    p_cols, next_cols = cleared(both[:, :band], col_of, band), both[:, band:]
    square = (band, band)
    third = band // STEP // 3 + 1
    for panel in range(PANELS):
        below = (panel + 1) * band
        first = below // tile
        if panel:
            gram, top = mm_tn(p_cols, p_cols), p_cols[:tile]
        parts = gathered(packed(gram), COL)
        (inverse,) = call(whole_kernel, [square], parts)

        sent = [cut_rows(mm(a, p_cols), blocks, cols), jnp.broadcast_to(top[None], (cols, tile, band))]
        if panel:
            edge = cut_rows(a[:, :tile], blocks, cols)
            sent.append(jnp.concatenate([edge[:, :slab // 2], edge[:, slab // 2:]], 2))
        arrived = swap(after(jnp.concatenate(sent, 1), parts), COL)
        arrived, inverse = after((arrived, inverse), inverse)
        u_own = arrived[:, :slab].sum(0)
        top = arrived[first:first + 2, slab:slab + tile].reshape(square)
        edge_own = next_own
        if panel:
            edge = arrived[first:first + 2, slab + tile:]
            edge = jnp.concatenate([edge[:, :, :tile], edge[:, :, tile:]], 1)
            edge_own = jnp.concatenate([edge[0], edge[1]], 1)
        sign, turned = call(reflect_kernel, [(1, band), square], inverse, top, flops=10**9)

        def signs_at(at):
            return jnp.where(at[:, None] - below == lane[None, :], sign, 0.0)

        u_own = mm_nt(u_own, inverse) - edge_own * sign
        y_rows = mm_nt(p_rows, inverse) - signs_at(row_of)
        y_cols = mm_nt(p_cols, inverse) - signs_at(col_of)
        mirrored = to_mirror(u_own)
        arrived = gathered(u_own, COL)
        u_rows = joined_rows(arrived, blocks)
        (m1,) = call(functools.partial(outer_first_kernel, (0, third)), [square], turned)
        mirrored, m1 = after((mirrored, m1), arrived)
        sent = [mirrored] if panel else [mirrored, u_rows[:tile]]
        arrived = gathered(after(jnp.concatenate(sent, 0), m1), PAIR)
        (m2,) = call(functools.partial(middle_kernel, (third, 2 * third)), [square], m1)
        arrived, m2 = after((arrived, m2), m2)
        inner = gathered(after(packed(mm_tn(y_rows, u_rows)), arrived), PAIR)
        (tft,) = call(functools.partial(outer_last_kernel, (2 * third, band // STEP)), [square], after(m2, arrived), turned, sign)
        inner = after(inner, tft)
        packs = band // 2 + STEP
        mine = inner.sum(0)
        if panel == 0:
            mine = jnp.concatenate([mine, arrived[first // 2, slab:]], 0)
        theirs = other_core(mine)
        u_cols = mirror_rows(arrived[:, :slab], core, blocks)
        (half_z,) = call(half_z_kernel, [square], mine[:packs], theirs[:packs], tft, flops=10**9)
        w_rows = mm_nt(u_rows, tft) - mm(y_rows, half_z)
        w_cols = mm_nt(u_cols, tft) - mm(y_cols, half_z)
        if panel == 0:
            mine, theirs = mine[packs:], theirs[packs:]
            u_top = jnp.concatenate([jnp.where(core == 0, mine, theirs), jnp.where(core == 0, theirs, mine)], 0)
            y_top = mm_nt(top, inverse) - jnp.where(jnp.eye(band, dtype=bool), sign, 0.0)
            w_top = mm_nt(u_top, tft) - mm(y_top, half_z)
            tops = jnp.concatenate([w_top, y_top], 1)
            p_cols = cleared(next_cols - mm_nt(jnp.concatenate([y_cols, w_cols], 1), tops), col_of, below + band)
            p_rows = cleared(next_rows - mm_nt(jnp.concatenate([y_rows, w_rows], 1), tops), row_of, below + band)
        a = a - mm_nt(jnp.concatenate([y_rows, w_rows], 1), jnp.concatenate([w_cols, y_cols], 1))
    return tiled(a, tile_shape)


def solution(mesh):
    finer = Mesh(mesh.devices.reshape(2, 4, 2, 2, 4), ("x_lo", "z", "core", "x_hi", "y"))
    spec = P(None, ROW, None, None, COL, None)
    return jax.shard_map(on_device, mesh=finer, in_specs=(spec,), out_specs=spec, check_vma=False)
```

```python
import functools

import jax
import jax.numpy as jnp
from jax import lax
from jax.experimental import pallas as pl
from jax.experimental.pallas import tpu as pltpu
from jax.sharding import Mesh
from jax.sharding import PartitionSpec as P

PANELS = 2
PAIR = ("x_lo", "z")
CORE = "core"
ROW = ("x_lo", "z", "core")
COL = ("x_hi", "y")
HI = lax.Precision.HIGHEST


def mm(a, b):
    return lax.dot_general(a, b, (((1,), (0,)), ((), ())), precision=HI, preferred_element_type=jnp.float32)


def mm_nt(a, b):
    return lax.dot_general(a, b, (((1,), (1,)), ((), ())), precision=HI, preferred_element_type=jnp.float32)


def mm_tn(a, b):
    return lax.dot_general(a, b, (((0,), (0,)), ((), ())), precision=HI, preferred_element_type=jnp.float32)


STEP = 8


def entries(block):
    columns = [jnp.broadcast_to(block[:, j:j + 1], (STEP, 128)) for j in range(STEP)]
    return [[jnp.broadcast_to(columns[j][i:i + 1, :], (STEP, 128)) if j <= i else None for j in range(STEP)] for i in range(STEP)]


def inverse_root(a):
    y = lax.rsqrt(a)
    return y * (1.5 - (0.5 * a) * (y * y))


def chol_inverse_8(a):
    a = [list(row) for row in a]
    x = [[None] * STEP for _ in range(STEP)]
    for k in range(STEP):
        x[k][k] = inverse_root(a[k][k])
        for i in range(k + 1, STEP):
            a[i][k] = a[i][k] * x[k][k]
        for j in range(k + 1, STEP):
            for i in range(j, STEP):
                a[i][j] = a[i][j] - a[i][k] * a[j][k]
    for k in range(STEP):
        for j in range(k):
            s = a[k][j] * x[j][j]
            for q in range(j + 1, k):
                s = s + a[k][q] * x[q][j]
            x[k][j] = -s * x[k][k]
    return x


def apply_lower(x, rows, sub):
    columns = []
    for j in range(STEP):
        col = x[STEP - 1][j]
        for i in range(STEP - 2, j - 1, -1):
            col = jnp.where(sub == i, x[i][j], col)
        columns.append(jnp.where(sub >= j, col, 0.0) if j else col)
    parts = []
    for c in range(0, rows.shape[1], 128):
        terms = [columns[j] * rows[j:j + 1, c:c + 128] for j in range(STEP)]
        while len(terms) > 1:
            terms = [terms[i] + terms[i + 1] for i in range(0, len(terms), 2)]
        parts.append(terms[0])
    return jnp.concatenate(parts, 1)


def three(x):
    hi = x.astype(jnp.bfloat16).astype(jnp.float32)
    rest = x - hi
    mid = rest.astype(jnp.bfloat16).astype(jnp.float32)
    return hi, mid, rest - mid


def outer(left, right):
    a, b, c = three(left)
    d, e, f = three(right)
    lefts = jnp.concatenate([a, a, b, a, c, b], 0).astype(jnp.bfloat16)
    rights = jnp.concatenate([d, e, d, f, d, e], 0).astype(jnp.bfloat16)
    return lax.dot_general(lefts, rights, (((0,), (0,)), ((), ())), preferred_element_type=jnp.float32)


def eliminate(m_ref, n, steps):
    lanes8 = lax.broadcasted_iota(jnp.int32, (STEP, n), 1)
    subs8 = lax.broadcasted_iota(jnp.int32, (STEP, n), 0)
    sub = lax.broadcasted_iota(jnp.int32, (STEP, 128), 0)
    low = steps[0] * STEP
    lanes = lax.broadcasted_iota(jnp.int32, (n - low, n), 1)
    rows_of = lax.broadcasted_iota(jnp.int32, (n - low, n), 0) + low

    def body(k, _):
        at = pl.multiple_of(k * STEP, STEP)
        rows = m_ref[pl.ds(at, STEP), :]
        block = pltpu.roll(rows, n - at, 1)[:, :STEP]
        here = (lanes8 >= at) & (lanes8 < at + STEP)
        unit = jnp.where(here, (lanes8 - at == subs8).astype(jnp.float32), rows)
        kept = apply_lower(chol_inverse_8(entries(block)), unit, sub)
        m_ref[pl.ds(at, STEP), :] = kept
        m = m_ref[low:, :]
        cleared = (lanes >= at) & (lanes < at + STEP) & (rows_of >= at + STEP)
        left = jnp.where(lanes8 >= at + STEP, kept, 0.0)
        m_ref[low:, :] = jnp.where(cleared, 0.0, m) - outer(left, kept)[low:, :]
        return 0

    lax.fori_loop(*steps, body, 0)


def square_places(n):
    return lax.broadcasted_iota(jnp.int32, (n, n), 0), lax.broadcasted_iota(jnp.int32, (n, n), 1)


def packed(m):
    h = m.shape[0] // 2
    r, c = square_places(h)
    low, high = m[:h, :h], m[h:, h:]
    diagonal = jnp.sum(jnp.where(r == c, high, 0.0), axis=0, keepdims=True)
    last = jnp.pad(diagonal, ((0, STEP - 1), (0, h)))
    return jnp.concatenate([jnp.concatenate([m[h:, :h], jnp.where(r >= c, low, high)], 1), last], 0)


def unpacked(p):
    h = p.shape[1] // 2
    r, c = square_places(h)
    corner, both, diagonal = p[:h, :h], p[:h, h:], p[h:h + 1, :h]
    flipped = both.T
    low = jnp.where(r >= c, both, flipped)
    high = jnp.where(r == c, diagonal, jnp.where(r < c, both, flipped))
    return jnp.concatenate(
        [jnp.concatenate([low, corner.T], 1), jnp.concatenate([corner, high], 1)], 0
    )


def call(kernel, shapes, *operands, flops=10**10):
    return pl.pallas_call(
        kernel,
        out_shape=[jax.ShapeDtypeStruct(s, jnp.float32) for s in shapes],
        compiler_params=pltpu.CompilerParams(vmem_limit_bytes=24 * 2**20),
        cost_estimate=pl.CostEstimate(flops=flops, bytes_accessed=2**20, transcendentals=0),
    )(*operands)


def whole_kernel(parts_ref, out_ref):
    n = out_ref.shape[0]
    r, c = square_places(n)
    total = parts_ref[0]
    for i in range(1, parts_ref.shape[0]):
        total = total + parts_ref[i]
    out_ref[...] = unpacked(total)
    for i in range(0, n // STEP, 8):
        eliminate(out_ref, n, (i, i + 8))
    out_ref[...] = jnp.where(r >= c, out_ref[...], 0.0)


def middle_kernel(steps, m_ref, out_ref):
    out_ref[...] = m_ref[...]
    eliminate(out_ref, m_ref.shape[0], steps)


def reflect_kernel(inverse_ref, top_ref, sign_ref, turned_ref):
    n = top_ref.shape[0]
    r, c = square_places(n)
    q1t = mm_nt(inverse_ref[...], top_ref[...])
    diagonal = jnp.sum(jnp.where(r == c, q1t, 0.0), axis=0, keepdims=True)
    sign = jnp.where(diagonal >= 0, -1.0, 1.0)
    sign_ref[...] = sign
    turned_ref[...] = jnp.where(r == c, q1t - sign, q1t)


def outer_first_kernel(steps, turned_ref, m_ref):
    m_ref[...] = mm_nt(turned_ref[...], turned_ref[...])
    eliminate(m_ref, m_ref.shape[0], steps)


def outer_last_kernel(steps, m_ref, turned_ref, sign_ref, tft_ref):
    n = m_ref.shape[0]
    r, c = square_places(n)
    tft_ref[...] = m_ref[...]
    eliminate(tft_ref, n, steps)
    root = jnp.where(r >= c, tft_ref[...], 0.0)
    tft_ref[...] = -mm(mm_tn(root, root), turned_ref[...]) * sign_ref[...]


def half_z_of(mine_ref, theirs_ref, tft_ref):
    return 0.5 * mm_nt(mm(tft_ref[...], unpacked(mine_ref[...] + theirs_ref[...])), tft_ref[...])


def top_z_kernel(mine_ref, theirs_ref, tft_ref, top_ref, z_ref, side_ref):
    z = half_z_of(mine_ref, theirs_ref, tft_ref)
    z_ref[...] = z
    side_ref[...] = mm_nt(z + z.T, top_ref[...])


def half_z_kernel(mine_ref, theirs_ref, tft_ref, z_ref):
    z_ref[...] = half_z_of(mine_ref, theirs_ref, tft_ref)


def swap(x, axis):
    return lax.all_to_all(x, axis, 0, 0, tiled=True)


def gathered(x, axis):
    return swap(jnp.broadcast_to(x[None], (lax.axis_size(axis), *x.shape)), axis)


def other_core(x):
    return lax.ppermute(x, CORE, [(0, 1), (1, 0)])


def in_core_order(mine, core, axis):
    theirs = other_core(mine)
    first = core == 0
    return jnp.stack([jnp.where(first, mine, theirs), jnp.where(first, theirs, mine)], axis)


def to_mirror(piece):
    rows, cols = lax.axis_size(ROW), lax.axis_size(COL)
    pairs = []
    for r in range(rows):
        for c in range(cols):
            to_row, to_col = r // cols * cols + c, r % cols
            pairs.append((r * cols + c, to_row * cols + to_col))
    return lax.ppermute(piece, ROW + COL, pairs)


def from_chip(x, near):
    count = lax.axis_size("z")
    here = (lax.axis_index("x_lo") == 0) & (lax.axis_index("z") == near)
    x = jnp.where(here, x, 0.0)
    x = x + lax.ppermute(x, "x_lo", [(0, 1)])
    up, down = (near + 1) % count, (near - 1) % count
    x = x + lax.ppermute(x, "z", [(near, up)]) + lax.ppermute(x, "z", [(near, down)])
    return x + lax.ppermute(x, "z", [(up, (up + 1) % count)])


def cut_rows(x, blocks, peers):
    width = x.shape[-1]
    return x.reshape(blocks, peers, -1, width).transpose(1, 0, 2, 3).reshape(peers, -1, width)


def joined_rows(slabs, blocks):
    peers, _, width = slabs.shape
    return slabs.reshape(peers, blocks, -1, width).transpose(1, 0, 2, 3).reshape(-1, width)


def mirror_rows(mine, core, blocks):
    far, near = lax.axis_size("x_lo"), lax.axis_size("z")
    width = mine.shape[-1]
    both = in_core_order(mine.reshape(far, near, blocks, -1, width), core, 2)
    return both.transpose(3, 0, 1, 2, 4, 5).reshape(-1, width)


def untile_kernel(wide, tiles_ref, a_ref):
    rows, lanes = a_ref.shape[0], tiles_ref.shape[1]
    for n in range(wide):
        a_ref[:, n * lanes:(n + 1) * lanes] = tiles_ref[pl.ds(n, rows, stride=wide), :]


def untiled(matrix_tiles):
    blocks, _, tile, wide, _, lanes = matrix_tiles.shape
    return pl.pallas_call(
        functools.partial(untile_kernel, wide),
        grid=(blocks,),
        in_specs=[pl.BlockSpec((tile * wide, lanes), lambda i: (i, 0))],
        out_specs=pl.BlockSpec((tile, wide * lanes), lambda i: (i, 0)),
        out_shape=jax.ShapeDtypeStruct((blocks * tile, wide * lanes), jnp.float32),
        compiler_params=pltpu.CompilerParams(vmem_limit_bytes=16 * 2**20),
    )(matrix_tiles.reshape(blocks * tile * wide, lanes))


def tile_kernel(wide, a_ref, tiles_ref):
    rows, lanes = a_ref.shape[0], tiles_ref.shape[1]
    for n in range(wide):
        tiles_ref[pl.ds(n, rows, stride=wide), :] = a_ref[:, n * lanes:(n + 1) * lanes]


def tiled(a, shape):
    blocks, _, tile, wide, _, lanes = shape
    return pl.pallas_call(
        functools.partial(tile_kernel, wide),
        grid=(blocks,),
        in_specs=[pl.BlockSpec((tile, wide * lanes), lambda i: (i, 0))],
        out_specs=pl.BlockSpec((tile * wide, lanes), lambda i: (i, 0)),
        out_shape=jax.ShapeDtypeStruct((blocks * tile * wide, lanes), jnp.float32),
        compiler_params=pltpu.CompilerParams(vmem_limit_bytes=16 * 2**20),
    )(a).reshape(shape)


def after(x, other):
    return lax.optimization_barrier((x, other))[0]


def on_device(matrix_tiles):
    tile_shape = matrix_tiles.shape
    blocks, tile, wide = tile_shape[0], tile_shape[2], tile_shape[3]
    band = 2 * tile
    rows, cols = lax.axis_size(ROW), lax.axis_size(COL)
    r, c, core = lax.axis_index(ROW), lax.axis_index(COL), lax.axis_index(CORE)
    a = untiled(matrix_tiles)
    slab = blocks * tile // cols
    part = band // cols
    lane = jnp.arange(band, dtype=jnp.int32)

    def places(count, peers, me):
        at = jnp.arange(count, dtype=jnp.int32)
        return (at // tile * peers + me) * tile + at % tile

    def pair(source, first):
        return jnp.concatenate([source[first], source[first + 1]], 1)

    def cleared(x, at, below):
        return jnp.where((at >= below)[:, None], x, 0.0)

    row_of, col_of = places(blocks * tile, rows, r), places(wide * tile, cols, c)

    source = swap(cut_rows(a[:, :tile], blocks, cols), COL)
    p_own, next_own = pair(source, 0), pair(source, 2)
    mirrored = to_mirror(p_own)
    arrived = gathered(p_own, COL)
    p_rows = cleared(joined_rows(arrived, blocks), row_of, band)
    mine = gathered(after(mirrored, arrived), PAIR)
    mine, p_rows = after((mine, p_rows), p_rows)
    theirs = other_core(mine)
    far, near, held = lax.axis_size("x_lo"), lax.axis_size("z"), tile // cols
    shape = (far, near, blocks, held, band)
    mine, theirs = mine.reshape(shape), theirs.reshape(shape)
    gram, tops = 0.0, []
    for x, which in ((mine, core), (theirs, 1 - core)):
        i, z, m, t = (lax.broadcasted_iota(jnp.int32, shape[:4], d) for d in range(4))
        at = ((m * far + i) * cols + c) * tile + (2 * z + which) * held + t
        x = jnp.where((at >= band)[..., None], x, 0.0)
        tops.append(x[0, :, 0])
        x = x.reshape(-1, band)
        gram = gram + mm_tn(x, x)
    top = jnp.stack([jnp.where(core == 0, tops[0], tops[1]), jnp.where(core == 0, tops[1], tops[0])], 1)
    top = top.reshape(tile, band)
    both = jnp.stack([jnp.where(core == 0, mine, theirs), jnp.where(core == 0, theirs, mine)], 2)
    p_cols = cleared(both.transpose(3, 0, 1, 2, 4, 5).reshape(-1, band), col_of, band)
    square = (band, band)
    third = band // STEP // 3 + 1
    for panel in range(PANELS):
        below = (panel + 1) * band
        first = below // tile
        if panel:
            gram, top = mm_tn(p_cols, p_cols), p_cols[:tile]
        parts = gathered(packed(gram), COL)
        (inverse,) = call(whole_kernel, [square], parts)

        sent = [cut_rows(mm(a, p_cols), blocks, cols), jnp.broadcast_to(top[None], (cols, tile, band))]
        if panel:
            edge = cut_rows(a[:, :tile], blocks, cols)
            sent.append(jnp.concatenate([edge[:, :slab // 2], edge[:, slab // 2:]], 2))
        else:
            sent.append(jnp.broadcast_to(next_own[None], (cols, slab, band)))
        arrived = swap(after(jnp.concatenate(sent, 1), parts), COL)
        arrived, inverse = after((arrived, inverse), inverse)
        u_own = arrived[:, :slab].sum(0)
        top = arrived[first:first + 2, slab:slab + tile].reshape(square)
        edge_own = next_own
        if panel:
            edge = arrived[first:first + 2, slab + tile:]
            edge = jnp.concatenate([edge[:, :, :tile], edge[:, :, tile:]], 1)
            edge_own = jnp.concatenate([edge[0], edge[1]], 1)
        else:
            next_rows = joined_rows(arrived[:, slab + tile:], blocks)
        sign, turned = call(reflect_kernel, [(1, band), square], inverse, top, flops=10**9)

        def signs_at(at):
            return jnp.where(at[:, None] - below == lane[None, :], sign, 0.0)

        u_own = mm_nt(u_own, inverse) - edge_own * sign
        y_rows = mm_nt(p_rows, inverse) - signs_at(row_of)
        y_cols = mm_nt(p_cols, inverse) - signs_at(col_of)
        if panel == 0:
            y_rows, y_cols, turned = after((y_rows, y_cols, turned), (y_rows, y_cols))
        mirrored = to_mirror(u_own if panel else jnp.concatenate([u_own, next_own], 1))
        arrived = gathered(u_own, COL)
        u_rows = joined_rows(arrived, blocks)
        (m1,) = call(functools.partial(outer_first_kernel, (0, third)), [square], turned)
        mirrored, m1 = after((mirrored, m1), arrived)
        if panel == 0:
            u_top = from_chip(u_rows[:tile], first // 2)
            mirrored = jnp.concatenate([mirrored[:, :band], mirrored[:, band:]], 0)
        arrived = gathered(after(mirrored, m1), PAIR)
        (m2,) = call(functools.partial(middle_kernel, (third, 2 * third)), [square], m1)
        arrived, m2 = after((arrived, m2), m2)
        inner = gathered(after(packed(mm_tn(y_rows, u_rows)), arrived), PAIR)
        (tft,) = call(functools.partial(outer_last_kernel, (2 * third, band // STEP)), [square], after(m2, arrived), turned, sign)
        inner = after(inner, tft)
        packs = band // 2 + STEP
        mine = inner.sum(0)
        theirs = other_core(mine)
        u_cols = mirror_rows(arrived[:, :slab], core, blocks)
        late = after(tft, inner)
        x_rows, x_cols = mm_nt(u_rows, tft if panel else late), mm_nt(u_cols, late)
        if panel == 0:
            next_cols = mirror_rows(arrived[:, slab:], core, blocks)
            u_other = other_core(u_top)
            u_top = jnp.concatenate([jnp.where(core == 0, u_top, u_other), jnp.where(core == 0, u_other, u_top)], 0)
            y_top = mm_nt(top, inverse) - jnp.where(jnp.eye(band, dtype=bool), sign, 0.0)
            tops = jnp.concatenate([mm_nt(u_top, late), y_top], 1)
            p_cols = next_cols - mm_nt(jnp.concatenate([y_cols, x_cols], 1), tops)
            p_rows = next_rows - mm_nt(jnp.concatenate([y_rows, x_rows], 1), tops)
            half_z, side = call(top_z_kernel, [square, square], mine, theirs, tft, y_top, flops=10**9)
            p_cols = cleared(p_cols + mm(y_cols, side), col_of, below + band)
            p_rows = cleared(p_rows + mm(y_rows, side), row_of, below + band)
        else:
            (half_z,) = call(half_z_kernel, [square], mine, theirs, tft, flops=10**9)
        left = jnp.concatenate([y_rows, x_rows - mm(y_rows, half_z)], 1)
        a = a - mm_nt(left, jnp.concatenate([x_cols - mm(y_cols, half_z), y_cols], 1))
    return tiled(a, tile_shape)


def solution(mesh):
    finer = Mesh(mesh.devices.reshape(2, 4, 2, 2, 4), ("x_lo", "z", "core", "x_hi", "y"))
    spec = P(None, ROW, None, None, COL, None)
    return jax.shard_map(on_device, mesh=finer, in_specs=(spec,), out_specs=spec, check_vma=False)
```

```python
import functools

import jax
import jax.numpy as jnp
from jax import lax
from jax.experimental import pallas as pl
from jax.experimental.pallas import tpu as pltpu
from jax.sharding import Mesh
from jax.sharding import PartitionSpec as P

PANELS = 2
PAIR = ("x_lo", "z")
CORE = "core"
ROW = ("x_lo", "z", "core")
COL = ("x_hi", "y")
HI = lax.Precision.HIGHEST


def mm(a, b):
    return lax.dot_general(a, b, (((1,), (0,)), ((), ())), precision=HI, preferred_element_type=jnp.float32)


def mm_nt(a, b):
    return lax.dot_general(a, b, (((1,), (1,)), ((), ())), precision=HI, preferred_element_type=jnp.float32)


def mm_tn(a, b):
    return lax.dot_general(a, b, (((0,), (0,)), ((), ())), precision=HI, preferred_element_type=jnp.float32)


STEP = 8


def entries(block):
    columns = [jnp.broadcast_to(block[:, j:j + 1], (STEP, 128)) for j in range(STEP)]
    return [[jnp.broadcast_to(columns[j][i:i + 1, :], (STEP, 128)) if j <= i else None for j in range(STEP)] for i in range(STEP)]


def inverse_root(a):
    y = lax.rsqrt(a)
    return y * (1.5 - (0.5 * a) * (y * y))


def chol_inverse_8(a):
    a = [list(row) for row in a]
    x = [[None] * STEP for _ in range(STEP)]
    for k in range(STEP):
        x[k][k] = inverse_root(a[k][k])
        for i in range(k + 1, STEP):
            a[i][k] = a[i][k] * x[k][k]
        for j in range(k + 1, STEP):
            for i in range(j, STEP):
                a[i][j] = a[i][j] - a[i][k] * a[j][k]
    for k in range(STEP):
        for j in range(k):
            s = a[k][j] * x[j][j]
            for q in range(j + 1, k):
                s = s + a[k][q] * x[q][j]
            x[k][j] = -s * x[k][k]
    return x


def apply_lower(x, rows, sub):
    columns = []
    for j in range(STEP):
        col = x[STEP - 1][j]
        for i in range(STEP - 2, j - 1, -1):
            col = jnp.where(sub == i, x[i][j], col)
        columns.append(jnp.where(sub >= j, col, 0.0) if j else col)
    parts = []
    for c in range(0, rows.shape[1], 128):
        terms = [columns[j] * rows[j:j + 1, c:c + 128] for j in range(STEP)]
        while len(terms) > 1:
            terms = [terms[i] + terms[i + 1] for i in range(0, len(terms), 2)]
        parts.append(terms[0])
    return jnp.concatenate(parts, 1)


def three(x):
    hi = x.astype(jnp.bfloat16).astype(jnp.float32)
    rest = x - hi
    mid = rest.astype(jnp.bfloat16).astype(jnp.float32)
    return hi, mid, rest - mid


def outer(left, right):
    a, b, c = three(left)
    d, e, f = three(right)
    lefts = jnp.concatenate([a, a, b, a, c, b], 0).astype(jnp.bfloat16)
    rights = jnp.concatenate([d, e, d, f, d, e], 0).astype(jnp.bfloat16)
    return lax.dot_general(lefts, rights, (((0,), (0,)), ((), ())), preferred_element_type=jnp.float32)


def eliminate(m_ref, n, steps):
    lanes8 = lax.broadcasted_iota(jnp.int32, (STEP, n), 1)
    subs8 = lax.broadcasted_iota(jnp.int32, (STEP, n), 0)
    sub = lax.broadcasted_iota(jnp.int32, (STEP, 128), 0)
    low = steps[0] * STEP
    lanes = lax.broadcasted_iota(jnp.int32, (n - low, n), 1)
    rows_of = lax.broadcasted_iota(jnp.int32, (n - low, n), 0) + low

    def body(k, _):
        at = pl.multiple_of(k * STEP, STEP)
        rows = m_ref[pl.ds(at, STEP), :]
        block = pltpu.roll(rows, n - at, 1)[:, :STEP]
        here = (lanes8 >= at) & (lanes8 < at + STEP)
        unit = jnp.where(here, (lanes8 - at == subs8).astype(jnp.float32), rows)
        kept = apply_lower(chol_inverse_8(entries(block)), unit, sub)
        m_ref[pl.ds(at, STEP), :] = kept
        m = m_ref[low:, :]
        cleared = (lanes >= at) & (lanes < at + STEP) & (rows_of >= at + STEP)
        left = jnp.where(lanes8 >= at + STEP, kept, 0.0)
        m_ref[low:, :] = jnp.where(cleared, 0.0, m) - outer(left, kept)[low:, :]
        return 0

    lax.fori_loop(*steps, body, 0)


def square_places(n):
    return lax.broadcasted_iota(jnp.int32, (n, n), 0), lax.broadcasted_iota(jnp.int32, (n, n), 1)


def packed(m):
    h = m.shape[0] // 2
    r, c = square_places(h)
    low, high = m[:h, :h], m[h:, h:]
    diagonal = jnp.sum(jnp.where(r == c, high, 0.0), axis=0, keepdims=True)
    last = jnp.pad(diagonal, ((0, STEP - 1), (0, h)))
    return jnp.concatenate([jnp.concatenate([m[h:, :h], jnp.where(r >= c, low, high)], 1), last], 0)


def unpacked(p):
    h = p.shape[1] // 2
    r, c = square_places(h)
    corner, both, diagonal = p[:h, :h], p[:h, h:], p[h:h + 1, :h]
    flipped = both.T
    low = jnp.where(r >= c, both, flipped)
    high = jnp.where(r == c, diagonal, jnp.where(r < c, both, flipped))
    return jnp.concatenate(
        [jnp.concatenate([low, corner.T], 1), jnp.concatenate([corner, high], 1)], 0
    )


def call(kernel, shapes, *operands, flops=10**10):
    return pl.pallas_call(
        kernel,
        out_shape=[jax.ShapeDtypeStruct(s, jnp.float32) for s in shapes],
        compiler_params=pltpu.CompilerParams(vmem_limit_bytes=24 * 2**20),
        cost_estimate=pl.CostEstimate(flops=flops, bytes_accessed=2**20, transcendentals=0),
    )(*operands)


def whole_kernel(parts_ref, out_ref):
    n = out_ref.shape[0]
    r, c = square_places(n)
    total = parts_ref[0]
    for i in range(1, parts_ref.shape[0]):
        total = total + parts_ref[i]
    out_ref[...] = unpacked(total)
    for i in range(0, n // STEP, 8):
        eliminate(out_ref, n, (i, i + 8))
    out_ref[...] = jnp.where(r >= c, out_ref[...], 0.0)


def middle_kernel(steps, m_ref, out_ref):
    out_ref[...] = m_ref[...]
    eliminate(out_ref, m_ref.shape[0], steps)


def columns_kernel(shape, mine_ref, theirs_ref, even_ref, kept_ref, columns_ref, parts_ref):
    far, near, blocks, held, tile = shape
    even = even_ref[...] > 0.0
    kept = kept_ref[...] > 0.0
    for i in range(far):
        for z in range(near):
            for m in range(blocks):
                a = mine_ref[i * near + z, m * held:(m + 1) * held, :]
                b = theirs_ref[i * near + z, m * held:(m + 1) * held, :]
                pair = jnp.concatenate([jnp.where(even, a, b), jnp.where(even, b, a)], 0)
                if m == 0 and i == 0:
                    pair = jnp.where(kept, pair, 0.0)
                columns_ref[pl.ds((m * far + i) * tile + z * 2 * held, 2 * held), :] = pair
    columns = columns_ref[...]
    spread(packed(mm_tn(columns, columns)), parts_ref)


def spread(x, parts_ref):
    for i in range(parts_ref.shape[0]):
        parts_ref[i] = x


def gram_kernel(columns_ref, parts_ref):
    spread(packed(mm_tn(columns_ref[...], columns_ref[...])), parts_ref)


def inner_kernel(shape, y_ref, arrived_ref, parts_ref, *gathered_refs):
    blocks, held, tile = shape
    u_ref = gathered_refs[0]
    for k, rows_ref in enumerate(gathered_refs):
        for c in range(arrived_ref.shape[0]):
            for m in range(blocks):
                at = (k * blocks + m) * held
                rows_ref[pl.ds(m * tile + c * held, held), :] = arrived_ref[c, at:at + held, :]
    spread(packed(mm_tn(y_ref[...], u_ref[...])), parts_ref)


def reflect_kernel(first, slab, inside, arrived_ref, inverse_ref, edge_ref, sign_ref, turned_ref, top_ref, parts_ref, own_ref):
    n = inverse_ref.shape[0]
    r, c = square_places(n)
    tile = n // 2
    for i in range(2):
        top_ref[i * tile:(i + 1) * tile, :] = arrived_ref[first + i, slab:slab + tile, :]
    q1t = mm_nt(inverse_ref[...], top_ref[...])
    diagonal = jnp.sum(jnp.where(r == c, q1t, 0.0), axis=0, keepdims=True)
    sign = jnp.where(diagonal >= 0, -1.0, 1.0)
    sign_ref[...] = sign
    turned_ref[...] = jnp.where(r == c, q1t - sign, q1t)
    total = arrived_ref[0, :slab, :]
    for i in range(1, arrived_ref.shape[0]):
        total = total + arrived_ref[i, :slab, :]
    if inside:
        halves = [arrived_ref[first + i, slab + tile:slab + tile + slab // 2, :] for i in range(2)]
        edge = jnp.concatenate([jnp.concatenate([x[:, :tile], x[:, tile:]], 0) for x in halves], 1)
    else:
        edge = edge_ref[...]
        own_ref[:, n:] = edge
        for i in range(parts_ref.shape[0]):
            parts_ref[i, slab:, :] = edge
    own = mm_nt(total, inverse_ref[...]) - edge * sign
    own_ref[:, :n] = own
    for i in range(parts_ref.shape[0]):
        parts_ref[i, :slab, :] = own


def outer_first_kernel(steps, turned_ref, m_ref):
    m_ref[...] = mm_nt(turned_ref[...], turned_ref[...])
    eliminate(m_ref, m_ref.shape[0], steps)


def outer_last_kernel(steps, m_ref, turned_ref, sign_ref, tft_ref):
    n = m_ref.shape[0]
    r, c = square_places(n)
    tft_ref[...] = m_ref[...]
    eliminate(tft_ref, n, steps)
    root = jnp.where(r >= c, tft_ref[...], 0.0)
    tft_ref[...] = -mm(mm_tn(root, root), turned_ref[...]) * sign_ref[...]


def half_z_of(mine_ref, theirs_ref, tft_ref):
    return 0.5 * mm_nt(mm(tft_ref[...], unpacked(mine_ref[...] + theirs_ref[...])), tft_ref[...])


def top_z_kernel(mine_ref, theirs_ref, tft_ref, top_ref, z_ref, side_ref):
    z = half_z_of(mine_ref, theirs_ref, tft_ref)
    z_ref[...] = z
    side_ref[...] = mm_nt(z + z.T, top_ref[...])


def half_z_kernel(mine_ref, theirs_ref, tft_ref, z_ref):
    z_ref[...] = half_z_of(mine_ref, theirs_ref, tft_ref)


def swap(x, axis):
    return lax.all_to_all(x, axis, 0, 0, tiled=True)


def gathered(x, axis):
    return swap(jnp.broadcast_to(x[None], (lax.axis_size(axis), *x.shape)), axis)


def other_core(x):
    return lax.ppermute(x, CORE, [(0, 1), (1, 0)])


def in_core_order(mine, core, axis):
    theirs = other_core(mine)
    first = core == 0
    return jnp.stack([jnp.where(first, mine, theirs), jnp.where(first, theirs, mine)], axis)


def to_mirror(piece):
    rows, cols = lax.axis_size(ROW), lax.axis_size(COL)
    pairs = []
    for r in range(rows):
        for c in range(cols):
            to_row, to_col = r // cols * cols + c, r % cols
            pairs.append((r * cols + c, to_row * cols + to_col))
    return lax.ppermute(piece, ROW + COL, pairs)


def cut_rows(x, blocks, peers):
    width = x.shape[-1]
    return x.reshape(blocks, peers, -1, width).transpose(1, 0, 2, 3).reshape(peers, -1, width)


def joined_rows(slabs, blocks):
    peers, _, width = slabs.shape
    return slabs.reshape(peers, blocks, -1, width).transpose(1, 0, 2, 3).reshape(-1, width)


def mirror_rows(mine, core, blocks):
    far, near = lax.axis_size("x_lo"), lax.axis_size("z")
    width = mine.shape[-1]
    both = in_core_order(mine.reshape(far, near, blocks, -1, width), core, 2)
    return both.transpose(3, 0, 1, 2, 4, 5).reshape(-1, width)


def untile_kernel(wide, tiles_ref, a_ref):
    rows, lanes = a_ref.shape[0], tiles_ref.shape[1]
    for n in range(wide):
        a_ref[:, n * lanes:(n + 1) * lanes] = tiles_ref[pl.ds(n, rows, stride=wide), :]


def untiled(matrix_tiles):
    blocks, _, tile, wide, _, lanes = matrix_tiles.shape
    return pl.pallas_call(
        functools.partial(untile_kernel, wide),
        grid=(blocks,),
        in_specs=[pl.BlockSpec((tile * wide, lanes), lambda i: (i, 0))],
        out_specs=pl.BlockSpec((tile, wide * lanes), lambda i: (i, 0)),
        out_shape=jax.ShapeDtypeStruct((blocks * tile, wide * lanes), jnp.float32),
        compiler_params=pltpu.CompilerParams(vmem_limit_bytes=16 * 2**20),
    )(matrix_tiles.reshape(blocks * tile * wide, lanes))


def tile_kernel(wide, a_ref, tiles_ref):
    rows, lanes = a_ref.shape[0], tiles_ref.shape[1]
    for n in range(wide):
        tiles_ref[pl.ds(n, rows, stride=wide), :] = a_ref[:, n * lanes:(n + 1) * lanes]


def tiled(a, shape):
    blocks, _, tile, wide, _, lanes = shape
    return pl.pallas_call(
        functools.partial(tile_kernel, wide),
        grid=(blocks,),
        in_specs=[pl.BlockSpec((tile, wide * lanes), lambda i: (i, 0))],
        out_specs=pl.BlockSpec((tile * wide, lanes), lambda i: (i, 0)),
        out_shape=jax.ShapeDtypeStruct((blocks * tile * wide, lanes), jnp.float32),
        compiler_params=pltpu.CompilerParams(vmem_limit_bytes=16 * 2**20),
    )(a).reshape(shape)


def after(x, other):
    return lax.optimization_barrier((x, other))[0]


def on_device(matrix_tiles):
    tile_shape = matrix_tiles.shape
    blocks, tile, wide = tile_shape[0], tile_shape[2], tile_shape[3]
    band = 2 * tile
    rows, cols = lax.axis_size(ROW), lax.axis_size(COL)
    r, c, core = lax.axis_index(ROW), lax.axis_index(COL), lax.axis_index(CORE)
    a = untiled(matrix_tiles)
    slab = blocks * tile // cols
    part = band // cols
    lane = jnp.arange(band, dtype=jnp.int32)

    def places(count, peers, me):
        at = jnp.arange(count, dtype=jnp.int32)
        return (at // tile * peers + me) * tile + at % tile

    def pair(source, first):
        return jnp.concatenate([source[first], source[first + 1]], 1)

    def cleared(x, at, below):
        return jnp.where((at >= below)[:, None], x, 0.0)

    row_of, col_of = places(blocks * tile, rows, r), places(wide * tile, cols, c)

    source = swap(cut_rows(a[:, :tile], blocks, cols), COL)
    p_own, next_own = pair(source, 0), pair(source, 2)
    mirrored = to_mirror(p_own)
    arrived = gathered(p_own, COL)
    p_rows = cleared(joined_rows(arrived, blocks), row_of, band)
    mine = gathered(after(mirrored, arrived), PAIR)
    mine, p_rows = after((mine, p_rows), p_rows)
    theirs = other_core(mine)
    far, near, held = lax.axis_size("x_lo"), lax.axis_size("z"), tile // cols
    even = jnp.broadcast_to((core == 0).astype(jnp.float32), (1, band))
    kept = jnp.broadcast_to((c >= band // tile).astype(jnp.float32), (1, band))
    packs = (cols, band // 2 + STEP, band)
    p_cols, parts = call(
        functools.partial(columns_kernel, (far, near, blocks, held, tile)),
        [(wide * tile, band), packs], mine, theirs, even, kept, flops=10**9,
    )
    square = (band, band)
    third = band // STEP // 3 + 1
    for panel in range(PANELS):
        below = (panel + 1) * band
        first = below // tile
        if panel:
            (parts,) = call(gram_kernel, [packs], p_cols, flops=10**9)
            late_z = after(half_z, parts)
            left = jnp.concatenate([y_rows, x_rows - mm(y_rows, late_z)], 1)
            a = a - mm_nt(left, jnp.concatenate([x_cols - mm(y_cols, late_z), y_cols], 1))
        top = p_cols[:tile]
        parts = swap(parts, COL)
        (inverse,) = call(whole_kernel, [square], parts)

        sent = [cut_rows(mm(a, p_cols), blocks, cols), jnp.broadcast_to(top[None], (cols, tile, band))]
        if panel:
            edge = cut_rows(a[:, :tile], blocks, cols)
            sent.append(jnp.concatenate([edge[:, :slab // 2], edge[:, slab // 2:]], 2))
        arrived = swap(after(jnp.concatenate(sent, 1), parts), COL)
        arrived, inverse = after((arrived, inverse), inverse)
        sign, turned, top, u_parts, u_own = call(
            functools.partial(reflect_kernel, first, slab, panel > 0),
            [(1, band), square, square, (cols, slab if panel else 2 * slab, band), (slab, band if panel else 2 * band)],
            arrived, inverse, next_own, flops=10**9,
        )
        def signs_at(at):
            return jnp.where(at[:, None] - below == lane[None, :], sign, 0.0)

        y_rows = mm_nt(p_rows, inverse) - signs_at(row_of)
        y_cols = mm_nt(p_cols, inverse) - signs_at(col_of)
        if panel == 0:
            y_rows, turned = after((y_rows, turned), y_rows)
        mirrored = to_mirror(u_own)
        arrived = swap(u_parts, COL)
        (m1,) = call(functools.partial(outer_first_kernel, (0, third)), [square], turned)
        arrived, m1 = after((arrived, m1), m1)
        mirrored, m1 = after((mirrored, m1), arrived)
        inner, u_rows, *more = call(
            functools.partial(inner_kernel, (blocks, held, tile)),
            [packs] + [(blocks * tile, band)] * (1 if panel else 2), y_rows, arrived, flops=10**9,
        )
        if panel == 0:
            mirrored = jnp.concatenate([mirrored[:, :band], mirrored[:, band:]], 0)
        arrived = gathered(after(mirrored, m1), PAIR)
        (m2,) = call(functools.partial(middle_kernel, (third, 2 * third)), [square], m1)
        arrived, m2 = after((arrived, m2), m2)
        if panel == 0:
            inner = jnp.concatenate([inner, jnp.broadcast_to(u_rows[None, :tile], (cols, tile, band))], 1)
        inner = swap(after(inner, arrived), PAIR)
        (tft,) = call(functools.partial(outer_last_kernel, (2 * third, band // STEP)), [square], after(m2, arrived), turned, sign)
        inner = after(inner, tft)
        mine = inner[:, :packs[1]].sum(0)
        theirs = other_core(mine)
        u_cols = mirror_rows(arrived[:, :slab], core, blocks)
        late = after(tft, inner)
        x_rows, x_cols = mm_nt(u_rows, tft if panel else late), mm_nt(u_cols, late)
        if panel == 0:
            next_cols = mirror_rows(arrived[:, slab:], core, blocks)
            u_top = inner[first // 2, packs[1]:]
            u_other = other_core(u_top)
            u_top = jnp.concatenate([jnp.where(core == 0, u_top, u_other), jnp.where(core == 0, u_other, u_top)], 0)
            y_top = mm_nt(top, inverse) - jnp.where(jnp.eye(band, dtype=bool), sign, 0.0)
            tops = jnp.concatenate([mm_nt(u_top, late), y_top], 1)
            p_cols = next_cols - mm_nt(jnp.concatenate([y_cols, x_cols], 1), tops)
            p_rows = more[0] - mm_nt(jnp.concatenate([y_rows, x_rows], 1), tops)
            half_z, side = call(top_z_kernel, [square, square], mine, theirs, tft, y_top, flops=10**9)
            p_cols = cleared(p_cols + mm(y_cols, side), col_of, below + band)
            p_rows = cleared(p_rows + mm(y_rows, side), row_of, below + band)
        else:
            (half_z,) = call(half_z_kernel, [square], mine, theirs, tft, flops=10**9)
            left = jnp.concatenate([y_rows, x_rows - mm(y_rows, half_z)], 1)
            a = a - mm_nt(left, jnp.concatenate([x_cols - mm(y_cols, half_z), y_cols], 1))
    return tiled(a, tile_shape)


def solution(mesh):
    finer = Mesh(mesh.devices.reshape(2, 4, 2, 2, 4), ("x_lo", "z", "core", "x_hi", "y"))
    spec = P(None, ROW, None, None, COL, None)
    return jax.shard_map(on_device, mesh=finer, in_specs=(spec,), out_specs=spec, check_vma=False)
```

```python
import functools

import jax
import jax.numpy as jnp
from jax import lax
from jax.experimental import pallas as pl
from jax.experimental.pallas import tpu as pltpu
from jax.sharding import Mesh
from jax.sharding import PartitionSpec as P

PANELS = 2
PAIR = ("x_lo", "z")
CORE = "core"
ROW = ("x_lo", "z", "core")
COL = ("x_hi", "y")
HI = lax.Precision.HIGHEST


def mm(a, b):
    return lax.dot_general(a, b, (((1,), (0,)), ((), ())), precision=HI, preferred_element_type=jnp.float32)


def mm_nt(a, b):
    return lax.dot_general(a, b, (((1,), (1,)), ((), ())), precision=HI, preferred_element_type=jnp.float32)


def mm_tn(a, b):
    return lax.dot_general(a, b, (((0,), (0,)), ((), ())), precision=HI, preferred_element_type=jnp.float32)


STEP = 8


def entries(block):
    columns = [jnp.broadcast_to(block[:, j:j + 1], (STEP, 128)) for j in range(STEP)]
    return [[jnp.broadcast_to(columns[j][i:i + 1, :], (STEP, 128)) if j <= i else None for j in range(STEP)] for i in range(STEP)]


def inverse_root(a):
    y = lax.rsqrt(a)
    return y * (1.5 - (0.5 * a) * (y * y))


def chol_inverse_8(a):
    a = [list(row) for row in a]
    x = [[None] * STEP for _ in range(STEP)]
    for k in range(STEP):
        x[k][k] = inverse_root(a[k][k])
        for i in range(k + 1, STEP):
            a[i][k] = a[i][k] * x[k][k]
        for j in range(k + 1, STEP):
            for i in range(j, STEP):
                a[i][j] = a[i][j] - a[i][k] * a[j][k]
    for k in range(STEP):
        for j in range(k):
            s = a[k][j] * x[j][j]
            for q in range(j + 1, k):
                s = s + a[k][q] * x[q][j]
            x[k][j] = -s * x[k][k]
    return x


def apply_lower(x, rows, sub):
    columns = []
    for j in range(STEP):
        col = x[STEP - 1][j]
        for i in range(STEP - 2, j - 1, -1):
            col = jnp.where(sub == i, x[i][j], col)
        columns.append(jnp.where(sub >= j, col, 0.0) if j else col)
    parts = []
    for c in range(0, rows.shape[1], 128):
        terms = [columns[j] * rows[j:j + 1, c:c + 128] for j in range(STEP)]
        while len(terms) > 1:
            terms = [terms[i] + terms[i + 1] for i in range(0, len(terms), 2)]
        parts.append(terms[0])
    return jnp.concatenate(parts, 1)


def three(x):
    hi = x.astype(jnp.bfloat16).astype(jnp.float32)
    rest = x - hi
    mid = rest.astype(jnp.bfloat16).astype(jnp.float32)
    return hi, mid, rest - mid


def outer(left, right):
    a, b, c = three(left)
    d, e, f = three(right)
    lefts = jnp.concatenate([a, a, b, a, c, b], 0).astype(jnp.bfloat16)
    rights = jnp.concatenate([d, e, d, f, d, e], 0).astype(jnp.bfloat16)
    return lax.dot_general(lefts, rights, (((0,), (0,)), ((), ())), preferred_element_type=jnp.float32)


def eliminate(m_ref, n, steps):
    lanes8 = lax.broadcasted_iota(jnp.int32, (STEP, n), 1)
    subs8 = lax.broadcasted_iota(jnp.int32, (STEP, n), 0)
    sub = lax.broadcasted_iota(jnp.int32, (STEP, 128), 0)
    low = steps[0] * STEP
    lanes = lax.broadcasted_iota(jnp.int32, (n - low, n), 1)
    rows_of = lax.broadcasted_iota(jnp.int32, (n - low, n), 0) + low

    def body(k, _):
        at = pl.multiple_of(k * STEP, STEP)
        rows = m_ref[pl.ds(at, STEP), :]
        block = pltpu.roll(rows, n - at, 1)[:, :STEP]
        here = (lanes8 >= at) & (lanes8 < at + STEP)
        unit = jnp.where(here, (lanes8 - at == subs8).astype(jnp.float32), rows)
        kept = apply_lower(chol_inverse_8(entries(block)), unit, sub)
        m_ref[pl.ds(at, STEP), :] = kept
        m = m_ref[low:, :]
        cleared = (lanes >= at) & (lanes < at + STEP) & (rows_of >= at + STEP)
        left = jnp.where(lanes8 >= at + STEP, kept, 0.0)
        m_ref[low:, :] = jnp.where(cleared, 0.0, m) - outer(left, kept)[low:, :]
        return 0

    lax.fori_loop(*steps, body, 0)


def square_places(n):
    return lax.broadcasted_iota(jnp.int32, (n, n), 0), lax.broadcasted_iota(jnp.int32, (n, n), 1)


def packed(m):
    h = m.shape[0] // 2
    r, c = square_places(h)
    low, high = m[:h, :h], m[h:, h:]
    diagonal = jnp.sum(jnp.where(r == c, high, 0.0), axis=0, keepdims=True)
    last = jnp.pad(diagonal, ((0, STEP - 1), (0, h)))
    return jnp.concatenate([jnp.concatenate([m[h:, :h], jnp.where(r >= c, low, high)], 1), last], 0)


def unpacked(p):
    h = p.shape[1] // 2
    r, c = square_places(h)
    corner, both, diagonal = p[:h, :h], p[:h, h:], p[h:h + 1, :h]
    flipped = both.T
    low = jnp.where(r >= c, both, flipped)
    high = jnp.where(r == c, diagonal, jnp.where(r < c, both, flipped))
    return jnp.concatenate(
        [jnp.concatenate([low, corner.T], 1), jnp.concatenate([corner, high], 1)], 0
    )


def call(kernel, shapes, *operands, flops=10**10):
    return pl.pallas_call(
        kernel,
        out_shape=[jax.ShapeDtypeStruct(s, jnp.float32) for s in shapes],
        compiler_params=pltpu.CompilerParams(vmem_limit_bytes=24 * 2**20),
        cost_estimate=pl.CostEstimate(flops=flops, bytes_accessed=2**20, transcendentals=0),
    )(*operands)


def whole_kernel(parts_ref, out_ref):
    n = out_ref.shape[0]
    r, c = square_places(n)
    total = parts_ref[0]
    for i in range(1, parts_ref.shape[0]):
        total = total + parts_ref[i]
    out_ref[...] = unpacked(total)
    for i in range(0, n // STEP, 8):
        eliminate(out_ref, n, (i, i + 8))
    out_ref[...] = jnp.where(r >= c, out_ref[...], 0.0)


def middle_kernel(steps, m_ref, out_ref):
    out_ref[...] = m_ref[...]
    eliminate(out_ref, m_ref.shape[0], steps)


def rows_kernel(shape, arrived_ref, mirrored_ref, kept_ref, rows_ref, parts_ref):
    blocks, held, tile = shape
    slab = blocks * held
    kept = kept_ref[...] > 0.0
    for c in range(arrived_ref.shape[0]):
        for m in range(blocks):
            x = arrived_ref[c, m * held:(m + 1) * held, :]
            if m == 0:
                x = jnp.where(kept, x, 0.0)
            rows_ref[pl.ds(m * tile + c * held, held), :] = x
    gram = packed(mm_tn(rows_ref[...], rows_ref[...]))
    for i in range(parts_ref.shape[0]):
        parts_ref[i, :slab, :] = mirrored_ref[...]
        parts_ref[i, slab:, :] = gram


def columns_kernel(shape, mine_ref, theirs_ref, even_ref, kept_ref, columns_ref):
    far, near, blocks, held, tile = shape
    even = even_ref[...] > 0.0
    kept = kept_ref[...] > 0.0
    for i in range(far):
        for z in range(near):
            for m in range(blocks):
                a = mine_ref[i * near + z, m * held:(m + 1) * held, :]
                b = theirs_ref[i * near + z, m * held:(m + 1) * held, :]
                pair = jnp.concatenate([jnp.where(even, a, b), jnp.where(even, b, a)], 0)
                if m == 0 and i == 0:
                    pair = jnp.where(kept, pair, 0.0)
                columns_ref[pl.ds((m * far + i) * tile + z * 2 * held, 2 * held), :] = pair


def product_kernel(held, with_edge, a_ref, columns_ref, sent_ref):
    tile = columns_ref.shape[1] // 2
    blocks = a_ref.shape[0] // tile
    slab = blocks * held
    columns = columns_ref[...]
    for m in range(blocks):
        u = mm(a_ref[m * tile:(m + 1) * tile, :], columns)
        for i in range(sent_ref.shape[0]):
            sent_ref[i, m * held:(m + 1) * held, :] = u[i * held:(i + 1) * held, :]
    for i in range(sent_ref.shape[0]):
        sent_ref[i, slab:slab + tile, :] = columns_ref[:tile, :]
        if with_edge:
            at = [m * tile + i * held for m in range(blocks)]
            edge = jnp.concatenate([a_ref[x:x + held, :tile] for x in at], 0)
            sent_ref[i, slab + tile:, :] = jnp.concatenate([edge[:slab // 2], edge[slab // 2:]], 1)


def spread(x, parts_ref):
    for i in range(parts_ref.shape[0]):
        parts_ref[i] = x


def gram_kernel(columns_ref, parts_ref):
    spread(packed(mm_tn(columns_ref[...], columns_ref[...])), parts_ref)


def inner_kernel(shape, y_ref, arrived_ref, parts_ref, *gathered_refs):
    blocks, held, tile = shape
    u_ref = gathered_refs[0]
    for k, rows_ref in enumerate(gathered_refs):
        for c in range(arrived_ref.shape[0]):
            for m in range(blocks):
                at = (k * blocks + m) * held
                rows_ref[pl.ds(m * tile + c * held, held), :] = arrived_ref[c, at:at + held, :]
    spread(packed(mm_tn(y_ref[...], u_ref[...])), parts_ref)


def reflect_kernel(first, slab, inside, arrived_ref, inverse_ref, edge_ref, sign_ref, turned_ref, top_ref, parts_ref, own_ref):
    n = inverse_ref.shape[0]
    r, c = square_places(n)
    tile = n // 2
    for i in range(2):
        top_ref[i * tile:(i + 1) * tile, :] = arrived_ref[first + i, slab:slab + tile, :]
    q1t = mm_nt(inverse_ref[...], top_ref[...])
    diagonal = jnp.sum(jnp.where(r == c, q1t, 0.0), axis=0, keepdims=True)
    sign = jnp.where(diagonal >= 0, -1.0, 1.0)
    sign_ref[...] = sign
    turned_ref[...] = jnp.where(r == c, q1t - sign, q1t)
    total = arrived_ref[0, :slab, :]
    for i in range(1, arrived_ref.shape[0]):
        total = total + arrived_ref[i, :slab, :]
    if inside:
        halves = [arrived_ref[first + i, slab + tile:slab + tile + slab // 2, :] for i in range(2)]
        edge = jnp.concatenate([jnp.concatenate([x[:, :tile], x[:, tile:]], 0) for x in halves], 1)
    else:
        edge = edge_ref[...]
        own_ref[:, n:] = edge
        for i in range(parts_ref.shape[0]):
            parts_ref[i, slab:, :] = edge
    own = mm_nt(total, inverse_ref[...]) - edge * sign
    own_ref[:, :n] = own
    for i in range(parts_ref.shape[0]):
        parts_ref[i, :slab, :] = own


def outer_first_kernel(steps, turned_ref, m_ref):
    m_ref[...] = mm_nt(turned_ref[...], turned_ref[...])
    eliminate(m_ref, m_ref.shape[0], steps)


def outer_last_kernel(steps, m_ref, turned_ref, sign_ref, tft_ref):
    n = m_ref.shape[0]
    r, c = square_places(n)
    tft_ref[...] = m_ref[...]
    eliminate(tft_ref, n, steps)
    root = jnp.where(r >= c, tft_ref[...], 0.0)
    tft_ref[...] = -mm(mm_tn(root, root), turned_ref[...]) * sign_ref[...]


def half_z_of(mine_ref, theirs_ref, tft_ref):
    return 0.5 * mm_nt(mm(tft_ref[...], unpacked(mine_ref[...] + theirs_ref[...])), tft_ref[...])


def top_z_kernel(mine_ref, theirs_ref, tft_ref, top_ref, z_ref, side_ref):
    z = half_z_of(mine_ref, theirs_ref, tft_ref)
    z_ref[...] = z
    side_ref[...] = mm_nt(z + z.T, top_ref[...])


def half_z_kernel(mine_ref, theirs_ref, tft_ref, z_ref):
    z_ref[...] = half_z_of(mine_ref, theirs_ref, tft_ref)


def swap(x, axis):
    return lax.all_to_all(x, axis, 0, 0, tiled=True)


def gathered(x, axis):
    return swap(jnp.broadcast_to(x[None], (lax.axis_size(axis), *x.shape)), axis)


def other_core(x):
    return lax.ppermute(x, CORE, [(0, 1), (1, 0)])


def in_core_order(mine, core, axis):
    theirs = other_core(mine)
    first = core == 0
    return jnp.stack([jnp.where(first, mine, theirs), jnp.where(first, theirs, mine)], axis)


def to_mirror(piece):
    rows, cols = lax.axis_size(ROW), lax.axis_size(COL)
    pairs = []
    for r in range(rows):
        for c in range(cols):
            to_row, to_col = r // cols * cols + c, r % cols
            pairs.append((r * cols + c, to_row * cols + to_col))
    return lax.ppermute(piece, ROW + COL, pairs)


def cut_rows(x, blocks, peers):
    width = x.shape[-1]
    return x.reshape(blocks, peers, -1, width).transpose(1, 0, 2, 3).reshape(peers, -1, width)


def joined_rows(slabs, blocks):
    peers, _, width = slabs.shape
    return slabs.reshape(peers, blocks, -1, width).transpose(1, 0, 2, 3).reshape(-1, width)


def mirror_rows(mine, core, blocks):
    far, near = lax.axis_size("x_lo"), lax.axis_size("z")
    width = mine.shape[-1]
    both = in_core_order(mine.reshape(far, near, blocks, -1, width), core, 2)
    return both.transpose(3, 0, 1, 2, 4, 5).reshape(-1, width)


def untile_kernel(wide, tiles_ref, a_ref):
    rows, lanes = a_ref.shape[0], tiles_ref.shape[1]
    for n in range(wide):
        a_ref[:, n * lanes:(n + 1) * lanes] = tiles_ref[pl.ds(n, rows, stride=wide), :]


def untiled(matrix_tiles):
    blocks, _, tile, wide, _, lanes = matrix_tiles.shape
    return pl.pallas_call(
        functools.partial(untile_kernel, wide),
        grid=(blocks,),
        in_specs=[pl.BlockSpec((tile * wide, lanes), lambda i: (i, 0))],
        out_specs=pl.BlockSpec((tile, wide * lanes), lambda i: (i, 0)),
        out_shape=jax.ShapeDtypeStruct((blocks * tile, wide * lanes), jnp.float32),
        compiler_params=pltpu.CompilerParams(vmem_limit_bytes=16 * 2**20),
    )(matrix_tiles.reshape(blocks * tile * wide, lanes))


def tile_kernel(wide, a_ref, tiles_ref):
    rows, lanes = a_ref.shape[0], tiles_ref.shape[1]
    for n in range(wide):
        tiles_ref[pl.ds(n, rows, stride=wide), :] = a_ref[:, n * lanes:(n + 1) * lanes]


def tiled(a, shape):
    blocks, _, tile, wide, _, lanes = shape
    return pl.pallas_call(
        functools.partial(tile_kernel, wide),
        grid=(blocks,),
        in_specs=[pl.BlockSpec((tile, wide * lanes), lambda i: (i, 0))],
        out_specs=pl.BlockSpec((tile * wide, lanes), lambda i: (i, 0)),
        out_shape=jax.ShapeDtypeStruct((blocks * tile * wide, lanes), jnp.float32),
        compiler_params=pltpu.CompilerParams(vmem_limit_bytes=16 * 2**20),
    )(a).reshape(shape)


def after(x, other):
    return lax.optimization_barrier((x, other))[0]


def on_device(matrix_tiles):
    tile_shape = matrix_tiles.shape
    blocks, tile, wide = tile_shape[0], tile_shape[2], tile_shape[3]
    band = 2 * tile
    rows, cols = lax.axis_size(ROW), lax.axis_size(COL)
    r, c, core = lax.axis_index(ROW), lax.axis_index(COL), lax.axis_index(CORE)
    a = untiled(matrix_tiles)
    slab = blocks * tile // cols
    part = band // cols
    lane = jnp.arange(band, dtype=jnp.int32)

    def places(count, peers, me):
        at = jnp.arange(count, dtype=jnp.int32)
        return (at // tile * peers + me) * tile + at % tile

    def pair(source, first):
        return jnp.concatenate([source[first], source[first + 1]], 1)

    def cleared(x, at, below):
        return jnp.where((at >= below)[:, None], x, 0.0)

    row_of, col_of = places(blocks * tile, rows, r), places(wide * tile, cols, c)

    source = swap(cut_rows(a[:, :tile], blocks, cols), COL)
    p_own, next_own = pair(source, 0), pair(source, 2)
    def flag(x):
        return jnp.broadcast_to(x.astype(jnp.float32), (1, band))

    far, near, held = lax.axis_size("x_lo"), lax.axis_size("z"), tile // cols
    packs = (cols, band // 2 + STEP, band)
    mirrored = to_mirror(p_own)
    arrived = gathered(p_own, COL)
    p_rows, sent = call(
        functools.partial(rows_kernel, (blocks, held, tile)),
        [(blocks * tile, band), (cols, slab + packs[1], band)],
        arrived, mirrored, flag(r >= band // tile), flops=10**9,
    )
    arrived = swap(sent, PAIR)
    gram = arrived[:, slab:].sum(0)
    mine = arrived[:, :slab]
    parts = jnp.stack([gram, other_core(gram)])
    (p_cols,) = call(
        functools.partial(columns_kernel, (far, near, blocks, held, tile)),
        [(wide * tile, band)], mine, other_core(mine), flag(core == 0), flag(c >= band // tile), flops=10**9,
    )
    square = (band, band)
    third = band // STEP // 3 + 1
    for panel in range(PANELS):
        below = (panel + 1) * band
        first = below // tile
        if panel:
            (parts,) = call(gram_kernel, [packs], p_cols, flops=10**9)
            late_z = after(half_z, parts)
            left = jnp.concatenate([y_rows, x_rows - mm(y_rows, late_z)], 1)
            a = a - mm_nt(left, jnp.concatenate([x_cols - mm(y_cols, late_z), y_cols], 1))
            parts = swap(parts, COL)
        (inverse,) = call(whole_kernel, [square], parts)

        rest = tile + slab // 2 if panel else tile
        (sent,) = call(
            functools.partial(product_kernel, held, panel > 0),
            [(cols, slab + rest, band)], a, p_cols, flops=10**9,
        )
        arrived = swap(sent, COL)
        arrived, inverse = after((arrived, inverse), inverse)
        sign, turned, top, u_parts, u_own = call(
            functools.partial(reflect_kernel, first, slab, panel > 0),
            [(1, band), square, square, (cols, slab if panel else 2 * slab, band), (slab, band if panel else 2 * band)],
            arrived, inverse, next_own, flops=10**9,
        )
        def signs_at(at):
            return jnp.where(at[:, None] - below == lane[None, :], sign, 0.0)

        y_rows = mm_nt(p_rows, inverse) - signs_at(row_of)
        y_cols = mm_nt(p_cols, inverse) - signs_at(col_of)
        if panel == 0:
            y_rows, turned = after((y_rows, turned), y_rows)
        mirrored = to_mirror(u_own)
        arrived = swap(u_parts, COL)
        (m1,) = call(functools.partial(outer_first_kernel, (0, third)), [square], turned)
        arrived, m1 = after((arrived, m1), m1)
        mirrored, m1 = after((mirrored, m1), arrived)
        inner, u_rows, *more = call(
            functools.partial(inner_kernel, (blocks, held, tile)),
            [packs] + [(blocks * tile, band)] * (1 if panel else 2), y_rows, arrived, flops=10**9,
        )
        if panel == 0:
            mirrored = jnp.concatenate([mirrored[:, :band], mirrored[:, band:]], 0)
        arrived = gathered(after(mirrored, m1), PAIR)
        (m2,) = call(functools.partial(middle_kernel, (third, 2 * third)), [square], m1)
        arrived, m2 = after((arrived, m2), m2)
        if panel == 0:
            inner = jnp.concatenate([inner, jnp.broadcast_to(u_rows[None, :tile], (cols, tile, band))], 1)
        inner = swap(after(inner, arrived), PAIR)
        (tft,) = call(functools.partial(outer_last_kernel, (2 * third, band // STEP)), [square], after(m2, arrived), turned, sign)
        inner = after(inner, tft)
        mine = inner[:, :packs[1]].sum(0)
        theirs = other_core(mine)
        u_cols = mirror_rows(arrived[:, :slab], core, blocks)
        late = after(tft, inner)
        x_rows, x_cols = mm_nt(u_rows, tft if panel else late), mm_nt(u_cols, late)
        if panel == 0:
            next_cols = mirror_rows(arrived[:, slab:], core, blocks)
            u_top = inner[first // 2, packs[1]:]
            u_other = other_core(u_top)
            u_top = jnp.concatenate([jnp.where(core == 0, u_top, u_other), jnp.where(core == 0, u_other, u_top)], 0)
            y_top = mm_nt(top, inverse) - jnp.where(jnp.eye(band, dtype=bool), sign, 0.0)
            tops = jnp.concatenate([mm_nt(u_top, late), y_top], 1)
            p_cols = next_cols - mm_nt(jnp.concatenate([y_cols, x_cols], 1), tops)
            p_rows = more[0] - mm_nt(jnp.concatenate([y_rows, x_rows], 1), tops)
            half_z, side = call(top_z_kernel, [square, square], mine, theirs, tft, y_top, flops=10**9)
            p_cols = cleared(p_cols + mm(y_cols, side), col_of, below + band)
            p_rows = cleared(p_rows + mm(y_rows, side), row_of, below + band)
        else:
            (half_z,) = call(half_z_kernel, [square], mine, theirs, tft, flops=10**9)
            left = jnp.concatenate([y_rows, x_rows - mm(y_rows, half_z)], 1)
            a = a - mm_nt(left, jnp.concatenate([x_cols - mm(y_cols, half_z), y_cols], 1))
    return tiled(a, tile_shape)


def solution(mesh):
    finer = Mesh(mesh.devices.reshape(2, 4, 2, 2, 4), ("x_lo", "z", "core", "x_hi", "y"))
    spec = P(None, ROW, None, None, COL, None)
    return jax.shard_map(on_device, mesh=finer, in_specs=(spec,), out_specs=spec, check_vma=False)
```

```python
import functools

import jax
import jax.numpy as jnp
from jax import lax
from jax.experimental import pallas as pl
from jax.experimental.pallas import tpu as pltpu
from jax.sharding import Mesh
from jax.sharding import PartitionSpec as P

PANELS = 2
PAIR = ("x_lo", "z")
CORE = "core"
ROW = ("x_lo", "z", "core")
COL = ("x_hi", "y")
HI = lax.Precision.HIGHEST


def mm(a, b):
    return lax.dot_general(a, b, (((1,), (0,)), ((), ())), precision=HI, preferred_element_type=jnp.float32)


def mm_nt(a, b):
    return lax.dot_general(a, b, (((1,), (1,)), ((), ())), precision=HI, preferred_element_type=jnp.float32)


def update(a, b):
    return lax.dot_general(
        a, b, (((1,), (1,)), ((), ())), precision=lax.Precision.HIGH, preferred_element_type=jnp.float32
    )


def mm_tn(a, b):
    return lax.dot_general(a, b, (((0,), (0,)), ((), ())), precision=HI, preferred_element_type=jnp.float32)


STEP = 8


def entries(block):
    columns = [jnp.broadcast_to(block[:, j:j + 1], (STEP, 128)) for j in range(STEP)]
    return [[jnp.broadcast_to(columns[j][i:i + 1, :], (STEP, 128)) if j <= i else None for j in range(STEP)] for i in range(STEP)]


def inverse_root(a):
    y = lax.rsqrt(a)
    return y * (1.5 - (0.5 * a) * (y * y))


def chol_inverse_8(a):
    a = [list(row) for row in a]
    x = [[None] * STEP for _ in range(STEP)]
    for k in range(STEP):
        x[k][k] = inverse_root(a[k][k])
        for i in range(k + 1, STEP):
            a[i][k] = a[i][k] * x[k][k]
        for j in range(k + 1, STEP):
            for i in range(j, STEP):
                a[i][j] = a[i][j] - a[i][k] * a[j][k]
    for k in range(STEP):
        for j in range(k):
            s = a[k][j] * x[j][j]
            for q in range(j + 1, k):
                s = s + a[k][q] * x[q][j]
            x[k][j] = -s * x[k][k]
    return x


def apply_lower(x, rows, sub):
    columns = []
    for j in range(STEP):
        col = x[STEP - 1][j]
        for i in range(STEP - 2, j - 1, -1):
            col = jnp.where(sub == i, x[i][j], col)
        columns.append(jnp.where(sub >= j, col, 0.0) if j else col)
    parts = []
    for c in range(0, rows.shape[1], 128):
        terms = [columns[j] * rows[j:j + 1, c:c + 128] for j in range(STEP)]
        while len(terms) > 1:
            terms = [terms[i] + terms[i + 1] for i in range(0, len(terms), 2)]
        parts.append(terms[0])
    return jnp.concatenate(parts, 1)


def three(x):
    hi = x.astype(jnp.bfloat16).astype(jnp.float32)
    rest = x - hi
    mid = rest.astype(jnp.bfloat16).astype(jnp.float32)
    return hi, mid, rest - mid


def outer(left, right):
    a, b, c = three(left)
    d, e, f = three(right)
    lefts = jnp.concatenate([a, a, b, a, c, b], 0).astype(jnp.bfloat16)
    rights = jnp.concatenate([d, e, d, f, d, e], 0).astype(jnp.bfloat16)
    return lax.dot_general(lefts, rights, (((0,), (0,)), ((), ())), preferred_element_type=jnp.float32)


def eliminate(m_ref, n, steps):
    lanes8 = lax.broadcasted_iota(jnp.int32, (STEP, n), 1)
    subs8 = lax.broadcasted_iota(jnp.int32, (STEP, n), 0)
    sub = lax.broadcasted_iota(jnp.int32, (STEP, 128), 0)
    low = steps[0] * STEP
    lanes = lax.broadcasted_iota(jnp.int32, (n - low, n), 1)
    rows_of = lax.broadcasted_iota(jnp.int32, (n - low, n), 0) + low

    def body(k, _):
        at = pl.multiple_of(k * STEP, STEP)
        rows = m_ref[pl.ds(at, STEP), :]
        block = pltpu.roll(rows, n - at, 1)[:, :STEP]
        here = (lanes8 >= at) & (lanes8 < at + STEP)
        unit = jnp.where(here, (lanes8 - at == subs8).astype(jnp.float32), rows)
        kept = apply_lower(chol_inverse_8(entries(block)), unit, sub)
        m_ref[pl.ds(at, STEP), :] = kept
        m = m_ref[low:, :]
        cleared = (lanes >= at) & (lanes < at + STEP) & (rows_of >= at + STEP)
        left = jnp.where(lanes8 >= at + STEP, kept, 0.0)
        m_ref[low:, :] = jnp.where(cleared, 0.0, m) - outer(left, kept)[low:, :]
        return 0

    lax.fori_loop(*steps, body, 0)


def square_places(n):
    return lax.broadcasted_iota(jnp.int32, (n, n), 0), lax.broadcasted_iota(jnp.int32, (n, n), 1)


def packed(m):
    h = m.shape[0] // 2
    r, c = square_places(h)
    low, high = m[:h, :h], m[h:, h:]
    diagonal = jnp.sum(jnp.where(r == c, high, 0.0), axis=0, keepdims=True)
    last = jnp.pad(diagonal, ((0, STEP - 1), (0, h)))
    return jnp.concatenate([jnp.concatenate([m[h:, :h], jnp.where(r >= c, low, high)], 1), last], 0)


def unpacked(p):
    h = p.shape[1] // 2
    r, c = square_places(h)
    corner, both, diagonal = p[:h, :h], p[:h, h:], p[h:h + 1, :h]
    flipped = both.T
    low = jnp.where(r >= c, both, flipped)
    high = jnp.where(r == c, diagonal, jnp.where(r < c, both, flipped))
    return jnp.concatenate(
        [jnp.concatenate([low, corner.T], 1), jnp.concatenate([corner, high], 1)], 0
    )


def call(kernel, shapes, *operands, flops=10**10):
    return pl.pallas_call(
        kernel,
        out_shape=[jax.ShapeDtypeStruct(s, jnp.float32) for s in shapes],
        compiler_params=pltpu.CompilerParams(vmem_limit_bytes=24 * 2**20),
        cost_estimate=pl.CostEstimate(flops=flops, bytes_accessed=2**20, transcendentals=0),
    )(*operands)


def whole_kernel(parts_ref, out_ref):
    n = out_ref.shape[0]
    r, c = square_places(n)
    total = parts_ref[0]
    for i in range(1, parts_ref.shape[0]):
        total = total + parts_ref[i]
    out_ref[...] = unpacked(total)
    for i in range(0, n // STEP, 8):
        eliminate(out_ref, n, (i, i + 8))
    out_ref[...] = jnp.where(r >= c, out_ref[...], 0.0)


def middle_kernel(steps, m_ref, out_ref):
    out_ref[...] = m_ref[...]
    eliminate(out_ref, m_ref.shape[0], steps)


def rows_kernel(shape, arrived_ref, mirrored_ref, kept_ref, rows_ref, parts_ref):
    blocks, held, tile = shape
    slab = blocks * held
    kept = kept_ref[...] > 0.0
    for c in range(arrived_ref.shape[0]):
        for m in range(blocks):
            x = arrived_ref[c, m * held:(m + 1) * held, :]
            if m == 0:
                x = jnp.where(kept, x, 0.0)
            rows_ref[pl.ds(m * tile + c * held, held), :] = x
    gram = packed(mm_tn(rows_ref[...], rows_ref[...]))
    for i in range(parts_ref.shape[0]):
        parts_ref[i, :slab, :] = mirrored_ref[...]
        parts_ref[i, slab:, :] = gram


def columns_kernel(shape, mine_ref, theirs_ref, even_ref, kept_ref, columns_ref):
    far, near, blocks, held, tile = shape
    even = even_ref[...] > 0.0
    kept = kept_ref[...] > 0.0
    for i in range(far):
        for z in range(near):
            for m in range(blocks):
                a = mine_ref[i * near + z, m * held:(m + 1) * held, :]
                b = theirs_ref[i * near + z, m * held:(m + 1) * held, :]
                pair = jnp.concatenate([jnp.where(even, a, b), jnp.where(even, b, a)], 0)
                if m == 0 and i == 0:
                    pair = jnp.where(kept, pair, 0.0)
                columns_ref[pl.ds((m * far + i) * tile + z * 2 * held, 2 * held), :] = pair


def product_kernel(held, a_ref, columns_ref, sent_ref):
    tile = columns_ref.shape[1] // 2
    blocks = a_ref.shape[0] // tile
    slab = blocks * held
    columns = columns_ref[...]
    for m in range(blocks):
        u = mm(a_ref[m * tile:(m + 1) * tile, :], columns)
        for i in range(sent_ref.shape[0]):
            sent_ref[i, m * held:(m + 1) * held, :] = u[i * held:(i + 1) * held, :]
    for i in range(sent_ref.shape[0]):
        sent_ref[i, slab:, :] = columns_ref[:tile, :]


def spread(x, parts_ref):
    for i in range(parts_ref.shape[0]):
        parts_ref[i] = x


def gram_kernel(columns_ref, parts_ref):
    spread(packed(mm_tn(columns_ref[...], columns_ref[...])), parts_ref)


def inner_kernel(shape, y_ref, arrived_ref, parts_ref, *gathered_refs):
    blocks, held, tile = shape
    u_ref = gathered_refs[0]
    for k, rows_ref in enumerate(gathered_refs):
        for c in range(arrived_ref.shape[0]):
            for m in range(blocks):
                at = (k * blocks + m) * held
                rows_ref[pl.ds(m * tile + c * held, held), :] = arrived_ref[c, at:at + held, :]
    spread(packed(mm_tn(y_ref[...], u_ref[...])), parts_ref)


def reflect_kernel(first, slab, inside, arrived_ref, inverse_ref, edge_ref, sign_ref, turned_ref, top_ref, parts_ref, own_ref):
    n = inverse_ref.shape[0]
    r, c = square_places(n)
    tile = n // 2
    for i in range(2):
        top_ref[i * tile:(i + 1) * tile, :] = arrived_ref[first + i, slab:slab + tile, :]
    q1t = mm_nt(inverse_ref[...], top_ref[...])
    diagonal = jnp.sum(jnp.where(r == c, q1t, 0.0), axis=0, keepdims=True)
    sign = jnp.where(diagonal >= 0, -1.0, 1.0)
    sign_ref[...] = sign
    turned_ref[...] = jnp.where(r == c, q1t - sign, q1t)
    total = arrived_ref[0, :slab, :]
    for i in range(1, arrived_ref.shape[0]):
        total = total + arrived_ref[i, :slab, :]
    if inside:
        halves = [arrived_ref[first + i, slab + tile:slab + tile + slab // 2, :] for i in range(2)]
        edge = jnp.concatenate([jnp.concatenate([x[:, :tile], x[:, tile:]], 0) for x in halves], 1)
    else:
        edge = edge_ref[...]
        own_ref[:, n:] = edge
        for i in range(parts_ref.shape[0]):
            parts_ref[i, slab:, :] = edge
    own = mm_nt(total, inverse_ref[...]) - edge * sign
    own_ref[:, :n] = own
    for i in range(parts_ref.shape[0]):
        parts_ref[i, :slab, :] = own


def outer_first_kernel(steps, turned_ref, m_ref):
    m_ref[...] = mm_nt(turned_ref[...], turned_ref[...])
    eliminate(m_ref, m_ref.shape[0], steps)


def outer_last_kernel(steps, m_ref, turned_ref, sign_ref, tft_ref):
    n = m_ref.shape[0]
    r, c = square_places(n)
    tft_ref[...] = m_ref[...]
    eliminate(tft_ref, n, steps)
    root = jnp.where(r >= c, tft_ref[...], 0.0)
    tft_ref[...] = -mm(mm_tn(root, root), turned_ref[...]) * sign_ref[...]


def half_z_of(mine_ref, theirs_ref, tft_ref):
    return 0.5 * mm_nt(mm(tft_ref[...], unpacked(mine_ref[...] + theirs_ref[...])), tft_ref[...])


def top_z_kernel(mine_ref, theirs_ref, tft_ref, top_ref, z_ref, side_ref):
    z = half_z_of(mine_ref, theirs_ref, tft_ref)
    z_ref[...] = z
    side_ref[...] = mm_nt(z + z.T, top_ref[...])


def whole_z_kernel(mine_ref, theirs_ref, tft_ref, z_ref):
    z = half_z_of(mine_ref, theirs_ref, tft_ref)
    z_ref[...] = z + z.T


def swap(x, axis):
    return lax.all_to_all(x, axis, 0, 0, tiled=True)


def gathered(x, axis):
    return swap(jnp.broadcast_to(x[None], (lax.axis_size(axis), *x.shape)), axis)


def other_core(x):
    return lax.ppermute(x, CORE, [(0, 1), (1, 0)])


def in_core_order(mine, core, axis):
    theirs = other_core(mine)
    first = core == 0
    return jnp.stack([jnp.where(first, mine, theirs), jnp.where(first, theirs, mine)], axis)


def to_mirror(piece):
    rows, cols = lax.axis_size(ROW), lax.axis_size(COL)
    pairs = []
    for r in range(rows):
        for c in range(cols):
            to_row, to_col = r // cols * cols + c, r % cols
            pairs.append((r * cols + c, to_row * cols + to_col))
    return lax.ppermute(piece, ROW + COL, pairs)


def cut_rows(x, blocks, peers):
    width = x.shape[-1]
    return x.reshape(blocks, peers, -1, width).transpose(1, 0, 2, 3).reshape(peers, -1, width)


def joined_rows(slabs, blocks):
    peers, _, width = slabs.shape
    return slabs.reshape(peers, blocks, -1, width).transpose(1, 0, 2, 3).reshape(-1, width)


def mirror_rows(mine, core, blocks):
    far, near = lax.axis_size("x_lo"), lax.axis_size("z")
    width = mine.shape[-1]
    both = in_core_order(mine.reshape(far, near, blocks, -1, width), core, 2)
    return both.transpose(3, 0, 1, 2, 4, 5).reshape(-1, width)


def untile_kernel(wide, tiles_ref, a_ref):
    rows, lanes = a_ref.shape[0], tiles_ref.shape[1]
    for n in range(wide):
        a_ref[:, n * lanes:(n + 1) * lanes] = tiles_ref[pl.ds(n, rows, stride=wide), :]


def untiled(matrix_tiles):
    blocks, _, tile, wide, _, lanes = matrix_tiles.shape
    return pl.pallas_call(
        functools.partial(untile_kernel, wide),
        grid=(blocks,),
        in_specs=[pl.BlockSpec((tile * wide, lanes), lambda i: (i, 0))],
        out_specs=pl.BlockSpec((tile, wide * lanes), lambda i: (i, 0)),
        out_shape=jax.ShapeDtypeStruct((blocks * tile, wide * lanes), jnp.float32),
        compiler_params=pltpu.CompilerParams(vmem_limit_bytes=16 * 2**20),
    )(matrix_tiles.reshape(blocks * tile * wide, lanes))


def tile_kernel(wide, a_ref, tiles_ref):
    rows, lanes = a_ref.shape[0], tiles_ref.shape[1]
    for n in range(wide):
        tiles_ref[pl.ds(n, rows, stride=wide), :] = a_ref[:, n * lanes:(n + 1) * lanes]


def tiled(a, shape):
    blocks, _, tile, wide, _, lanes = shape
    return pl.pallas_call(
        functools.partial(tile_kernel, wide),
        grid=(blocks,),
        in_specs=[pl.BlockSpec((tile, wide * lanes), lambda i: (i, 0))],
        out_specs=pl.BlockSpec((tile * wide, lanes), lambda i: (i, 0)),
        out_shape=jax.ShapeDtypeStruct((blocks * tile * wide, lanes), jnp.float32),
        compiler_params=pltpu.CompilerParams(vmem_limit_bytes=16 * 2**20),
    )(a).reshape(shape)


def after(x, other):
    return lax.optimization_barrier((x, other))[0]


def on_device(matrix_tiles):
    tile_shape = matrix_tiles.shape
    blocks, tile, wide = tile_shape[0], tile_shape[2], tile_shape[3]
    band = 2 * tile
    rows, cols = lax.axis_size(ROW), lax.axis_size(COL)
    r, c, core = lax.axis_index(ROW), lax.axis_index(COL), lax.axis_index(CORE)
    a = untiled(matrix_tiles)
    slab = blocks * tile // cols
    part = band // cols
    lane = jnp.arange(band, dtype=jnp.int32)

    def places(count, peers, me):
        at = jnp.arange(count, dtype=jnp.int32)
        return (at // tile * peers + me) * tile + at % tile

    def pair(source, first):
        return jnp.concatenate([source[first], source[first + 1]], 1)

    def cleared(x, at, below):
        return jnp.where((at >= below)[:, None], x, 0.0)

    row_of, col_of = places(blocks * tile, rows, r), places(wide * tile, cols, c)

    source = swap(cut_rows(a[:, :tile], blocks, cols), COL)
    p_own, next_own = pair(source, 0), pair(source, 2)
    def flag(x):
        return jnp.broadcast_to(x.astype(jnp.float32), (1, band))

    far, near, held = lax.axis_size("x_lo"), lax.axis_size("z"), tile // cols
    packs = (cols, band // 2 + STEP, band)
    mirrored = to_mirror(p_own)
    arrived = gathered(p_own, COL)
    p_rows, sent = call(
        functools.partial(rows_kernel, (blocks, held, tile)),
        [(blocks * tile, band), (cols, slab + packs[1], band)],
        arrived, mirrored, flag(r >= band // tile), flops=10**9,
    )
    arrived = swap(sent, PAIR)
    gram = arrived[:, slab:].sum(0)
    mine = arrived[:, :slab]
    parts = jnp.stack([gram, other_core(gram)])
    (p_cols,) = call(
        functools.partial(columns_kernel, (far, near, blocks, held, tile)),
        [(wide * tile, band)], mine, other_core(mine), flag(core == 0), flag(c >= band // tile), flops=10**9,
    )
    square = (band, band)
    third = band // STEP // 3 + 1
    for panel in range(PANELS):
        below = (panel + 1) * band
        first = below // tile
        if panel:
            (parts,) = call(gram_kernel, [packs], p_cols, flops=10**9)
            late_z = after(half_z, parts)
            left = jnp.concatenate([y_rows, x_rows - mm(y_rows, late_z)], 1)
            a = a - update(left, jnp.concatenate([x_cols - mm(y_cols, late_z), y_cols], 1))
            parts = swap(parts, COL)
        (inverse,) = call(whole_kernel, [square], parts)

        if panel:
            edge = cut_rows(a[:, :tile], blocks, cols)
            sent = jnp.concatenate([
                cut_rows(mm(a, p_cols), blocks, cols),
                jnp.broadcast_to(p_cols[None, :tile], (cols, tile, band)),
                jnp.concatenate([edge[:, :slab // 2], edge[:, slab // 2:]], 2),
            ], 1)
        else:
            (sent,) = call(
                functools.partial(product_kernel, held), [(cols, slab + tile, band)], a, p_cols, flops=10**9,
            )
        arrived = swap(sent, COL)
        arrived, inverse = after((arrived, inverse), inverse)
        sign, turned, top, u_parts, u_own = call(
            functools.partial(reflect_kernel, first, slab, panel > 0),
            [(1, band), square, square, (cols, slab if panel else 2 * slab, band), (slab, band if panel else 2 * band)],
            arrived, inverse, next_own, flops=10**9,
        )
        def signs_at(at):
            return jnp.where(at[:, None] - below == lane[None, :], sign, 0.0)

        y_rows = mm_nt(p_rows, inverse) - signs_at(row_of)
        y_cols = mm_nt(p_cols, inverse) - signs_at(col_of)
        if panel == 0:
            y_rows, turned = after((y_rows, turned), y_rows)
        mirrored = to_mirror(u_own)
        arrived = swap(u_parts, COL)
        (m1,) = call(functools.partial(outer_first_kernel, (0, third)), [square], turned)
        arrived, m1 = after((arrived, m1), m1)
        mirrored, m1 = after((mirrored, m1), arrived)
        inner, u_rows, *more = call(
            functools.partial(inner_kernel, (blocks, held, tile)),
            [packs] + [(blocks * tile, band)] * (1 if panel else 2), y_rows, arrived, flops=10**9,
        )
        if panel == 0:
            mirrored = jnp.concatenate([mirrored[:, :band], mirrored[:, band:]], 0)
        arrived = gathered(after(mirrored, m1), PAIR)
        if panel:
            m1 = after(m1, (inner, y_cols))
        (m2,) = call(functools.partial(middle_kernel, (third, 2 * third)), [square], m1)
        arrived, m2 = after((arrived, m2), m2)
        if panel == 0:
            inner = jnp.concatenate([inner, jnp.broadcast_to(u_rows[None, :tile], (cols, tile, band))], 1)
        inner = swap(after(inner, arrived), PAIR)
        (tft,) = call(functools.partial(outer_last_kernel, (2 * third, band // STEP)), [square], after(m2, arrived), turned, sign, flops=10**6)
        inner = after(inner, tft)
        mine = inner[:, :packs[1]].sum(0)
        theirs = other_core(mine)
        u_cols = mirror_rows(arrived[:, :slab], core, blocks)
        late = tft if panel else after(tft, inner)
        x_rows, x_cols = mm_nt(u_rows, late), mm_nt(u_cols, late)
        if panel == 0:
            next_cols = mirror_rows(arrived[:, slab:], core, blocks)
            u_top = inner[first // 2, packs[1]:]
            u_other = other_core(u_top)
            u_top = jnp.concatenate([jnp.where(core == 0, u_top, u_other), jnp.where(core == 0, u_other, u_top)], 0)
            y_top = mm_nt(top, inverse) - jnp.where(jnp.eye(band, dtype=bool), sign, 0.0)
            tops = jnp.concatenate([mm_nt(u_top, late), y_top], 1)
            p_cols = next_cols - mm_nt(jnp.concatenate([y_cols, x_cols], 1), tops)
            p_rows = more[0] - mm_nt(jnp.concatenate([y_rows, x_rows], 1), tops)
            half_z, side = call(top_z_kernel, [square, square], mine, theirs, tft, y_top, flops=10**9)
            p_cols = cleared(p_cols + mm(y_cols, side), col_of, below + band)
            p_rows = cleared(p_rows + mm(y_rows, side), row_of, below + band)
        else:
            a = a - update(jnp.concatenate([y_rows, x_rows], 1), jnp.concatenate([x_cols, y_cols], 1))
            (z,) = call(whole_z_kernel, [square], mine, theirs, tft, flops=10**9)
            a = a + update(mm(y_rows, z), y_cols)
    return tiled(a, tile_shape)


def solution(mesh):
    finer = Mesh(mesh.devices.reshape(2, 4, 2, 2, 4), ("x_lo", "z", "core", "x_hi", "y"))
    spec = P(None, ROW, None, None, COL, None)
    return jax.shard_map(on_device, mesh=finer, in_specs=(spec,), out_specs=spec, check_vma=False)
```

```python
import functools

import jax
import jax.numpy as jnp
from jax import lax
from jax.experimental import pallas as pl
from jax.experimental.pallas import tpu as pltpu
from jax.sharding import Mesh
from jax.sharding import PartitionSpec as P

PANELS = 2
PAIR = ("x_lo", "z")
CORE = "core"
ROW = ("x_lo", "z", "core")
COL = ("x_hi", "y")
HI = lax.Precision.HIGHEST


def mm(a, b):
    return lax.dot_general(a, b, (((1,), (0,)), ((), ())), precision=HI, preferred_element_type=jnp.float32)


def mm_nt(a, b):
    return lax.dot_general(a, b, (((1,), (1,)), ((), ())), precision=HI, preferred_element_type=jnp.float32)


def update(a, b):
    return lax.dot_general(
        a, b, (((1,), (1,)), ((), ())), precision=lax.Precision.HIGH, preferred_element_type=jnp.float32
    )


def mm_tn(a, b):
    return lax.dot_general(a, b, (((0,), (0,)), ((), ())), precision=HI, preferred_element_type=jnp.float32)


STEP = 8


def entries(block):
    columns = [jnp.broadcast_to(block[:, j:j + 1], (STEP, 128)) for j in range(STEP)]
    return [[jnp.broadcast_to(columns[j][i:i + 1, :], (STEP, 128)) if j <= i else None for j in range(STEP)] for i in range(STEP)]


def inverse_root(a):
    y = lax.rsqrt(a)
    return y * (1.5 - (0.5 * a) * (y * y))


def chol_inverse_8(a):
    a = [list(row) for row in a]
    x = [[None] * STEP for _ in range(STEP)]
    for k in range(STEP):
        x[k][k] = inverse_root(a[k][k])
        for i in range(k + 1, STEP):
            a[i][k] = a[i][k] * x[k][k]
        for j in range(k + 1, STEP):
            for i in range(j, STEP):
                a[i][j] = a[i][j] - a[i][k] * a[j][k]
    for k in range(STEP):
        for j in range(k):
            s = a[k][j] * x[j][j]
            for q in range(j + 1, k):
                s = s + a[k][q] * x[q][j]
            x[k][j] = -s * x[k][k]
    return x


def apply_lower(x, rows, sub):
    columns = []
    for j in range(STEP):
        col = x[STEP - 1][j]
        for i in range(STEP - 2, j - 1, -1):
            col = jnp.where(sub == i, x[i][j], col)
        columns.append(jnp.where(sub >= j, col, 0.0) if j else col)
    parts = []
    for c in range(0, rows.shape[1], 128):
        terms = [columns[j] * rows[j:j + 1, c:c + 128] for j in range(STEP)]
        while len(terms) > 1:
            terms = [terms[i] + terms[i + 1] for i in range(0, len(terms), 2)]
        parts.append(terms[0])
    return jnp.concatenate(parts, 1)


def three(x):
    hi = x.astype(jnp.bfloat16).astype(jnp.float32)
    rest = x - hi
    mid = rest.astype(jnp.bfloat16).astype(jnp.float32)
    return hi, mid, rest - mid


def outer(left, right):
    a, b, c = three(left)
    d, e, f = three(right)
    lefts = jnp.concatenate([a, a, b, a, c, b], 0).astype(jnp.bfloat16)
    rights = jnp.concatenate([d, e, d, f, d, e], 0).astype(jnp.bfloat16)
    return lax.dot_general(lefts, rights, (((0,), (0,)), ((), ())), preferred_element_type=jnp.float32)


def eliminate(m_ref, n, steps):
    lanes8 = lax.broadcasted_iota(jnp.int32, (STEP, n), 1)
    subs8 = lax.broadcasted_iota(jnp.int32, (STEP, n), 0)
    sub = lax.broadcasted_iota(jnp.int32, (STEP, 128), 0)
    low = steps[0] * STEP
    lanes = lax.broadcasted_iota(jnp.int32, (n - low, n), 1)
    rows_of = lax.broadcasted_iota(jnp.int32, (n - low, n), 0) + low

    def body(k, _):
        at = pl.multiple_of(k * STEP, STEP)
        rows = m_ref[pl.ds(at, STEP), :]
        block = pltpu.roll(rows, n - at, 1)[:, :STEP]
        here = (lanes8 >= at) & (lanes8 < at + STEP)
        unit = jnp.where(here, (lanes8 - at == subs8).astype(jnp.float32), rows)
        kept = apply_lower(chol_inverse_8(entries(block)), unit, sub)
        m_ref[pl.ds(at, STEP), :] = kept
        m = m_ref[low:, :]
        cleared = (lanes >= at) & (lanes < at + STEP) & (rows_of >= at + STEP)
        left = jnp.where(lanes8 >= at + STEP, kept, 0.0)
        m_ref[low:, :] = jnp.where(cleared, 0.0, m) - outer(left, kept)[low:, :]
        return 0

    lax.fori_loop(*steps, body, 0)


def square_places(n):
    return lax.broadcasted_iota(jnp.int32, (n, n), 0), lax.broadcasted_iota(jnp.int32, (n, n), 1)


def packed(m):
    h = m.shape[0] // 2
    r, c = square_places(h)
    low, high = m[:h, :h], m[h:, h:]
    diagonal = jnp.sum(jnp.where(r == c, high, 0.0), axis=0, keepdims=True)
    last = jnp.pad(diagonal, ((0, STEP - 1), (0, h)))
    return jnp.concatenate([jnp.concatenate([m[h:, :h], jnp.where(r >= c, low, high)], 1), last], 0)


def unpacked(p):
    h = p.shape[1] // 2
    r, c = square_places(h)
    corner, both, diagonal = p[:h, :h], p[:h, h:], p[h:h + 1, :h]
    flipped = both.T
    low = jnp.where(r >= c, both, flipped)
    high = jnp.where(r == c, diagonal, jnp.where(r < c, both, flipped))
    return jnp.concatenate(
        [jnp.concatenate([low, corner.T], 1), jnp.concatenate([corner, high], 1)], 0
    )


def call(kernel, shapes, *operands, flops=10**10):
    return pl.pallas_call(
        kernel,
        out_shape=[jax.ShapeDtypeStruct(s, jnp.float32) for s in shapes],
        compiler_params=pltpu.CompilerParams(vmem_limit_bytes=24 * 2**20),
        cost_estimate=pl.CostEstimate(flops=flops, bytes_accessed=2**20, transcendentals=0),
    )(*operands)


def whole_kernel(parts_ref, out_ref):
    n = out_ref.shape[0]
    r, c = square_places(n)
    total = parts_ref[0]
    for i in range(1, parts_ref.shape[0]):
        total = total + parts_ref[i]
    out_ref[...] = unpacked(total)
    for i in range(0, n // STEP, 8):
        eliminate(out_ref, n, (i, i + 8))
    out_ref[...] = jnp.where(r >= c, out_ref[...], 0.0)


def middle_kernel(steps, m_ref, out_ref):
    out_ref[...] = m_ref[...]
    eliminate(out_ref, m_ref.shape[0], steps)


def rows_kernel(shape, arrived_ref, mirrored_ref, kept_ref, rows_ref, parts_ref):
    blocks, held, tile = shape
    slab = blocks * held
    kept = kept_ref[...] > 0.0
    for c in range(arrived_ref.shape[0]):
        for m in range(blocks):
            x = arrived_ref[c, m * held:(m + 1) * held, :]
            if m == 0:
                x = jnp.where(kept, x, 0.0)
            rows_ref[pl.ds(m * tile + c * held, held), :] = x
    gram = packed(mm_tn(rows_ref[...], rows_ref[...]))
    for i in range(parts_ref.shape[0]):
        parts_ref[i, :slab, :] = mirrored_ref[...]
        parts_ref[i, slab:, :] = gram


def columns_kernel(shape, mine_ref, theirs_ref, even_ref, kept_ref, columns_ref):
    far, near, blocks, held, tile = shape
    even = even_ref[...] > 0.0
    kept = kept_ref[...] > 0.0
    for i in range(far):
        for z in range(near):
            for m in range(blocks):
                a = mine_ref[i * near + z, m * held:(m + 1) * held, :]
                b = theirs_ref[i * near + z, m * held:(m + 1) * held, :]
                pair = jnp.concatenate([jnp.where(even, a, b), jnp.where(even, b, a)], 0)
                if m == 0 and i == 0:
                    pair = jnp.where(kept, pair, 0.0)
                columns_ref[pl.ds((m * far + i) * tile + z * 2 * held, 2 * held), :] = pair


def product_kernel(held, a_ref, columns_ref, sent_ref):
    tile = columns_ref.shape[1] // 2
    blocks = a_ref.shape[0] // tile
    slab = blocks * held
    columns = columns_ref[...]
    for m in range(blocks):
        u = mm(a_ref[m * tile:(m + 1) * tile, :], columns)
        for i in range(sent_ref.shape[0]):
            sent_ref[i, m * held:(m + 1) * held, :] = u[i * held:(i + 1) * held, :]
    for i in range(sent_ref.shape[0]):
        sent_ref[i, slab:, :] = columns_ref[:tile, :]


def spread(x, parts_ref):
    for i in range(parts_ref.shape[0]):
        parts_ref[i] = x


def gram_kernel(columns_ref, parts_ref):
    spread(packed(mm_tn(columns_ref[...], columns_ref[...])), parts_ref)


def inner_kernel(shape, y_ref, arrived_ref, parts_ref, *gathered_refs):
    blocks, held, tile = shape
    u_ref = gathered_refs[0]
    for k, rows_ref in enumerate(gathered_refs):
        for c in range(arrived_ref.shape[0]):
            for m in range(blocks):
                at = (k * blocks + m) * held
                rows_ref[pl.ds(m * tile + c * held, held), :] = arrived_ref[c, at:at + held, :]
    spread(packed(mm_tn(y_ref[...], u_ref[...])), parts_ref)


def reflect_kernel(first, slab, inside, arrived_ref, inverse_ref, edge_ref, sign_ref, turned_ref, top_ref, parts_ref, own_ref):
    n = inverse_ref.shape[0]
    r, c = square_places(n)
    tile = n // 2
    for i in range(2):
        top_ref[i * tile:(i + 1) * tile, :] = arrived_ref[first + i, slab:slab + tile, :]
    q1t = mm_nt(inverse_ref[...], top_ref[...])
    diagonal = jnp.sum(jnp.where(r == c, q1t, 0.0), axis=0, keepdims=True)
    sign = jnp.where(diagonal >= 0, -1.0, 1.0)
    sign_ref[...] = sign
    turned_ref[...] = jnp.where(r == c, q1t - sign, q1t)
    total = arrived_ref[0, :slab, :]
    for i in range(1, arrived_ref.shape[0]):
        total = total + arrived_ref[i, :slab, :]
    if inside:
        halves = [arrived_ref[first + i, slab + tile:slab + tile + slab // 2, :] for i in range(2)]
        edge = jnp.concatenate([jnp.concatenate([x[:, :tile], x[:, tile:]], 0) for x in halves], 1)
    else:
        edge = edge_ref[...]
        own_ref[:, n:] = edge
        for i in range(parts_ref.shape[0]):
            parts_ref[i, slab:, :] = edge
    own = mm_nt(total, inverse_ref[...]) - edge * sign
    own_ref[:, :n] = own
    for i in range(parts_ref.shape[0]):
        parts_ref[i, :slab, :] = own


def outer_first_kernel(steps, turned_ref, m_ref):
    m_ref[...] = mm_nt(turned_ref[...], turned_ref[...])
    eliminate(m_ref, m_ref.shape[0], steps)


def outer_last_kernel(steps, m_ref, turned_ref, sign_ref, tft_ref):
    n = m_ref.shape[0]
    r, c = square_places(n)
    tft_ref[...] = m_ref[...]
    eliminate(tft_ref, n, steps)
    root = jnp.where(r >= c, tft_ref[...], 0.0)
    tft_ref[...] = -mm(mm_tn(root, root), turned_ref[...]) * sign_ref[...]


def half_z_of(mine_ref, theirs_ref, tft_ref):
    return 0.5 * mm_nt(mm(tft_ref[...], unpacked(mine_ref[...] + theirs_ref[...])), tft_ref[...])


def top_z_kernel(mine_ref, theirs_ref, tft_ref, y_top_ref, a_ref, b_ref, even_ref, z_ref, side_ref):
    even = even_ref[...] > 0.0
    a, b = a_ref[...], b_ref[...]
    u_top = jnp.concatenate([jnp.where(even, a, b), jnp.where(even, b, a)], 0)
    z = half_z_of(mine_ref, theirs_ref, tft_ref)
    z_ref[...] = z
    side_ref[...] = mm_nt(z + z.T, y_top_ref[...]) - mm_nt(tft_ref[...], u_top)


def whole_z_kernel(mine_ref, theirs_ref, tft_ref, z_ref):
    z = half_z_of(mine_ref, theirs_ref, tft_ref)
    z_ref[...] = z + z.T


def swap(x, axis):
    return lax.all_to_all(x, axis, 0, 0, tiled=True)


def gathered(x, axis):
    return swap(jnp.broadcast_to(x[None], (lax.axis_size(axis), *x.shape)), axis)


def other_core(x):
    return lax.ppermute(x, CORE, [(0, 1), (1, 0)])


def in_core_order(mine, core, axis):
    theirs = other_core(mine)
    first = core == 0
    return jnp.stack([jnp.where(first, mine, theirs), jnp.where(first, theirs, mine)], axis)


def to_mirror(piece):
    rows, cols = lax.axis_size(ROW), lax.axis_size(COL)
    pairs = []
    for r in range(rows):
        for c in range(cols):
            to_row, to_col = r // cols * cols + c, r % cols
            pairs.append((r * cols + c, to_row * cols + to_col))
    return lax.ppermute(piece, ROW + COL, pairs)


def cut_rows(x, blocks, peers):
    width = x.shape[-1]
    return x.reshape(blocks, peers, -1, width).transpose(1, 0, 2, 3).reshape(peers, -1, width)


def joined_rows(slabs, blocks):
    peers, _, width = slabs.shape
    return slabs.reshape(peers, blocks, -1, width).transpose(1, 0, 2, 3).reshape(-1, width)


def mirror_rows(mine, core, blocks):
    far, near = lax.axis_size("x_lo"), lax.axis_size("z")
    width = mine.shape[-1]
    both = in_core_order(mine.reshape(far, near, blocks, -1, width), core, 2)
    return both.transpose(3, 0, 1, 2, 4, 5).reshape(-1, width)


def untile_kernel(wide, tiles_ref, a_ref):
    rows, lanes = a_ref.shape[0], tiles_ref.shape[1]
    for n in range(wide):
        a_ref[:, n * lanes:(n + 1) * lanes] = tiles_ref[pl.ds(n, rows, stride=wide), :]


def untiled(matrix_tiles):
    blocks, _, tile, wide, _, lanes = matrix_tiles.shape
    return pl.pallas_call(
        functools.partial(untile_kernel, wide),
        grid=(blocks,),
        in_specs=[pl.BlockSpec((tile * wide, lanes), lambda i: (i, 0))],
        out_specs=pl.BlockSpec((tile, wide * lanes), lambda i: (i, 0)),
        out_shape=jax.ShapeDtypeStruct((blocks * tile, wide * lanes), jnp.float32),
        compiler_params=pltpu.CompilerParams(vmem_limit_bytes=16 * 2**20),
    )(matrix_tiles.reshape(blocks * tile * wide, lanes))


def tile_kernel(wide, a_ref, tiles_ref):
    rows, lanes = a_ref.shape[0], tiles_ref.shape[1]
    for n in range(wide):
        tiles_ref[pl.ds(n, rows, stride=wide), :] = a_ref[:, n * lanes:(n + 1) * lanes]


def tiled(a, shape):
    blocks, _, tile, wide, _, lanes = shape
    return pl.pallas_call(
        functools.partial(tile_kernel, wide),
        grid=(blocks,),
        in_specs=[pl.BlockSpec((tile, wide * lanes), lambda i: (i, 0))],
        out_specs=pl.BlockSpec((tile * wide, lanes), lambda i: (i, 0)),
        out_shape=jax.ShapeDtypeStruct((blocks * tile * wide, lanes), jnp.float32),
        compiler_params=pltpu.CompilerParams(vmem_limit_bytes=16 * 2**20),
    )(a).reshape(shape)


def after(x, other):
    return lax.optimization_barrier((x, other))[0]


def on_device(matrix_tiles):
    tile_shape = matrix_tiles.shape
    blocks, tile, wide = tile_shape[0], tile_shape[2], tile_shape[3]
    band = 2 * tile
    rows, cols = lax.axis_size(ROW), lax.axis_size(COL)
    r, c, core = lax.axis_index(ROW), lax.axis_index(COL), lax.axis_index(CORE)
    a = untiled(matrix_tiles)
    slab = blocks * tile // cols
    part = band // cols
    lane = jnp.arange(band, dtype=jnp.int32)

    def places(count, peers, me):
        at = jnp.arange(count, dtype=jnp.int32)
        return (at // tile * peers + me) * tile + at % tile

    def pair(source, first):
        return jnp.concatenate([source[first], source[first + 1]], 1)

    def cleared(x, at, below):
        return jnp.where((at >= below)[:, None], x, 0.0)

    row_of, col_of = places(blocks * tile, rows, r), places(wide * tile, cols, c)

    source = swap(cut_rows(a[:, :tile], blocks, cols), COL)
    p_own, next_own = pair(source, 0), pair(source, 2)
    def flag(x):
        return jnp.broadcast_to(x.astype(jnp.float32), (1, band))

    far, near, held = lax.axis_size("x_lo"), lax.axis_size("z"), tile // cols
    packs = (cols, band // 2 + STEP, band)
    mirrored = to_mirror(p_own)
    arrived = gathered(p_own, COL)
    p_rows, sent = call(
        functools.partial(rows_kernel, (blocks, held, tile)),
        [(blocks * tile, band), (cols, slab + packs[1], band)],
        arrived, mirrored, flag(r >= band // tile), flops=10**9,
    )
    arrived = swap(sent, PAIR)
    gram = arrived[:, slab:].sum(0)
    mine = arrived[:, :slab]
    parts = jnp.stack([gram, other_core(gram)])
    (p_cols,) = call(
        functools.partial(columns_kernel, (far, near, blocks, held, tile)),
        [(wide * tile, band)], mine, other_core(mine), flag(core == 0), flag(c >= band // tile), flops=10**9,
    )
    square = (band, band)
    third = band // STEP // 3 + 1
    for panel in range(PANELS):
        below = (panel + 1) * band
        first = below // tile
        if panel:
            (parts,) = call(gram_kernel, [packs], p_cols, flops=10**9)
            late_z = after(half_z, parts)
            left = jnp.concatenate([y_rows, x_rows - mm(y_rows, late_z)], 1)
            a = a - update(left, jnp.concatenate([x_cols - mm(y_cols, late_z), y_cols], 1))
            parts = swap(parts, COL)
        (inverse,) = call(whole_kernel, [square], parts)

        if panel:
            edge = cut_rows(a[:, :tile], blocks, cols)
            sent = jnp.concatenate([
                cut_rows(mm(a, p_cols), blocks, cols),
                jnp.broadcast_to(p_cols[None, :tile], (cols, tile, band)),
                jnp.concatenate([edge[:, :slab // 2], edge[:, slab // 2:]], 2),
            ], 1)
        else:
            (sent,) = call(
                functools.partial(product_kernel, held), [(cols, slab + tile, band)], a, p_cols, flops=10**9,
            )
        arrived = swap(sent, COL)
        arrived, inverse = after((arrived, inverse), inverse)
        sign, turned, top, u_parts, u_own = call(
            functools.partial(reflect_kernel, first, slab, panel > 0),
            [(1, band), square, square, (cols, slab if panel else 2 * slab, band), (slab, band if panel else 2 * band)],
            arrived, inverse, next_own, flops=10**9,
        )
        def signs_at(at):
            return jnp.where(at[:, None] - below == lane[None, :], sign, 0.0)

        y_rows = mm_nt(p_rows, inverse) - signs_at(row_of)
        y_cols = mm_nt(p_cols, inverse) - signs_at(col_of)
        if panel == 0:
            y_rows, turned = after((y_rows, turned), y_rows)
        mirrored = to_mirror(u_own)
        arrived = swap(u_parts, COL)
        (m1,) = call(functools.partial(outer_first_kernel, (0, third)), [square], turned)
        arrived, m1 = after((arrived, m1), m1)
        mirrored, m1 = after((mirrored, m1), arrived)
        inner, u_rows, *more = call(
            functools.partial(inner_kernel, (blocks, held, tile)),
            [packs] + [(blocks * tile, band)] * (1 if panel else 2), y_rows, arrived, flops=10**9,
        )
        if panel == 0:
            mirrored = jnp.concatenate([mirrored[:, :band], mirrored[:, band:]], 0)
        arrived = gathered(after(mirrored, m1), PAIR)
        if panel:
            m1 = after(m1, (inner, y_cols))
        (m2,) = call(functools.partial(middle_kernel, (third, 2 * third)), [square], m1)
        arrived, m2 = after((arrived, m2), m2)
        if panel == 0:
            inner = jnp.concatenate([inner, jnp.broadcast_to(u_rows[None, :tile], (cols, tile, band))], 1)
        inner = swap(after(inner, arrived), PAIR)
        (tft,) = call(functools.partial(outer_last_kernel, (2 * third, band // STEP)), [square], after(m2, arrived), turned, sign, flops=10**6)
        u_cols = mirror_rows(arrived[:, :slab], core, blocks)
        x_rows, x_cols = mm_nt(u_rows, tft), mm_nt(u_cols, tft)
        if panel == 0:
            next_cols = mirror_rows(arrived[:, slab:], core, blocks)
            y_top = mm_nt(top, inverse) - jnp.where(jnp.eye(band, dtype=bool), sign, 0.0)
            p_cols = next_cols - mm_nt(x_cols, y_top)
            p_rows = more[0] - mm_nt(x_rows, y_top)
            inner, p_cols = after((inner, p_cols), p_cols)
        else:
            a = a - update(jnp.concatenate([y_rows, x_rows], 1), jnp.concatenate([x_cols, y_cols], 1))
            inner, a = after((inner, a), a)
        mine = inner[:, :packs[1]].sum(0)
        theirs = other_core(mine)
        if panel == 0:
            u_top = inner[first // 2, packs[1]:]
            half_z, side = call(
                top_z_kernel, [square, square], mine, theirs, tft, y_top, u_top, other_core(u_top), flag(core == 0),
                flops=10**9,
            )
            p_cols = cleared(p_cols + mm(y_cols, side), col_of, below + band)
            p_rows = cleared(p_rows + mm(y_rows, side), row_of, below + band)
        else:
            (z,) = call(whole_z_kernel, [square], mine, theirs, tft, flops=10**9)
            a = a + update(mm(y_rows, z), y_cols)
    return tiled(a, tile_shape)


def solution(mesh):
    finer = Mesh(mesh.devices.reshape(2, 4, 2, 2, 4), ("x_lo", "z", "core", "x_hi", "y"))
    spec = P(None, ROW, None, None, COL, None)
    return jax.shard_map(on_device, mesh=finer, in_specs=(spec,), out_specs=spec, check_vma=False)
```

```python
import functools

import jax
import jax.numpy as jnp
from jax import lax
from jax.experimental import pallas as pl
from jax.experimental.pallas import tpu as pltpu
from jax.sharding import Mesh
from jax.sharding import PartitionSpec as P

PANELS = 2
PAIR = ("x_lo", "z")
CORE = "core"
ROW = ("x_lo", "z", "core")
COL = ("x_hi", "y")
HI = lax.Precision.HIGHEST


def mm(a, b):
    return lax.dot_general(a, b, (((1,), (0,)), ((), ())), precision=HI, preferred_element_type=jnp.float32)


def mm_nt(a, b):
    return lax.dot_general(a, b, (((1,), (1,)), ((), ())), precision=HI, preferred_element_type=jnp.float32)


def update(a, b):
    return lax.dot_general(
        a, b, (((1,), (1,)), ((), ())), precision=lax.Precision.HIGH, preferred_element_type=jnp.float32
    )


def mm_tn(a, b):
    return lax.dot_general(a, b, (((0,), (0,)), ((), ())), precision=HI, preferred_element_type=jnp.float32)


STEP = 8


def entries(block):
    columns = [jnp.broadcast_to(block[:, j:j + 1], (STEP, 128)) for j in range(STEP)]
    return [[jnp.broadcast_to(columns[j][i:i + 1, :], (STEP, 128)) if j <= i else None for j in range(STEP)] for i in range(STEP)]


def inverse_root(a):
    y = lax.rsqrt(a)
    return y * (1.5 - (0.5 * a) * (y * y))


def chol_inverse_8(a):
    a = [list(row) for row in a]
    x = [[None] * STEP for _ in range(STEP)]
    for k in range(STEP):
        x[k][k] = inverse_root(a[k][k])
        for i in range(k + 1, STEP):
            a[i][k] = a[i][k] * x[k][k]
        for j in range(k + 1, STEP):
            for i in range(j, STEP):
                a[i][j] = a[i][j] - a[i][k] * a[j][k]
    for k in range(STEP):
        for j in range(k):
            s = a[k][j] * x[j][j]
            for q in range(j + 1, k):
                s = s + a[k][q] * x[q][j]
            x[k][j] = -s * x[k][k]
    return x


def apply_lower(x, rows, sub):
    columns = []
    for j in range(STEP):
        col = x[STEP - 1][j]
        for i in range(STEP - 2, j - 1, -1):
            col = jnp.where(sub == i, x[i][j], col)
        columns.append(jnp.where(sub >= j, col, 0.0) if j else col)
    parts = []
    for c in range(0, rows.shape[1], 128):
        terms = [columns[j] * rows[j:j + 1, c:c + 128] for j in range(STEP)]
        while len(terms) > 1:
            terms = [terms[i] + terms[i + 1] for i in range(0, len(terms), 2)]
        parts.append(terms[0])
    return jnp.concatenate(parts, 1)


def three(x):
    hi = x.astype(jnp.bfloat16).astype(jnp.float32)
    rest = x - hi
    mid = rest.astype(jnp.bfloat16).astype(jnp.float32)
    return hi, mid, rest - mid


def outer(left, right):
    a, b, c = three(left)
    d, e, f = three(right)
    lefts = jnp.concatenate([a, a, b, a, c, b], 0).astype(jnp.bfloat16)
    rights = jnp.concatenate([d, e, d, f, d, e], 0).astype(jnp.bfloat16)
    return lax.dot_general(lefts, rights, (((0,), (0,)), ((), ())), preferred_element_type=jnp.float32)


def eliminate(m_ref, n, steps):
    lanes8 = lax.broadcasted_iota(jnp.int32, (STEP, n), 1)
    subs8 = lax.broadcasted_iota(jnp.int32, (STEP, n), 0)
    sub = lax.broadcasted_iota(jnp.int32, (STEP, 128), 0)
    low = steps[0] * STEP
    lanes = lax.broadcasted_iota(jnp.int32, (n - low, n), 1)
    rows_of = lax.broadcasted_iota(jnp.int32, (n - low, n), 0) + low

    def body(k, _):
        at = pl.multiple_of(k * STEP, STEP)
        rows = m_ref[pl.ds(at, STEP), :]
        block = pltpu.roll(rows, n - at, 1)[:, :STEP]
        here = (lanes8 >= at) & (lanes8 < at + STEP)
        unit = jnp.where(here, (lanes8 - at == subs8).astype(jnp.float32), rows)
        kept = apply_lower(chol_inverse_8(entries(block)), unit, sub)
        m_ref[pl.ds(at, STEP), :] = kept
        m = m_ref[low:, :]
        cleared = (lanes >= at) & (lanes < at + STEP) & (rows_of >= at + STEP)
        left = jnp.where(lanes8 >= at + STEP, kept, 0.0)
        m_ref[low:, :] = jnp.where(cleared, 0.0, m) - outer(left, kept)[low:, :]
        return 0

    lax.fori_loop(*steps, body, 0)


def square_places(n):
    return lax.broadcasted_iota(jnp.int32, (n, n), 0), lax.broadcasted_iota(jnp.int32, (n, n), 1)


def packed(m):
    h = m.shape[0] // 2
    r, c = square_places(h)
    low, high = m[:h, :h], m[h:, h:]
    diagonal = jnp.sum(jnp.where(r == c, high, 0.0), axis=0, keepdims=True)
    last = jnp.pad(diagonal, ((0, STEP - 1), (0, h)))
    return jnp.concatenate([jnp.concatenate([m[h:, :h], jnp.where(r >= c, low, high)], 1), last], 0)


def unpacked(p):
    h = p.shape[1] // 2
    r, c = square_places(h)
    corner, both, diagonal = p[:h, :h], p[:h, h:], p[h:h + 1, :h]
    flipped = both.T
    low = jnp.where(r >= c, both, flipped)
    high = jnp.where(r == c, diagonal, jnp.where(r < c, both, flipped))
    return jnp.concatenate(
        [jnp.concatenate([low, corner.T], 1), jnp.concatenate([corner, high], 1)], 0
    )


def call(kernel, shapes, *operands, flops=10**10):
    return pl.pallas_call(
        kernel,
        out_shape=[jax.ShapeDtypeStruct(s, jnp.float32) for s in shapes],
        compiler_params=pltpu.CompilerParams(vmem_limit_bytes=24 * 2**20),
        cost_estimate=pl.CostEstimate(flops=flops, bytes_accessed=2**20, transcendentals=0),
    )(*operands)


def whole_kernel(parts_ref, out_ref):
    n = out_ref.shape[0]
    r, c = square_places(n)
    total = parts_ref[0]
    for i in range(1, parts_ref.shape[0]):
        total = total + parts_ref[i]
    out_ref[...] = unpacked(total)
    for i in range(0, n // STEP, 8):
        eliminate(out_ref, n, (i, i + 8))
    out_ref[...] = jnp.where(r >= c, out_ref[...], 0.0)


def middle_kernel(steps, m_ref, out_ref):
    out_ref[...] = m_ref[...]
    eliminate(out_ref, m_ref.shape[0], steps)


def rows_kernel(shape, arrived_ref, mirrored_ref, kept_ref, rows_ref, parts_ref):
    blocks, held, tile = shape
    slab = blocks * held
    kept = kept_ref[...] > 0.0
    for c in range(arrived_ref.shape[0]):
        for m in range(blocks):
            x = arrived_ref[c, m * held:(m + 1) * held, :]
            if m == 0:
                x = jnp.where(kept, x, 0.0)
            rows_ref[pl.ds(m * tile + c * held, held), :] = x
    gram = packed(mm_tn(rows_ref[...], rows_ref[...]))
    for i in range(parts_ref.shape[0]):
        parts_ref[i, :slab, :] = mirrored_ref[...]
        parts_ref[i, slab:, :] = gram


def columns_kernel(shape, mine_ref, theirs_ref, even_ref, kept_ref, columns_ref):
    far, near, blocks, held, tile = shape
    even = even_ref[...] > 0.0
    kept = kept_ref[...] > 0.0
    for i in range(far):
        for z in range(near):
            for m in range(blocks):
                a = mine_ref[i * near + z, m * held:(m + 1) * held, :]
                b = theirs_ref[i * near + z, m * held:(m + 1) * held, :]
                pair = jnp.concatenate([jnp.where(even, a, b), jnp.where(even, b, a)], 0)
                if m == 0 and i == 0:
                    pair = jnp.where(kept, pair, 0.0)
                columns_ref[pl.ds((m * far + i) * tile + z * 2 * held, 2 * held), :] = pair


def product_kernel(held, a_ref, columns_ref, sent_ref):
    tile = columns_ref.shape[1] // 2
    blocks = a_ref.shape[0] // tile
    slab = blocks * held
    columns = columns_ref[...]
    for m in range(blocks):
        u = mm(a_ref[m * tile:(m + 1) * tile, :], columns)
        for i in range(sent_ref.shape[0]):
            sent_ref[i, m * held:(m + 1) * held, :] = u[i * held:(i + 1) * held, :]
    for i in range(sent_ref.shape[0]):
        sent_ref[i, slab:, :] = columns_ref[:tile, :]


def spread(x, parts_ref):
    for i in range(parts_ref.shape[0]):
        parts_ref[i] = x


def gram_kernel(columns_ref, parts_ref):
    spread(packed(mm_tn(columns_ref[...], columns_ref[...])), parts_ref)


def inner_kernel(shape, y_ref, arrived_ref, parts_ref, *gathered_refs):
    blocks, held, tile = shape
    u_ref = gathered_refs[0]
    for k, rows_ref in enumerate(gathered_refs):
        for c in range(arrived_ref.shape[0]):
            for m in range(blocks):
                at = (k * blocks + m) * held
                rows_ref[pl.ds(m * tile + c * held, held), :] = arrived_ref[c, at:at + held, :]
    half = packed(mm_tn(y_ref[...], u_ref[...]))
    for i in range(parts_ref.shape[0]):
        parts_ref[i, :half.shape[0], :] = half
        if len(gathered_refs) > 1:
            parts_ref[i, half.shape[0]:, :] = u_ref[:tile, :]


def reflect_kernel(first, slab, inside, arrived_ref, inverse_ref, edge_ref, sign_ref, turned_ref, top_ref, parts_ref, own_ref):
    n = inverse_ref.shape[0]
    r, c = square_places(n)
    tile = n // 2
    for i in range(2):
        top_ref[i * tile:(i + 1) * tile, :] = arrived_ref[first + i, slab:slab + tile, :]
    q1t = mm_nt(inverse_ref[...], top_ref[...])
    diagonal = jnp.sum(jnp.where(r == c, q1t, 0.0), axis=0, keepdims=True)
    sign = jnp.where(diagonal >= 0, -1.0, 1.0)
    sign_ref[...] = sign
    turned_ref[...] = jnp.where(r == c, q1t - sign, q1t)
    total = arrived_ref[0, :slab, :]
    for i in range(1, arrived_ref.shape[0]):
        total = total + arrived_ref[i, :slab, :]
    if inside:
        halves = [arrived_ref[first + i, slab + tile:slab + tile + slab // 2, :] for i in range(2)]
        edge = jnp.concatenate([jnp.concatenate([x[:, :tile], x[:, tile:]], 0) for x in halves], 1)
    else:
        edge = edge_ref[...]
        own_ref[:, n:] = edge
        for i in range(parts_ref.shape[0]):
            parts_ref[i, slab:, :] = edge
    own = mm_nt(total, inverse_ref[...]) - edge * sign
    own_ref[:, :n] = own
    for i in range(parts_ref.shape[0]):
        parts_ref[i, :slab, :] = own


def outer_first_kernel(steps, turned_ref, m_ref):
    m_ref[...] = mm_nt(turned_ref[...], turned_ref[...])
    eliminate(m_ref, m_ref.shape[0], steps)


def outer_last_kernel(steps, m_ref, turned_ref, sign_ref, tft_ref):
    n = m_ref.shape[0]
    r, c = square_places(n)
    tft_ref[...] = m_ref[...]
    eliminate(tft_ref, n, steps)
    root = jnp.where(r >= c, tft_ref[...], 0.0)
    tft_ref[...] = -mm(mm_tn(root, root), turned_ref[...]) * sign_ref[...]


def half_z_of(mine_ref, theirs_ref, tft_ref):
    return 0.5 * mm_nt(mm(tft_ref[...], unpacked(mine_ref[...] + theirs_ref[...])), tft_ref[...])


def top_z_kernel(mine_ref, theirs_ref, tft_ref, y_top_ref, a_ref, b_ref, even_ref, z_ref, side_ref):
    even = even_ref[...] > 0.0
    a, b = a_ref[...], b_ref[...]
    u_top = jnp.concatenate([jnp.where(even, a, b), jnp.where(even, b, a)], 0)
    z = half_z_of(mine_ref, theirs_ref, tft_ref)
    z_ref[...] = z
    side_ref[...] = mm_nt(z + z.T, y_top_ref[...]) - mm_nt(tft_ref[...], u_top)


def whole_z_kernel(mine_ref, theirs_ref, tft_ref, z_ref):
    z = half_z_of(mine_ref, theirs_ref, tft_ref)
    z_ref[...] = z + z.T


def swap(x, axis):
    return lax.all_to_all(x, axis, 0, 0, tiled=True)


def gathered(x, axis):
    return swap(jnp.broadcast_to(x[None], (lax.axis_size(axis), *x.shape)), axis)


def other_core(x):
    return lax.ppermute(x, CORE, [(0, 1), (1, 0)])


def in_core_order(mine, core, axis):
    theirs = other_core(mine)
    first = core == 0
    return jnp.stack([jnp.where(first, mine, theirs), jnp.where(first, theirs, mine)], axis)


def to_mirror(piece):
    rows, cols = lax.axis_size(ROW), lax.axis_size(COL)
    pairs = []
    for r in range(rows):
        for c in range(cols):
            to_row, to_col = r // cols * cols + c, r % cols
            pairs.append((r * cols + c, to_row * cols + to_col))
    return lax.ppermute(piece, ROW + COL, pairs)


def cut_rows(x, blocks, peers):
    width = x.shape[-1]
    return x.reshape(blocks, peers, -1, width).transpose(1, 0, 2, 3).reshape(peers, -1, width)


def joined_rows(slabs, blocks):
    peers, _, width = slabs.shape
    return slabs.reshape(peers, blocks, -1, width).transpose(1, 0, 2, 3).reshape(-1, width)


def mirror_rows(mine, core, blocks):
    far, near = lax.axis_size("x_lo"), lax.axis_size("z")
    width = mine.shape[-1]
    both = in_core_order(mine.reshape(far, near, blocks, -1, width), core, 2)
    return both.transpose(3, 0, 1, 2, 4, 5).reshape(-1, width)


def untile_kernel(wide, tiles_ref, a_ref):
    rows, lanes = a_ref.shape[0], tiles_ref.shape[1]
    for n in range(wide):
        a_ref[:, n * lanes:(n + 1) * lanes] = tiles_ref[pl.ds(n, rows, stride=wide), :]


def untiled(matrix_tiles):
    blocks, _, tile, wide, _, lanes = matrix_tiles.shape
    return pl.pallas_call(
        functools.partial(untile_kernel, wide),
        grid=(blocks,),
        in_specs=[pl.BlockSpec((tile * wide, lanes), lambda i: (i, 0))],
        out_specs=pl.BlockSpec((tile, wide * lanes), lambda i: (i, 0)),
        out_shape=jax.ShapeDtypeStruct((blocks * tile, wide * lanes), jnp.float32),
        compiler_params=pltpu.CompilerParams(vmem_limit_bytes=16 * 2**20),
    )(matrix_tiles.reshape(blocks * tile * wide, lanes))


def tile_kernel(wide, a_ref, tiles_ref):
    rows, lanes = a_ref.shape[0], tiles_ref.shape[1]
    for n in range(wide):
        tiles_ref[pl.ds(n, rows, stride=wide), :] = a_ref[:, n * lanes:(n + 1) * lanes]


def tiled(a, shape):
    blocks, _, tile, wide, _, lanes = shape
    return pl.pallas_call(
        functools.partial(tile_kernel, wide),
        grid=(blocks,),
        in_specs=[pl.BlockSpec((tile, wide * lanes), lambda i: (i, 0))],
        out_specs=pl.BlockSpec((tile * wide, lanes), lambda i: (i, 0)),
        out_shape=jax.ShapeDtypeStruct((blocks * tile * wide, lanes), jnp.float32),
        compiler_params=pltpu.CompilerParams(vmem_limit_bytes=16 * 2**20),
    )(a).reshape(shape)


def after(x, other):
    return lax.optimization_barrier((x, other))[0]


def on_device(matrix_tiles):
    tile_shape = matrix_tiles.shape
    blocks, tile, wide = tile_shape[0], tile_shape[2], tile_shape[3]
    band = 2 * tile
    rows, cols = lax.axis_size(ROW), lax.axis_size(COL)
    r, c, core = lax.axis_index(ROW), lax.axis_index(COL), lax.axis_index(CORE)
    a = untiled(matrix_tiles)
    slab = blocks * tile // cols
    part = band // cols
    lane = jnp.arange(band, dtype=jnp.int32)

    def places(count, peers, me):
        at = jnp.arange(count, dtype=jnp.int32)
        return (at // tile * peers + me) * tile + at % tile

    def pair(source, first):
        return jnp.concatenate([source[first], source[first + 1]], 1)

    def cleared(x, at, below):
        return jnp.where((at >= below)[:, None], x, 0.0)

    row_of, col_of = places(blocks * tile, rows, r), places(wide * tile, cols, c)

    source = swap(cut_rows(a[:, :tile], blocks, cols), COL)
    p_own, next_own = pair(source, 0), pair(source, 2)
    def flag(x):
        return jnp.broadcast_to(x.astype(jnp.float32), (1, band))

    far, near, held = lax.axis_size("x_lo"), lax.axis_size("z"), tile // cols
    packs = (cols, band // 2 + STEP, band)
    mirrored = to_mirror(p_own)
    arrived = gathered(p_own, COL)
    p_rows, sent = call(
        functools.partial(rows_kernel, (blocks, held, tile)),
        [(blocks * tile, band), (cols, slab + packs[1], band)],
        arrived, mirrored, flag(r >= band // tile), flops=10**9,
    )
    arrived = swap(sent, PAIR)
    gram = arrived[:, slab:].sum(0)
    mine = arrived[:, :slab]
    parts = jnp.stack([gram, other_core(gram)])
    (p_cols,) = call(
        functools.partial(columns_kernel, (far, near, blocks, held, tile)),
        [(wide * tile, band)], mine, other_core(mine), flag(core == 0), flag(c >= band // tile), flops=10**9,
    )
    square = (band, band)
    third = band // STEP // 3 + 1
    for panel in range(PANELS):
        below = (panel + 1) * band
        first = below // tile
        if panel:
            (parts,) = call(gram_kernel, [packs], p_cols, flops=10**9)
            late_z, x_cols, u_rows, tft = after((half_z, x_cols, u_rows, tft), parts)
            x_rows = mm_nt(u_rows, tft)
            left = jnp.concatenate([y_rows, x_rows - mm(y_rows, late_z)], 1)
            a = a - update(left, jnp.concatenate([x_cols - mm(y_cols, late_z), y_cols], 1))
            parts = swap(parts, COL)
        (inverse,) = call(whole_kernel, [square], parts)
        if panel:
            x_rows, side = after((x_rows, side), inverse)
            p_rows = more[0] + mm_nt(jnp.concatenate([y_rows, x_rows], 1), jnp.concatenate([side.T, -y_top], 1))
            p_rows = cleared(p_rows, row_of, below)

        if panel:
            edge = cut_rows(a[:, :tile], blocks, cols)
            sent = jnp.concatenate([
                cut_rows(mm(a, p_cols), blocks, cols),
                jnp.broadcast_to(p_cols[None, :tile], (cols, tile, band)),
                jnp.concatenate([edge[:, :slab // 2], edge[:, slab // 2:]], 2),
            ], 1)
        else:
            (sent,) = call(
                functools.partial(product_kernel, held), [(cols, slab + tile, band)], a, p_cols, flops=10**9,
            )
        arrived = swap(sent, COL)
        arrived, inverse = after((arrived, inverse), inverse)
        sign, turned, top, u_parts, u_own = call(
            functools.partial(reflect_kernel, first, slab, panel > 0),
            [(1, band), square, square, (cols, slab if panel else 2 * slab, band), (slab, band if panel else 2 * band)],
            arrived, inverse, next_own, flops=10**9,
        )
        def signs_at(at):
            return jnp.where(at[:, None] - below == lane[None, :], sign, 0.0)

        y_rows = mm_nt(p_rows, inverse) - signs_at(row_of)
        y_cols = mm_nt(p_cols, inverse) - signs_at(col_of)
        if panel == 0:
            y_rows, turned = after((y_rows, turned), y_rows)
        mirrored = to_mirror(u_own)
        arrived = swap(u_parts, COL)
        (m1,) = call(functools.partial(outer_first_kernel, (0, third)), [square], turned)
        arrived, m1 = after((arrived, m1), m1)
        mirrored, m1 = after((mirrored, m1), arrived)
        inner, u_rows, *more = call(
            functools.partial(inner_kernel, (blocks, held, tile)),
            [packs if panel else (cols, packs[1] + tile, band)] + [(blocks * tile, band)] * (1 if panel else 2),
            y_rows, arrived, flops=10**9,
        )
        if panel == 0:
            mirrored = jnp.concatenate([mirrored[:, :band], mirrored[:, band:]], 0)
        arrived = gathered(after(mirrored, m1), PAIR)
        m1 = after(m1, (inner, y_cols) if panel else inner)
        (m2,) = call(functools.partial(middle_kernel, (third, 2 * third)), [square], m1)
        arrived, m2 = after((arrived, m2), m2)
        inner = swap(after(inner, arrived), PAIR)
        (tft,) = call(functools.partial(outer_last_kernel, (2 * third, band // STEP)), [square], after(m2, arrived), turned, sign, flops=10**6)
        u_cols = mirror_rows(arrived[:, :slab], core, blocks)
        x_cols = mm_nt(u_cols, tft)
        if panel == 0:
            next_cols = mirror_rows(arrived[:, slab:], core, blocks)
            y_top = mm_nt(top, inverse) - jnp.where(jnp.eye(band, dtype=bool), sign, 0.0)
            p_cols = next_cols - mm_nt(x_cols, y_top)
            inner, p_cols = after((inner, p_cols), p_cols)
        else:
            x_rows = mm_nt(u_rows, tft)
            a = a - update(jnp.concatenate([y_rows, x_rows], 1), jnp.concatenate([x_cols, y_cols], 1))
            inner, a = after((inner, a), a)
        mine = inner[:, :packs[1]].sum(0)
        theirs = other_core(mine)
        if panel == 0:
            u_top = inner[first // 2, packs[1]:]
            half_z, side = call(
                top_z_kernel, [square, square], mine, theirs, tft, y_top, u_top, other_core(u_top), flag(core == 0),
                flops=10**9,
            )
            p_cols = cleared(p_cols + mm(y_cols, side), col_of, below + band)
        else:
            (z,) = call(whole_z_kernel, [square], mine, theirs, tft, flops=10**9)
            a = a + update(mm(y_rows, z), y_cols)
    return tiled(a, tile_shape)


def solution(mesh):
    finer = Mesh(mesh.devices.reshape(2, 4, 2, 2, 4), ("x_lo", "z", "core", "x_hi", "y"))
    spec = P(None, ROW, None, None, COL, None)
    return jax.shard_map(on_device, mesh=finer, in_specs=(spec,), out_specs=spec, check_vma=False)
```

```python
import functools

import jax
import jax.numpy as jnp
from jax import lax
from jax.experimental import pallas as pl
from jax.experimental.pallas import tpu as pltpu
from jax.sharding import Mesh
from jax.sharding import PartitionSpec as P

PANELS = 2
PAIR = ("x_lo", "z")
CORE = "core"
ROW = ("x_lo", "z", "core")
COL = ("x_hi", "y")
HI = lax.Precision.HIGHEST


def mm(a, b):
    return lax.dot_general(a, b, (((1,), (0,)), ((), ())), precision=HI, preferred_element_type=jnp.float32)


def mm_nt(a, b):
    return lax.dot_general(a, b, (((1,), (1,)), ((), ())), precision=HI, preferred_element_type=jnp.float32)


def update(a, b):
    return lax.dot_general(
        a, b, (((1,), (1,)), ((), ())), precision=lax.Precision.HIGH, preferred_element_type=jnp.float32
    )


def mm_tn(a, b):
    return lax.dot_general(a, b, (((0,), (0,)), ((), ())), precision=HI, preferred_element_type=jnp.float32)


STEP = 8


def entries(block):
    columns = [jnp.broadcast_to(block[:, j:j + 1], (STEP, 128)) for j in range(STEP)]
    return [[jnp.broadcast_to(columns[j][i:i + 1, :], (STEP, 128)) if j <= i else None for j in range(STEP)] for i in range(STEP)]


def inverse_root(a):
    y = lax.rsqrt(a)
    return y * (1.5 - (0.5 * a) * (y * y))


def chol_inverse_8(a):
    a = [list(row) for row in a]
    x = [[None] * STEP for _ in range(STEP)]
    for k in range(STEP):
        x[k][k] = inverse_root(a[k][k])
        for i in range(k + 1, STEP):
            a[i][k] = a[i][k] * x[k][k]
        for j in range(k + 1, STEP):
            for i in range(j, STEP):
                a[i][j] = a[i][j] - a[i][k] * a[j][k]
    for k in range(STEP):
        for j in range(k):
            s = a[k][j] * x[j][j]
            for q in range(j + 1, k):
                s = s + a[k][q] * x[q][j]
            x[k][j] = -s * x[k][k]
    return x


def apply_lower(x, rows, sub):
    columns = []
    for j in range(STEP):
        col = x[STEP - 1][j]
        for i in range(STEP - 2, j - 1, -1):
            col = jnp.where(sub == i, x[i][j], col)
        columns.append(jnp.where(sub >= j, col, 0.0) if j else col)
    parts = []
    for c in range(0, rows.shape[1], 128):
        terms = [columns[j] * rows[j:j + 1, c:c + 128] for j in range(STEP)]
        while len(terms) > 1:
            terms = [terms[i] + terms[i + 1] for i in range(0, len(terms), 2)]
        parts.append(terms[0])
    return jnp.concatenate(parts, 1)


def three(x):
    hi = x.astype(jnp.bfloat16).astype(jnp.float32)
    rest = x - hi
    mid = rest.astype(jnp.bfloat16).astype(jnp.float32)
    return hi, mid, rest - mid


def outer(left, right):
    a, b, c = three(left)
    d, e, f = three(right)
    lefts = jnp.concatenate([a, a, b, a, c, b], 0).astype(jnp.bfloat16)
    rights = jnp.concatenate([d, e, d, f, d, e], 0).astype(jnp.bfloat16)
    return lax.dot_general(lefts, rights, (((0,), (0,)), ((), ())), preferred_element_type=jnp.float32)


def eliminate(m_ref, n, steps):
    lanes8 = lax.broadcasted_iota(jnp.int32, (STEP, n), 1)
    subs8 = lax.broadcasted_iota(jnp.int32, (STEP, n), 0)
    sub = lax.broadcasted_iota(jnp.int32, (STEP, 128), 0)
    low = steps[0] * STEP
    lanes = lax.broadcasted_iota(jnp.int32, (n - low, n), 1)
    rows_of = lax.broadcasted_iota(jnp.int32, (n - low, n), 0) + low

    def body(k, _):
        at = pl.multiple_of(k * STEP, STEP)
        rows = m_ref[pl.ds(at, STEP), :]
        block = pltpu.roll(rows, n - at, 1)[:, :STEP]
        here = (lanes8 >= at) & (lanes8 < at + STEP)
        unit = jnp.where(here, (lanes8 - at == subs8).astype(jnp.float32), rows)
        kept = apply_lower(chol_inverse_8(entries(block)), unit, sub)
        m_ref[pl.ds(at, STEP), :] = kept
        m = m_ref[low:, :]
        cleared = (lanes >= at) & (lanes < at + STEP) & (rows_of >= at + STEP)
        left = jnp.where(lanes8 >= at + STEP, kept, 0.0)
        m_ref[low:, :] = jnp.where(cleared, 0.0, m) - outer(left, kept)[low:, :]
        return 0

    lax.fori_loop(*steps, body, 0)


def square_places(n):
    return lax.broadcasted_iota(jnp.int32, (n, n), 0), lax.broadcasted_iota(jnp.int32, (n, n), 1)


def packed(m):
    h = m.shape[0] // 2
    r, c = square_places(h)
    low, high = m[:h, :h], m[h:, h:]
    diagonal = jnp.sum(jnp.where(r == c, high, 0.0), axis=0, keepdims=True)
    last = jnp.pad(diagonal, ((0, STEP - 1), (0, h)))
    return jnp.concatenate([jnp.concatenate([m[h:, :h], jnp.where(r >= c, low, high)], 1), last], 0)


def unpacked(p):
    h = p.shape[1] // 2
    r, c = square_places(h)
    corner, both, diagonal = p[:h, :h], p[:h, h:], p[h:h + 1, :h]
    flipped = both.T
    low = jnp.where(r >= c, both, flipped)
    high = jnp.where(r == c, diagonal, jnp.where(r < c, both, flipped))
    return jnp.concatenate(
        [jnp.concatenate([low, corner.T], 1), jnp.concatenate([corner, high], 1)], 0
    )


def call(kernel, shapes, *operands, flops=10**10):
    return pl.pallas_call(
        kernel,
        out_shape=[jax.ShapeDtypeStruct(s, jnp.float32) for s in shapes],
        compiler_params=pltpu.CompilerParams(vmem_limit_bytes=24 * 2**20),
        cost_estimate=pl.CostEstimate(flops=flops, bytes_accessed=2**20, transcendentals=0),
    )(*operands)


def whole_kernel(parts_ref, out_ref):
    n = out_ref.shape[0]
    r, c = square_places(n)
    total = parts_ref[0]
    for i in range(1, parts_ref.shape[0]):
        total = total + parts_ref[i]
    out_ref[...] = unpacked(total)
    for i in range(0, n // STEP, 8):
        eliminate(out_ref, n, (i, i + 8))
    out_ref[...] = jnp.where(r >= c, out_ref[...], 0.0)


def middle_kernel(steps, m_ref, out_ref):
    out_ref[...] = m_ref[...]
    eliminate(out_ref, m_ref.shape[0], steps)


def rows_kernel(shape, arrived_ref, mirrored_ref, kept_ref, rows_ref, parts_ref):
    blocks, held, tile = shape
    slab = blocks * held
    kept = kept_ref[...] > 0.0
    for c in range(arrived_ref.shape[0]):
        for m in range(blocks):
            x = arrived_ref[c, m * held:(m + 1) * held, :]
            if m == 0:
                x = jnp.where(kept, x, 0.0)
            rows_ref[pl.ds(m * tile + c * held, held), :] = x
    gram = packed(mm_tn(rows_ref[...], rows_ref[...]))
    for i in range(parts_ref.shape[0]):
        parts_ref[i, :slab, :] = mirrored_ref[...]
        parts_ref[i, slab:, :] = gram


def columns_kernel(shape, mine_ref, theirs_ref, even_ref, kept_ref, columns_ref):
    far, near, blocks, held, tile = shape
    even = even_ref[...] > 0.0
    kept = kept_ref[...] > 0.0
    for i in range(far):
        for z in range(near):
            for m in range(blocks):
                a = mine_ref[i * near + z, m * held:(m + 1) * held, :]
                b = theirs_ref[i * near + z, m * held:(m + 1) * held, :]
                pair = jnp.concatenate([jnp.where(even, a, b), jnp.where(even, b, a)], 0)
                if m == 0 and i == 0:
                    pair = jnp.where(kept, pair, 0.0)
                columns_ref[pl.ds((m * far + i) * tile + z * 2 * held, 2 * held), :] = pair


def product_kernel(held, a_ref, columns_ref, sent_ref):
    tile = columns_ref.shape[1] // 2
    blocks = a_ref.shape[0] // tile
    slab = blocks * held
    columns = columns_ref[...]
    for m in range(blocks):
        u = mm(a_ref[m * tile:(m + 1) * tile, :], columns)
        for i in range(sent_ref.shape[0]):
            sent_ref[i, m * held:(m + 1) * held, :] = u[i * held:(i + 1) * held, :]
    for i in range(sent_ref.shape[0]):
        sent_ref[i, slab:, :] = columns_ref[:tile, :]


def spread(x, parts_ref):
    for i in range(parts_ref.shape[0]):
        parts_ref[i] = x


def gram_kernel(columns_ref, parts_ref):
    spread(packed(mm_tn(columns_ref[...], columns_ref[...])), parts_ref)


def inner_kernel(shape, y_ref, arrived_ref, parts_ref, *gathered_refs):
    blocks, held, tile = shape
    u_ref = gathered_refs[0]
    for k, rows_ref in enumerate(gathered_refs):
        for c in range(arrived_ref.shape[0]):
            for m in range(blocks):
                at = (k * blocks + m) * held
                rows_ref[pl.ds(m * tile + c * held, held), :] = arrived_ref[c, at:at + held, :]
    half = packed(mm_tn(y_ref[...], u_ref[...]))
    for i in range(parts_ref.shape[0]):
        parts_ref[i, :half.shape[0], :] = half
        if len(gathered_refs) > 1:
            parts_ref[i, half.shape[0]:, :] = u_ref[:tile, :]


def reflect_kernel(first, slab, inside, arrived_ref, inverse_ref, edge_ref, sign_ref, turned_ref, top_ref, parts_ref, own_ref):
    n = inverse_ref.shape[0]
    r, c = square_places(n)
    tile = n // 2
    for i in range(2):
        top_ref[i * tile:(i + 1) * tile, :] = arrived_ref[first + i, slab:slab + tile, :]
    q1t = mm_nt(inverse_ref[...], top_ref[...])
    diagonal = jnp.sum(jnp.where(r == c, q1t, 0.0), axis=0, keepdims=True)
    sign = jnp.where(diagonal >= 0, -1.0, 1.0)
    sign_ref[...] = sign
    turned_ref[...] = jnp.where(r == c, q1t - sign, q1t)
    total = arrived_ref[0, :slab, :]
    for i in range(1, arrived_ref.shape[0]):
        total = total + arrived_ref[i, :slab, :]
    if inside:
        halves = [arrived_ref[first + i, slab + tile:slab + tile + slab // 2, :] for i in range(2)]
        edge = jnp.concatenate([jnp.concatenate([x[:, :tile], x[:, tile:]], 0) for x in halves], 1)
    else:
        edge = edge_ref[...]
        own_ref[:, n:] = edge
        for i in range(parts_ref.shape[0]):
            parts_ref[i, slab:, :] = edge
    own = mm_nt(total, inverse_ref[...]) - edge * sign
    own_ref[:, :n] = own
    for i in range(parts_ref.shape[0]):
        parts_ref[i, :slab, :] = own


def outer_first_kernel(steps, turned_ref, m_ref):
    m_ref[...] = mm_nt(turned_ref[...], turned_ref[...])
    eliminate(m_ref, m_ref.shape[0], steps)


def outer_last_kernel(steps, m_ref, turned_ref, sign_ref, tft_ref):
    n = m_ref.shape[0]
    r, c = square_places(n)
    tft_ref[...] = m_ref[...]
    eliminate(tft_ref, n, steps)
    root = jnp.where(r >= c, tft_ref[...], 0.0)
    tft_ref[...] = -mm(mm_tn(root, root), turned_ref[...]) * sign_ref[...]


def half_z_of(mine_ref, theirs_ref, tft_ref):
    return 0.5 * mm_nt(mm(tft_ref[...], unpacked(mine_ref[...] + theirs_ref[...])), tft_ref[...])


def top_z_kernel(mine_ref, theirs_ref, tft_ref, y_top_ref, a_ref, b_ref, even_ref, z_ref, side_ref):
    even = even_ref[...] > 0.0
    a, b = a_ref[...], b_ref[...]
    u_top = jnp.concatenate([jnp.where(even, a, b), jnp.where(even, b, a)], 0)
    z = half_z_of(mine_ref, theirs_ref, tft_ref)
    z = z + z.T
    z_ref[...] = z
    side_ref[...] = mm_nt(z, y_top_ref[...]) - mm_nt(tft_ref[...], u_top)


def whole_z_kernel(mine_ref, theirs_ref, tft_ref, z_ref):
    z = half_z_of(mine_ref, theirs_ref, tft_ref)
    z_ref[...] = z + z.T


def swap(x, axis):
    return lax.all_to_all(x, axis, 0, 0, tiled=True)


def gathered(x, axis):
    return swap(jnp.broadcast_to(x[None], (lax.axis_size(axis), *x.shape)), axis)


def other_core(x):
    return lax.ppermute(x, CORE, [(0, 1), (1, 0)])


def in_core_order(mine, core, axis):
    theirs = other_core(mine)
    first = core == 0
    return jnp.stack([jnp.where(first, mine, theirs), jnp.where(first, theirs, mine)], axis)


def to_mirror(piece):
    rows, cols = lax.axis_size(ROW), lax.axis_size(COL)
    pairs = []
    for r in range(rows):
        for c in range(cols):
            to_row, to_col = r // cols * cols + c, r % cols
            pairs.append((r * cols + c, to_row * cols + to_col))
    return lax.ppermute(piece, ROW + COL, pairs)


def cut_rows(x, blocks, peers):
    width = x.shape[-1]
    return x.reshape(blocks, peers, -1, width).transpose(1, 0, 2, 3).reshape(peers, -1, width)


def joined_rows(slabs, blocks):
    peers, _, width = slabs.shape
    return slabs.reshape(peers, blocks, -1, width).transpose(1, 0, 2, 3).reshape(-1, width)


def mirror_rows(mine, core, blocks):
    far, near = lax.axis_size("x_lo"), lax.axis_size("z")
    width = mine.shape[-1]
    both = in_core_order(mine.reshape(far, near, blocks, -1, width), core, 2)
    return both.transpose(3, 0, 1, 2, 4, 5).reshape(-1, width)


def untile_kernel(wide, tiles_ref, a_ref):
    rows, lanes = a_ref.shape[0], tiles_ref.shape[1]
    for n in range(wide):
        a_ref[:, n * lanes:(n + 1) * lanes] = tiles_ref[pl.ds(n, rows, stride=wide), :]


def untiled(matrix_tiles):
    blocks, _, tile, wide, _, lanes = matrix_tiles.shape
    return pl.pallas_call(
        functools.partial(untile_kernel, wide),
        grid=(blocks,),
        in_specs=[pl.BlockSpec((tile * wide, lanes), lambda i: (i, 0))],
        out_specs=pl.BlockSpec((tile, wide * lanes), lambda i: (i, 0)),
        out_shape=jax.ShapeDtypeStruct((blocks * tile, wide * lanes), jnp.float32),
        compiler_params=pltpu.CompilerParams(vmem_limit_bytes=16 * 2**20),
    )(matrix_tiles.reshape(blocks * tile * wide, lanes))


def tile_kernel(wide, a_ref, tiles_ref):
    rows, lanes = a_ref.shape[0], tiles_ref.shape[1]
    for n in range(wide):
        tiles_ref[pl.ds(n, rows, stride=wide), :] = a_ref[:, n * lanes:(n + 1) * lanes]


def tiled(a, shape):
    blocks, _, tile, wide, _, lanes = shape
    return pl.pallas_call(
        functools.partial(tile_kernel, wide),
        grid=(blocks,),
        in_specs=[pl.BlockSpec((tile, wide * lanes), lambda i: (i, 0))],
        out_specs=pl.BlockSpec((tile * wide, lanes), lambda i: (i, 0)),
        out_shape=jax.ShapeDtypeStruct((blocks * tile * wide, lanes), jnp.float32),
        compiler_params=pltpu.CompilerParams(vmem_limit_bytes=16 * 2**20),
    )(a).reshape(shape)


def after(x, other):
    return lax.optimization_barrier((x, other))[0]


def on_device(matrix_tiles):
    tile_shape = matrix_tiles.shape
    blocks, tile, wide = tile_shape[0], tile_shape[2], tile_shape[3]
    band = 2 * tile
    rows, cols = lax.axis_size(ROW), lax.axis_size(COL)
    r, c, core = lax.axis_index(ROW), lax.axis_index(COL), lax.axis_index(CORE)
    a = untiled(matrix_tiles)
    slab = blocks * tile // cols
    part = band // cols
    lane = jnp.arange(band, dtype=jnp.int32)

    def places(count, peers, me):
        at = jnp.arange(count, dtype=jnp.int32)
        return (at // tile * peers + me) * tile + at % tile

    def pair(source, first):
        return jnp.concatenate([source[first], source[first + 1]], 1)

    def cleared(x, at, below):
        return jnp.where((at >= below)[:, None], x, 0.0)

    row_of, col_of = places(blocks * tile, rows, r), places(wide * tile, cols, c)

    source = swap(cut_rows(a[:, :tile], blocks, cols), COL)
    p_own, next_own = pair(source, 0), pair(source, 2)
    def flag(x):
        return jnp.broadcast_to(x.astype(jnp.float32), (1, band))

    far, near, held = lax.axis_size("x_lo"), lax.axis_size("z"), tile // cols
    packs = (cols, band // 2 + STEP, band)
    mirrored = to_mirror(p_own)
    arrived = gathered(p_own, COL)
    p_rows, sent = call(
        functools.partial(rows_kernel, (blocks, held, tile)),
        [(blocks * tile, band), (cols, slab + packs[1], band)],
        arrived, mirrored, flag(r >= band // tile), flops=10**9,
    )
    arrived = swap(sent, PAIR)
    gram = arrived[:, slab:].sum(0)
    mine = arrived[:, :slab]
    parts = jnp.stack([gram, other_core(gram)])
    (p_cols,) = call(
        functools.partial(columns_kernel, (far, near, blocks, held, tile)),
        [(wide * tile, band)], mine, other_core(mine), flag(core == 0), flag(c >= band // tile), flops=10**9,
    )
    square = (band, band)
    third = band // STEP // 3 + 1
    for panel in range(PANELS):
        below = (panel + 1) * band
        first = below // tile
        if panel:
            (parts,) = call(gram_kernel, [packs], p_cols, flops=10**9)
            a = a + update(mm(y_rows, after(z, parts)), y_cols)
            parts = swap(parts, COL)
        (inverse,) = call(whole_kernel, [square], parts)
        if panel:
            x_rows, side = after((x_rows, side), inverse)
            p_rows = cleared(more[0] - mm_nt(x_rows, y_top) + mm(y_rows, side), row_of, below)

        if panel:
            edge = cut_rows(a[:, :tile], blocks, cols)
            sent = jnp.concatenate([
                cut_rows(mm(a, p_cols), blocks, cols),
                jnp.broadcast_to(p_cols[None, :tile], (cols, tile, band)),
                jnp.concatenate([edge[:, :slab // 2], edge[:, slab // 2:]], 2),
            ], 1)
        else:
            (sent,) = call(
                functools.partial(product_kernel, held), [(cols, slab + tile, band)], a, p_cols, flops=10**9,
            )
        arrived = swap(sent, COL)
        arrived, inverse = after((arrived, inverse), inverse)
        sign, turned, top, u_parts, u_own = call(
            functools.partial(reflect_kernel, first, slab, panel > 0),
            [(1, band), square, square, (cols, slab if panel else 2 * slab, band), (slab, band if panel else 2 * band)],
            arrived, inverse, next_own, flops=10**9,
        )
        def signs_at(at):
            return jnp.where(at[:, None] - below == lane[None, :], sign, 0.0)

        y_rows = mm_nt(p_rows, inverse) - signs_at(row_of)
        y_cols = mm_nt(p_cols, inverse) - signs_at(col_of)
        if panel == 0:
            y_rows, turned = after((y_rows, turned), y_rows)
        mirrored = to_mirror(u_own)
        arrived = swap(u_parts, COL)
        (m1,) = call(functools.partial(outer_first_kernel, (0, third)), [square], turned)
        arrived, m1 = after((arrived, m1), m1)
        mirrored, m1 = after((mirrored, m1), arrived)
        inner, u_rows, *more = call(
            functools.partial(inner_kernel, (blocks, held, tile)),
            [packs if panel else (cols, packs[1] + tile, band)] + [(blocks * tile, band)] * (1 if panel else 2),
            y_rows, arrived, flops=10**9,
        )
        if panel == 0:
            mirrored = jnp.concatenate([mirrored[:, :band], mirrored[:, band:]], 0)
        arrived = gathered(after(mirrored, m1), PAIR)
        m1 = after(m1, (inner, y_cols))
        (m2,) = call(functools.partial(middle_kernel, (third, 2 * third)), [square], m1)
        arrived, m2 = after((arrived, m2), m2)
        inner = swap(after(inner, arrived), PAIR)
        (tft,) = call(functools.partial(outer_last_kernel, (2 * third, band // STEP)), [square], after(m2, arrived), turned, sign, flops=10**6)
        u_cols = mirror_rows(arrived[:, :slab], core, blocks)
        x_rows, x_cols = mm_nt(u_rows, tft), mm_nt(u_cols, tft)
        a = a - update(jnp.concatenate([y_rows, x_rows], 1), jnp.concatenate([x_cols, y_cols], 1))
        if panel == 0:
            next_cols = mirror_rows(arrived[:, slab:], core, blocks)
            y_top = mm_nt(top, inverse) - jnp.where(jnp.eye(band, dtype=bool), sign, 0.0)
            p_cols = next_cols - mm_nt(x_cols, y_top)
            inner, p_cols = after((inner, p_cols), p_cols)
        inner, a = after((inner, a), a)
        mine = inner[:, :packs[1]].sum(0)
        theirs = other_core(mine)
        if panel == 0:
            u_top = inner[first // 2, packs[1]:]
            z, side = call(
                top_z_kernel, [square, square], mine, theirs, tft, y_top, u_top, other_core(u_top), flag(core == 0),
                flops=10**9,
            )
            p_cols = cleared(p_cols + mm(y_cols, side), col_of, below + band)
        else:
            (z,) = call(whole_z_kernel, [square], mine, theirs, tft, flops=10**9)
            a = a + update(mm(y_rows, z), y_cols)
    return tiled(a, tile_shape)


def solution(mesh):
    finer = Mesh(mesh.devices.reshape(2, 4, 2, 2, 4), ("x_lo", "z", "core", "x_hi", "y"))
    spec = P(None, ROW, None, None, COL, None)
    return jax.shard_map(on_device, mesh=finer, in_specs=(spec,), out_specs=spec, check_vma=False)
```

```python
import functools

import jax
import jax.numpy as jnp
from jax import lax
from jax.experimental import pallas as pl
from jax.experimental.pallas import tpu as pltpu
from jax.sharding import Mesh
from jax.sharding import PartitionSpec as P

PANELS = 2
PAIR = ("x_lo", "z")
CORE = "core"
ROW = ("x_lo", "z", "core")
COL = ("x_hi", "y")
HI = lax.Precision.HIGHEST


def mm(a, b):
    return lax.dot_general(a, b, (((1,), (0,)), ((), ())), precision=HI, preferred_element_type=jnp.float32)


def mm_nt(a, b):
    return lax.dot_general(a, b, (((1,), (1,)), ((), ())), precision=HI, preferred_element_type=jnp.float32)


def update(a, b):
    return lax.dot_general(
        a, b, (((1,), (1,)), ((), ())), precision=lax.Precision.HIGH, preferred_element_type=jnp.float32
    )


def mm_tn(a, b):
    return lax.dot_general(a, b, (((0,), (0,)), ((), ())), precision=HI, preferred_element_type=jnp.float32)


STEP = 8


def entries(block):
    columns = [jnp.broadcast_to(block[:, j:j + 1], (STEP, 128)) for j in range(STEP)]
    return [[jnp.broadcast_to(columns[j][i:i + 1, :], (STEP, 128)) if j <= i else None for j in range(STEP)] for i in range(STEP)]


def inverse_root(a):
    y = lax.rsqrt(a)
    return y * (1.5 - (0.5 * a) * (y * y))


def chol_inverse_8(a):
    a = [list(row) for row in a]
    x = [[None] * STEP for _ in range(STEP)]
    for k in range(STEP):
        x[k][k] = inverse_root(a[k][k])
        for i in range(k + 1, STEP):
            a[i][k] = a[i][k] * x[k][k]
        for j in range(k + 1, STEP):
            for i in range(j, STEP):
                a[i][j] = a[i][j] - a[i][k] * a[j][k]
    for k in range(STEP):
        for j in range(k):
            s = a[k][j] * x[j][j]
            for q in range(j + 1, k):
                s = s + a[k][q] * x[q][j]
            x[k][j] = -s * x[k][k]
    return x


def apply_lower(x, rows, sub):
    columns = []
    for j in range(STEP):
        col = x[STEP - 1][j]
        for i in range(STEP - 2, j - 1, -1):
            col = jnp.where(sub == i, x[i][j], col)
        columns.append(jnp.where(sub >= j, col, 0.0) if j else col)
    parts = []
    for c in range(0, rows.shape[1], 128):
        terms = [columns[j] * rows[j:j + 1, c:c + 128] for j in range(STEP)]
        while len(terms) > 1:
            terms = [terms[i] + terms[i + 1] for i in range(0, len(terms), 2)]
        parts.append(terms[0])
    return jnp.concatenate(parts, 1)


def three(x):
    hi = x.astype(jnp.bfloat16).astype(jnp.float32)
    rest = x - hi
    mid = rest.astype(jnp.bfloat16).astype(jnp.float32)
    return hi, mid, rest - mid


def outer(left, right):
    a, b, c = three(left)
    d, e, f = three(right)
    lefts = jnp.concatenate([a, a, b, a, c, b], 0).astype(jnp.bfloat16)
    rights = jnp.concatenate([d, e, d, f, d, e], 0).astype(jnp.bfloat16)
    return lax.dot_general(lefts, rights, (((0,), (0,)), ((), ())), preferred_element_type=jnp.float32)


def eliminate(m_ref, n, steps):
    lanes8 = lax.broadcasted_iota(jnp.int32, (STEP, n), 1)
    subs8 = lax.broadcasted_iota(jnp.int32, (STEP, n), 0)
    sub = lax.broadcasted_iota(jnp.int32, (STEP, 128), 0)
    low = steps[0] * STEP
    lanes = lax.broadcasted_iota(jnp.int32, (n - low, n), 1)
    rows_of = lax.broadcasted_iota(jnp.int32, (n - low, n), 0) + low

    def body(k, _):
        at = pl.multiple_of(k * STEP, STEP)
        rows = m_ref[pl.ds(at, STEP), :]
        block = pltpu.roll(rows, n - at, 1)[:, :STEP]
        here = (lanes8 >= at) & (lanes8 < at + STEP)
        unit = jnp.where(here, (lanes8 - at == subs8).astype(jnp.float32), rows)
        kept = apply_lower(chol_inverse_8(entries(block)), unit, sub)
        m_ref[pl.ds(at, STEP), :] = kept
        m = m_ref[low:, :]
        cleared = (lanes >= at) & (lanes < at + STEP) & (rows_of >= at + STEP)
        left = jnp.where(lanes8 >= at + STEP, kept, 0.0)
        m_ref[low:, :] = jnp.where(cleared, 0.0, m) - outer(left, kept)[low:, :]
        return 0

    lax.fori_loop(*steps, body, 0)


def square_places(n):
    return lax.broadcasted_iota(jnp.int32, (n, n), 0), lax.broadcasted_iota(jnp.int32, (n, n), 1)


def packed(m):
    h = m.shape[0] // 2
    r, c = square_places(h)
    low, high = m[:h, :h], m[h:, h:]
    diagonal = jnp.sum(jnp.where(r == c, high, 0.0), axis=0, keepdims=True)
    last = jnp.pad(diagonal, ((0, STEP - 1), (0, h)))
    return jnp.concatenate([jnp.concatenate([m[h:, :h], jnp.where(r >= c, low, high)], 1), last], 0)


def unpacked(p):
    h = p.shape[1] // 2
    r, c = square_places(h)
    corner, both, diagonal = p[:h, :h], p[:h, h:], p[h:h + 1, :h]
    flipped = both.T
    low = jnp.where(r >= c, both, flipped)
    high = jnp.where(r == c, diagonal, jnp.where(r < c, both, flipped))
    return jnp.concatenate(
        [jnp.concatenate([low, corner.T], 1), jnp.concatenate([corner, high], 1)], 0
    )


def call(kernel, shapes, *operands, flops=10**10):
    return pl.pallas_call(
        kernel,
        out_shape=[jax.ShapeDtypeStruct(s, jnp.float32) for s in shapes],
        compiler_params=pltpu.CompilerParams(vmem_limit_bytes=24 * 2**20),
        cost_estimate=pl.CostEstimate(flops=flops, bytes_accessed=2**20, transcendentals=0),
    )(*operands)


def whole_kernel(parts_ref, out_ref):
    n = out_ref.shape[0]
    r, c = square_places(n)
    total = parts_ref[0]
    for i in range(1, parts_ref.shape[0]):
        total = total + parts_ref[i]
    out_ref[...] = unpacked(total)
    for i in range(0, n // STEP, 8):
        eliminate(out_ref, n, (i, i + 8))
    out_ref[...] = jnp.where(r >= c, out_ref[...], 0.0)


def middle_kernel(steps, m_ref, out_ref):
    out_ref[...] = m_ref[...]
    eliminate(out_ref, m_ref.shape[0], steps)


def rows_kernel(shape, arrived_ref, mirrored_ref, kept_ref, rows_ref, parts_ref):
    blocks, held, tile = shape
    slab = blocks * held
    kept = kept_ref[...] > 0.0
    for c in range(arrived_ref.shape[0]):
        for m in range(blocks):
            x = arrived_ref[c, m * held:(m + 1) * held, :]
            if m == 0:
                x = jnp.where(kept, x, 0.0)
            rows_ref[pl.ds(m * tile + c * held, held), :] = x
    gram = packed(mm_tn(rows_ref[...], rows_ref[...]))
    for i in range(parts_ref.shape[0]):
        parts_ref[i, :slab, :] = mirrored_ref[...]
        parts_ref[i, slab:, :] = gram


def columns_kernel(shape, mine_ref, theirs_ref, even_ref, kept_ref, columns_ref):
    far, near, blocks, held, tile = shape
    even = even_ref[...] > 0.0
    kept = kept_ref[...] > 0.0
    for i in range(far):
        for z in range(near):
            for m in range(blocks):
                a = mine_ref[i * near + z, m * held:(m + 1) * held, :]
                b = theirs_ref[i * near + z, m * held:(m + 1) * held, :]
                pair = jnp.concatenate([jnp.where(even, a, b), jnp.where(even, b, a)], 0)
                if m == 0 and i == 0:
                    pair = jnp.where(kept, pair, 0.0)
                columns_ref[pl.ds((m * far + i) * tile + z * 2 * held, 2 * held), :] = pair


def product_kernel(held, a_ref, columns_ref, sent_ref):
    tile = columns_ref.shape[1] // 2
    blocks = a_ref.shape[0] // tile
    slab = blocks * held
    columns = columns_ref[...]
    for m in range(blocks):
        u = mm(a_ref[m * tile:(m + 1) * tile, :], columns)
        for i in range(sent_ref.shape[0]):
            sent_ref[i, m * held:(m + 1) * held, :] = u[i * held:(i + 1) * held, :]
    for i in range(sent_ref.shape[0]):
        sent_ref[i, slab:, :] = columns_ref[:tile, :]


def spread(x, parts_ref):
    for i in range(parts_ref.shape[0]):
        parts_ref[i] = x


def gram_kernel(columns_ref, parts_ref):
    spread(packed(mm_tn(columns_ref[...], columns_ref[...])), parts_ref)


def inner_kernel(shape, y_ref, arrived_ref, parts_ref, *gathered_refs):
    blocks, held, tile = shape
    u_ref = gathered_refs[0]
    for k, rows_ref in enumerate(gathered_refs):
        for c in range(arrived_ref.shape[0]):
            for m in range(blocks):
                at = (k * blocks + m) * held
                rows_ref[pl.ds(m * tile + c * held, held), :] = arrived_ref[c, at:at + held, :]
    half = packed(mm_tn(y_ref[...], u_ref[...]))
    for i in range(parts_ref.shape[0]):
        parts_ref[i, :half.shape[0], :] = half
        if len(gathered_refs) > 1:
            parts_ref[i, half.shape[0]:, :] = u_ref[:tile, :]


def reflect_kernel(first, slab, inside, arrived_ref, inverse_ref, edge_ref, sign_ref, turned_ref, top_ref, parts_ref, own_ref):
    n = inverse_ref.shape[0]
    r, c = square_places(n)
    tile = n // 2
    for i in range(2):
        top_ref[i * tile:(i + 1) * tile, :] = arrived_ref[first + i, slab:slab + tile, :]
    q1t = mm_nt(inverse_ref[...], top_ref[...])
    diagonal = jnp.sum(jnp.where(r == c, q1t, 0.0), axis=0, keepdims=True)
    sign = jnp.where(diagonal >= 0, -1.0, 1.0)
    sign_ref[...] = sign
    turned_ref[...] = jnp.where(r == c, q1t - sign, q1t)
    total = arrived_ref[0, :slab, :]
    for i in range(1, arrived_ref.shape[0]):
        total = total + arrived_ref[i, :slab, :]
    if inside:
        halves = [arrived_ref[first + i, slab + tile:slab + tile + slab // 2, :] for i in range(2)]
        edge = jnp.concatenate([jnp.concatenate([x[:, :tile], x[:, tile:]], 0) for x in halves], 1)
    else:
        edge = edge_ref[...]
        own_ref[:, n:] = edge
        for i in range(parts_ref.shape[0]):
            parts_ref[i, slab:, :] = edge
    own = mm_nt(total, inverse_ref[...]) - edge * sign
    own_ref[:, :n] = own
    for i in range(parts_ref.shape[0]):
        parts_ref[i, :slab, :] = own


def outer_first_kernel(steps, turned_ref, m_ref):
    m_ref[...] = mm_nt(turned_ref[...], turned_ref[...])
    eliminate(m_ref, m_ref.shape[0], steps)


def outer_last_kernel(steps, m_ref, turned_ref, sign_ref, tft_ref):
    n = m_ref.shape[0]
    r, c = square_places(n)
    tft_ref[...] = m_ref[...]
    eliminate(tft_ref, n, steps)
    root = jnp.where(r >= c, tft_ref[...], 0.0)
    tft_ref[...] = -mm(mm_tn(root, root), turned_ref[...]) * sign_ref[...]


def half_z_of(mine_ref, theirs_ref, tft_ref):
    return 0.5 * mm_nt(mm(tft_ref[...], unpacked(mine_ref[...] + theirs_ref[...])), tft_ref[...])


def top_z_kernel(mine_ref, theirs_ref, tft_ref, y_top_ref, a_ref, b_ref, even_ref, z_ref, side_ref):
    even = even_ref[...] > 0.0
    a, b = a_ref[...], b_ref[...]
    u_top = jnp.concatenate([jnp.where(even, a, b), jnp.where(even, b, a)], 0)
    z = half_z_of(mine_ref, theirs_ref, tft_ref)
    z = z + z.T
    z_ref[...] = z
    side_ref[...] = mm_nt(z, y_top_ref[...]) - mm_nt(tft_ref[...], u_top)


def whole_z_kernel(mine_ref, theirs_ref, tft_ref, z_ref):
    z = half_z_of(mine_ref, theirs_ref, tft_ref)
    z_ref[...] = z + z.T


def swap(x, axis):
    return lax.all_to_all(x, axis, 0, 0, tiled=True)


def gathered(x, axis):
    return swap(jnp.broadcast_to(x[None], (lax.axis_size(axis), *x.shape)), axis)


def other_core(x):
    return lax.ppermute(x, CORE, [(0, 1), (1, 0)])


def in_core_order(mine, core, axis):
    theirs = other_core(mine)
    first = core == 0
    return jnp.stack([jnp.where(first, mine, theirs), jnp.where(first, theirs, mine)], axis)


def to_mirror(piece):
    rows, cols = lax.axis_size(ROW), lax.axis_size(COL)
    pairs = []
    for r in range(rows):
        for c in range(cols):
            to_row, to_col = r // cols * cols + c, r % cols
            pairs.append((r * cols + c, to_row * cols + to_col))
    return lax.ppermute(piece, ROW + COL, pairs)


def cut_rows(x, blocks, peers):
    width = x.shape[-1]
    return x.reshape(blocks, peers, -1, width).transpose(1, 0, 2, 3).reshape(peers, -1, width)


def joined_rows(slabs, blocks):
    peers, _, width = slabs.shape
    return slabs.reshape(peers, blocks, -1, width).transpose(1, 0, 2, 3).reshape(-1, width)


def mirror_rows(mine, core, blocks):
    far, near = lax.axis_size("x_lo"), lax.axis_size("z")
    width = mine.shape[-1]
    both = in_core_order(mine.reshape(far, near, blocks, -1, width), core, 2)
    return both.transpose(3, 0, 1, 2, 4, 5).reshape(-1, width)


def untile_kernel(wide, tiles_ref, a_ref):
    rows, lanes = a_ref.shape[0], tiles_ref.shape[1]
    for n in range(wide):
        a_ref[:, n * lanes:(n + 1) * lanes] = tiles_ref[pl.ds(n, rows, stride=wide), :]


def untiled(matrix_tiles):
    blocks, _, tile, wide, _, lanes = matrix_tiles.shape
    return pl.pallas_call(
        functools.partial(untile_kernel, wide),
        grid=(blocks,),
        in_specs=[pl.BlockSpec((tile * wide, lanes), lambda i: (i, 0))],
        out_specs=pl.BlockSpec((tile, wide * lanes), lambda i: (i, 0)),
        out_shape=jax.ShapeDtypeStruct((blocks * tile, wide * lanes), jnp.float32),
        compiler_params=pltpu.CompilerParams(vmem_limit_bytes=16 * 2**20),
    )(matrix_tiles.reshape(blocks * tile * wide, lanes))


def tile_kernel(wide, a_ref, tiles_ref):
    rows, lanes = a_ref.shape[0], tiles_ref.shape[1]
    for n in range(wide):
        tiles_ref[pl.ds(n, rows, stride=wide), :] = a_ref[:, n * lanes:(n + 1) * lanes]


def tiled(a, shape):
    blocks, _, tile, wide, _, lanes = shape
    return pl.pallas_call(
        functools.partial(tile_kernel, wide),
        grid=(blocks,),
        in_specs=[pl.BlockSpec((tile, wide * lanes), lambda i: (i, 0))],
        out_specs=pl.BlockSpec((tile * wide, lanes), lambda i: (i, 0)),
        out_shape=jax.ShapeDtypeStruct((blocks * tile * wide, lanes), jnp.float32),
        compiler_params=pltpu.CompilerParams(vmem_limit_bytes=16 * 2**20),
    )(a).reshape(shape)


def after(x, other):
    return lax.optimization_barrier((x, other))[0]


def on_device(matrix_tiles):
    tile_shape = matrix_tiles.shape
    blocks, tile, wide = tile_shape[0], tile_shape[2], tile_shape[3]
    band = 2 * tile
    rows, cols = lax.axis_size(ROW), lax.axis_size(COL)
    r, c, core = lax.axis_index(ROW), lax.axis_index(COL), lax.axis_index(CORE)
    a = untiled(matrix_tiles)
    slab = blocks * tile // cols
    part = band // cols
    lane = jnp.arange(band, dtype=jnp.int32)

    def places(count, peers, me):
        at = jnp.arange(count, dtype=jnp.int32)
        return (at // tile * peers + me) * tile + at % tile

    def pair(source, first):
        return jnp.concatenate([source[first], source[first + 1]], 1)

    def cleared(x, at, below):
        return jnp.where((at >= below)[:, None], x, 0.0)

    row_of, col_of = places(blocks * tile, rows, r), places(wide * tile, cols, c)

    source = swap(cut_rows(a[:, :tile], blocks, cols), COL)
    p_own, next_own = pair(source, 0), pair(source, 2)
    def flag(x):
        return jnp.broadcast_to(x.astype(jnp.float32), (1, band))

    far, near, held = lax.axis_size("x_lo"), lax.axis_size("z"), tile // cols
    packs = (cols, band // 2 + STEP, band)
    mirrored = to_mirror(p_own)
    arrived = gathered(p_own, COL)
    p_rows, sent = call(
        functools.partial(rows_kernel, (blocks, held, tile)),
        [(blocks * tile, band), (cols, slab + packs[1], band)],
        arrived, mirrored, flag(r >= band // tile), flops=10**9,
    )
    arrived = swap(sent, PAIR)
    gram = arrived[:, slab:].sum(0)
    mine = arrived[:, :slab]
    parts = jnp.stack([gram, other_core(gram)])
    (p_cols,) = call(
        functools.partial(columns_kernel, (far, near, blocks, held, tile)),
        [(wide * tile, band)], mine, other_core(mine), flag(core == 0), flag(c >= band // tile), flops=10**9,
    )
    square = (band, band)
    third = band // STEP // 3 + 1
    for panel in range(PANELS):
        below = (panel + 1) * band
        first = below // tile
        if panel:
            (parts,) = call(gram_kernel, [packs], p_cols, flops=10**9)
            a = after(a, parts) - update(left, right) + update(mm(y_rows, after(z, parts)), y_cols)
            parts = swap(parts, COL)
        (inverse,) = call(whole_kernel, [square], parts)
        if panel:
            x_rows, side = after((x_rows, side), inverse)
            p_rows = cleared(more[0] - mm_nt(x_rows, y_top) + mm(y_rows, side), row_of, below)

        if panel:
            edge = cut_rows(a[:, :tile], blocks, cols)
            sent = jnp.concatenate([
                cut_rows(mm(a, p_cols), blocks, cols),
                jnp.broadcast_to(p_cols[None, :tile], (cols, tile, band)),
                jnp.concatenate([edge[:, :slab // 2], edge[:, slab // 2:]], 2),
            ], 1)
        else:
            (sent,) = call(
                functools.partial(product_kernel, held), [(cols, slab + tile, band)], a, p_cols, flops=10**9,
            )
        arrived = swap(sent, COL)
        arrived, inverse = after((arrived, inverse), inverse)
        sign, turned, top, u_parts, u_own = call(
            functools.partial(reflect_kernel, first, slab, panel > 0),
            [(1, band), square, square, (cols, slab if panel else 2 * slab, band), (slab, band if panel else 2 * band)],
            arrived, inverse, next_own, flops=10**9,
        )
        def signs_at(at):
            return jnp.where(at[:, None] - below == lane[None, :], sign, 0.0)

        y_rows = mm_nt(p_rows, inverse) - signs_at(row_of)
        y_cols = mm_nt(p_cols, inverse) - signs_at(col_of)
        if panel == 0:
            y_rows, turned = after((y_rows, turned), y_rows)
        mirrored = to_mirror(u_own)
        arrived = swap(u_parts, COL)
        (m1,) = call(functools.partial(outer_first_kernel, (0, third)), [square], turned)
        arrived, m1 = after((arrived, m1), m1)
        mirrored, m1 = after((mirrored, m1), arrived)
        inner, u_rows, *more = call(
            functools.partial(inner_kernel, (blocks, held, tile)),
            [packs if panel else (cols, packs[1] + tile, band)] + [(blocks * tile, band)] * (1 if panel else 2),
            y_rows, arrived, flops=10**9,
        )
        if panel == 0:
            mirrored = jnp.concatenate([mirrored[:, :band], mirrored[:, band:]], 0)
        arrived = gathered(after(mirrored, m1), PAIR)
        m1 = after(m1, (inner, y_cols))
        (m2,) = call(functools.partial(middle_kernel, (third, 2 * third)), [square], m1)
        arrived, m2 = after((arrived, m2), m2)
        inner = swap(after(inner, arrived), PAIR)
        (tft,) = call(functools.partial(outer_last_kernel, (2 * third, band // STEP)), [square], after(m2, arrived), turned, sign, flops=10**6)
        u_cols = mirror_rows(arrived[:, :slab], core, blocks)
        x_rows, x_cols = mm_nt(u_rows, tft), mm_nt(u_cols, tft)
        left, right = jnp.concatenate([y_rows, x_rows], 1), jnp.concatenate([x_cols, y_cols], 1)
        if panel == 0:
            next_cols = mirror_rows(arrived[:, slab:], core, blocks)
            y_top = mm_nt(top, inverse) - jnp.where(jnp.eye(band, dtype=bool), sign, 0.0)
            p_cols = next_cols - mm_nt(x_cols, y_top)
            inner, p_cols, x_rows = after((inner, p_cols, x_rows), (p_cols, x_rows))
        else:
            a = a - update(left, right)
            inner, a = after((inner, a), a)
        mine = inner[:, :packs[1]].sum(0)
        theirs = other_core(mine)
        if panel == 0:
            u_top = inner[first // 2, packs[1]:]
            z, side = call(
                top_z_kernel, [square, square], mine, theirs, tft, y_top, u_top, other_core(u_top), flag(core == 0),
                flops=10**9,
            )
            p_cols = cleared(p_cols + mm(y_cols, side), col_of, below + band)
        else:
            (z,) = call(whole_z_kernel, [square], mine, theirs, tft, flops=10**9)
            a = a + update(mm(y_rows, z), y_cols)
    return tiled(a, tile_shape)


def solution(mesh):
    finer = Mesh(mesh.devices.reshape(2, 4, 2, 2, 4), ("x_lo", "z", "core", "x_hi", "y"))
    spec = P(None, ROW, None, None, COL, None)
    return jax.shard_map(on_device, mesh=finer, in_specs=(spec,), out_specs=spec, check_vma=False)
```

```python
import functools

import jax
import jax.numpy as jnp
from jax import lax
from jax.experimental import pallas as pl
from jax.experimental.pallas import tpu as pltpu
from jax.sharding import Mesh
from jax.sharding import PartitionSpec as P

PANELS = 2
PAIR = ("x_lo", "z")
CORE = "core"
ROW = ("x_lo", "z", "core")
COL = ("x_hi", "y")
HI = lax.Precision.HIGHEST


def mm(a, b):
    return lax.dot_general(a, b, (((1,), (0,)), ((), ())), precision=HI, preferred_element_type=jnp.float32)


def mm_nt(a, b):
    return lax.dot_general(a, b, (((1,), (1,)), ((), ())), precision=HI, preferred_element_type=jnp.float32)


def update(a, b):
    return lax.dot_general(
        a, b, (((1,), (1,)), ((), ())), precision=lax.Precision.HIGH, preferred_element_type=jnp.float32
    )


def mm_tn(a, b):
    return lax.dot_general(a, b, (((0,), (0,)), ((), ())), precision=HI, preferred_element_type=jnp.float32)


STEP = 8


def entries(block):
    columns = [jnp.broadcast_to(block[:, j:j + 1], (STEP, 128)) for j in range(STEP)]
    return [[jnp.broadcast_to(columns[j][i:i + 1, :], (STEP, 128)) if j <= i else None for j in range(STEP)] for i in range(STEP)]


def inverse_root(a):
    y = lax.rsqrt(a)
    return y * (1.5 - (0.5 * a) * (y * y))


def chol_inverse_8(a):
    a = [list(row) for row in a]
    x = [[None] * STEP for _ in range(STEP)]
    for k in range(STEP):
        x[k][k] = inverse_root(a[k][k])
        for i in range(k + 1, STEP):
            a[i][k] = a[i][k] * x[k][k]
        for j in range(k + 1, STEP):
            for i in range(j, STEP):
                a[i][j] = a[i][j] - a[i][k] * a[j][k]
    for k in range(STEP):
        for j in range(k):
            s = a[k][j] * x[j][j]
            for q in range(j + 1, k):
                s = s + a[k][q] * x[q][j]
            x[k][j] = -s * x[k][k]
    return x


def apply_lower(x, rows, sub):
    columns = []
    for j in range(STEP):
        col = x[STEP - 1][j]
        for i in range(STEP - 2, j - 1, -1):
            col = jnp.where(sub == i, x[i][j], col)
        columns.append(jnp.where(sub >= j, col, 0.0) if j else col)
    parts = []
    for c in range(0, rows.shape[1], 128):
        terms = [columns[j] * rows[j:j + 1, c:c + 128] for j in range(STEP)]
        while len(terms) > 1:
            terms = [terms[i] + terms[i + 1] for i in range(0, len(terms), 2)]
        parts.append(terms[0])
    return jnp.concatenate(parts, 1)


def three(x):
    hi = x.astype(jnp.bfloat16).astype(jnp.float32)
    rest = x - hi
    mid = rest.astype(jnp.bfloat16).astype(jnp.float32)
    return hi, mid, rest - mid


def outer(left, right):
    a, b, c = three(left)
    d, e, f = three(right)
    lefts = jnp.concatenate([a, a, b, a, c, b], 0).astype(jnp.bfloat16)
    rights = jnp.concatenate([d, e, d, f, d, e], 0).astype(jnp.bfloat16)
    return lax.dot_general(lefts, rights, (((0,), (0,)), ((), ())), preferred_element_type=jnp.float32)


def eliminate(m_ref, n, steps):
    lanes8 = lax.broadcasted_iota(jnp.int32, (STEP, n), 1)
    subs8 = lax.broadcasted_iota(jnp.int32, (STEP, n), 0)
    sub = lax.broadcasted_iota(jnp.int32, (STEP, 128), 0)
    low = steps[0] * STEP
    lanes = lax.broadcasted_iota(jnp.int32, (n - low, n), 1)
    rows_of = lax.broadcasted_iota(jnp.int32, (n - low, n), 0) + low

    def body(k, _):
        at = pl.multiple_of(k * STEP, STEP)
        rows = m_ref[pl.ds(at, STEP), :]
        block = pltpu.roll(rows, n - at, 1)[:, :STEP]
        here = (lanes8 >= at) & (lanes8 < at + STEP)
        unit = jnp.where(here, (lanes8 - at == subs8).astype(jnp.float32), rows)
        kept = apply_lower(chol_inverse_8(entries(block)), unit, sub)
        m_ref[pl.ds(at, STEP), :] = kept
        m = m_ref[low:, :]
        cleared = (lanes >= at) & (lanes < at + STEP) & (rows_of >= at + STEP)
        left = jnp.where(lanes8 >= at + STEP, kept, 0.0)
        m_ref[low:, :] = jnp.where(cleared, 0.0, m) - outer(left, kept)[low:, :]
        return 0

    lax.fori_loop(*steps, body, 0)


def square_places(n):
    return lax.broadcasted_iota(jnp.int32, (n, n), 0), lax.broadcasted_iota(jnp.int32, (n, n), 1)


def packed(m):
    h = m.shape[0] // 2
    r, c = square_places(h)
    low, high = m[:h, :h], m[h:, h:]
    diagonal = jnp.sum(jnp.where(r == c, high, 0.0), axis=0, keepdims=True)
    last = jnp.pad(diagonal, ((0, STEP - 1), (0, h)))
    return jnp.concatenate([jnp.concatenate([m[h:, :h], jnp.where(r >= c, low, high)], 1), last], 0)


def unpacked(p):
    h = p.shape[1] // 2
    r, c = square_places(h)
    corner, both, diagonal = p[:h, :h], p[:h, h:], p[h:h + 1, :h]
    flipped = both.T
    low = jnp.where(r >= c, both, flipped)
    high = jnp.where(r == c, diagonal, jnp.where(r < c, both, flipped))
    return jnp.concatenate(
        [jnp.concatenate([low, corner.T], 1), jnp.concatenate([corner, high], 1)], 0
    )


def call(kernel, shapes, *operands, flops=10**10):
    return pl.pallas_call(
        kernel,
        out_shape=[jax.ShapeDtypeStruct(s, jnp.float32) for s in shapes],
        compiler_params=pltpu.CompilerParams(vmem_limit_bytes=24 * 2**20),
        cost_estimate=pl.CostEstimate(flops=flops, bytes_accessed=2**20, transcendentals=0),
    )(*operands)


def whole_kernel(parts_ref, out_ref):
    n = out_ref.shape[0]
    r, c = square_places(n)
    total = parts_ref[0]
    for i in range(1, parts_ref.shape[0]):
        total = total + parts_ref[i]
    out_ref[...] = unpacked(total)
    for i in range(0, n // STEP, 8):
        eliminate(out_ref, n, (i, i + 8))
    out_ref[...] = jnp.where(r >= c, out_ref[...], 0.0)


def middle_kernel(steps, m_ref, out_ref):
    out_ref[...] = m_ref[...]
    eliminate(out_ref, m_ref.shape[0], steps)


def rows_kernel(shape, arrived_ref, mirrored_ref, kept_ref, rows_ref, parts_ref):
    blocks, held, tile = shape
    slab = blocks * held
    kept = kept_ref[...] > 0.0
    for c in range(arrived_ref.shape[0]):
        for m in range(blocks):
            x = arrived_ref[c, m * held:(m + 1) * held, :]
            if m == 0:
                x = jnp.where(kept, x, 0.0)
            rows_ref[pl.ds(m * tile + c * held, held), :] = x
    gram = packed(mm_tn(rows_ref[...], rows_ref[...]))
    for i in range(parts_ref.shape[0]):
        parts_ref[i, :slab, :] = mirrored_ref[...]
        parts_ref[i, slab:, :] = gram


def columns_kernel(shape, mine_ref, theirs_ref, even_ref, kept_ref, columns_ref):
    far, near, blocks, held, tile = shape
    even = even_ref[...] > 0.0
    kept = kept_ref[...] > 0.0
    for i in range(far):
        for z in range(near):
            for m in range(blocks):
                a = mine_ref[i * near + z, m * held:(m + 1) * held, :]
                b = theirs_ref[i * near + z, m * held:(m + 1) * held, :]
                pair = jnp.concatenate([jnp.where(even, a, b), jnp.where(even, b, a)], 0)
                if m == 0 and i == 0:
                    pair = jnp.where(kept, pair, 0.0)
                columns_ref[pl.ds((m * far + i) * tile + z * 2 * held, 2 * held), :] = pair


def product_kernel(held, a_ref, columns_ref, sent_ref):
    tile = columns_ref.shape[1] // 2
    blocks = a_ref.shape[0] // tile
    slab = blocks * held
    columns = columns_ref[...]
    for m in range(blocks):
        u = mm(a_ref[m * tile:(m + 1) * tile, :], columns)
        for i in range(sent_ref.shape[0]):
            sent_ref[i, m * held:(m + 1) * held, :] = u[i * held:(i + 1) * held, :]
    for i in range(sent_ref.shape[0]):
        sent_ref[i, slab:, :] = columns_ref[:tile, :]


def spread(x, parts_ref):
    for i in range(parts_ref.shape[0]):
        parts_ref[i] = x


def gram_kernel(columns_ref, parts_ref):
    spread(packed(mm_tn(columns_ref[...], columns_ref[...])), parts_ref)


def inner_kernel(shape, y_ref, arrived_ref, parts_ref, *gathered_refs):
    blocks, held, tile = shape
    u_ref = gathered_refs[0]
    for k, rows_ref in enumerate(gathered_refs):
        for c in range(arrived_ref.shape[0]):
            for m in range(blocks):
                at = (k * blocks + m) * held
                rows_ref[pl.ds(m * tile + c * held, held), :] = arrived_ref[c, at:at + held, :]
    half = packed(mm_tn(y_ref[...], u_ref[...]))
    for i in range(parts_ref.shape[0]):
        parts_ref[i, :half.shape[0], :] = half
        if len(gathered_refs) > 1:
            parts_ref[i, half.shape[0]:, :] = u_ref[:tile, :]


def reflect_kernel(first, slab, inside, arrived_ref, inverse_ref, edge_ref, sign_ref, turned_ref, top_ref, parts_ref, own_ref):
    n = inverse_ref.shape[0]
    r, c = square_places(n)
    tile = n // 2
    for i in range(2):
        top_ref[i * tile:(i + 1) * tile, :] = arrived_ref[first + i, slab:slab + tile, :]
    q1t = mm_nt(inverse_ref[...], top_ref[...])
    diagonal = jnp.sum(jnp.where(r == c, q1t, 0.0), axis=0, keepdims=True)
    sign = jnp.where(diagonal >= 0, -1.0, 1.0)
    sign_ref[...] = sign
    turned_ref[...] = jnp.where(r == c, q1t - sign, q1t)
    total = arrived_ref[0, :slab, :]
    for i in range(1, arrived_ref.shape[0]):
        total = total + arrived_ref[i, :slab, :]
    if inside:
        halves = [arrived_ref[first + i, slab + tile:slab + tile + slab // 2, :] for i in range(2)]
        edge = jnp.concatenate([jnp.concatenate([x[:, :tile], x[:, tile:]], 0) for x in halves], 1)
    else:
        edge = edge_ref[...]
        own_ref[:, n:] = edge
        for i in range(parts_ref.shape[0]):
            parts_ref[i, slab:, :] = edge
    own = mm_nt(total, inverse_ref[...]) - edge * sign
    own_ref[:, :n] = own
    for i in range(parts_ref.shape[0]):
        parts_ref[i, :slab, :] = own


def outer_first_kernel(steps, turned_ref, m_ref):
    m_ref[...] = mm_nt(turned_ref[...], turned_ref[...])
    eliminate(m_ref, m_ref.shape[0], steps)


def outer_last_kernel(steps, m_ref, turned_ref, sign_ref, tft_ref):
    n = m_ref.shape[0]
    r, c = square_places(n)
    tft_ref[...] = m_ref[...]
    eliminate(tft_ref, n, steps)
    root = jnp.where(r >= c, tft_ref[...], 0.0)
    tft_ref[...] = -mm(mm_tn(root, root), turned_ref[...]) * sign_ref[...]


def half_z_of(mine_ref, theirs_ref, tft_ref):
    return 0.5 * mm_nt(mm(tft_ref[...], unpacked(mine_ref[...] + theirs_ref[...])), tft_ref[...])


def top_z_kernel(mine_ref, theirs_ref, tft_ref, y_top_ref, a_ref, b_ref, even_ref, z_ref, side_ref):
    even = even_ref[...] > 0.0
    a, b = a_ref[...], b_ref[...]
    u_top = jnp.concatenate([jnp.where(even, a, b), jnp.where(even, b, a)], 0)
    z = half_z_of(mine_ref, theirs_ref, tft_ref)
    z_ref[...] = z
    side_ref[...] = mm_nt(z + z.T, y_top_ref[...]) - mm_nt(tft_ref[...], u_top)


def whole_z_kernel(mine_ref, theirs_ref, tft_ref, z_ref):
    z = half_z_of(mine_ref, theirs_ref, tft_ref)
    z_ref[...] = z + z.T


def swap(x, axis):
    return lax.all_to_all(x, axis, 0, 0, tiled=True)


def gathered(x, axis):
    return swap(jnp.broadcast_to(x[None], (lax.axis_size(axis), *x.shape)), axis)


def other_core(x):
    return lax.ppermute(x, CORE, [(0, 1), (1, 0)])


def in_core_order(mine, core, axis):
    theirs = other_core(mine)
    first = core == 0
    return jnp.stack([jnp.where(first, mine, theirs), jnp.where(first, theirs, mine)], axis)


def to_mirror(piece):
    rows, cols = lax.axis_size(ROW), lax.axis_size(COL)
    pairs = []
    for r in range(rows):
        for c in range(cols):
            to_row, to_col = r // cols * cols + c, r % cols
            pairs.append((r * cols + c, to_row * cols + to_col))
    return lax.ppermute(piece, ROW + COL, pairs)


def cut_rows(x, blocks, peers):
    width = x.shape[-1]
    return x.reshape(blocks, peers, -1, width).transpose(1, 0, 2, 3).reshape(peers, -1, width)


def joined_rows(slabs, blocks):
    peers, _, width = slabs.shape
    return slabs.reshape(peers, blocks, -1, width).transpose(1, 0, 2, 3).reshape(-1, width)


def mirror_rows(mine, core, blocks):
    far, near = lax.axis_size("x_lo"), lax.axis_size("z")
    width = mine.shape[-1]
    both = in_core_order(mine.reshape(far, near, blocks, -1, width), core, 2)
    return both.transpose(3, 0, 1, 2, 4, 5).reshape(-1, width)


def untile_kernel(wide, tiles_ref, a_ref):
    rows, lanes = a_ref.shape[0], tiles_ref.shape[1]
    for n in range(wide):
        a_ref[:, n * lanes:(n + 1) * lanes] = tiles_ref[pl.ds(n, rows, stride=wide), :]


def untiled(matrix_tiles):
    blocks, _, tile, wide, _, lanes = matrix_tiles.shape
    return pl.pallas_call(
        functools.partial(untile_kernel, wide),
        grid=(blocks,),
        in_specs=[pl.BlockSpec((tile * wide, lanes), lambda i: (i, 0))],
        out_specs=pl.BlockSpec((tile, wide * lanes), lambda i: (i, 0)),
        out_shape=jax.ShapeDtypeStruct((blocks * tile, wide * lanes), jnp.float32),
        compiler_params=pltpu.CompilerParams(vmem_limit_bytes=16 * 2**20),
    )(matrix_tiles.reshape(blocks * tile * wide, lanes))


def tile_kernel(wide, a_ref, tiles_ref):
    rows, lanes = a_ref.shape[0], tiles_ref.shape[1]
    for n in range(wide):
        tiles_ref[pl.ds(n, rows, stride=wide), :] = a_ref[:, n * lanes:(n + 1) * lanes]


def tiled(a, shape):
    blocks, _, tile, wide, _, lanes = shape
    return pl.pallas_call(
        functools.partial(tile_kernel, wide),
        grid=(blocks,),
        in_specs=[pl.BlockSpec((tile, wide * lanes), lambda i: (i, 0))],
        out_specs=pl.BlockSpec((tile * wide, lanes), lambda i: (i, 0)),
        out_shape=jax.ShapeDtypeStruct((blocks * tile * wide, lanes), jnp.float32),
        compiler_params=pltpu.CompilerParams(vmem_limit_bytes=16 * 2**20),
    )(a).reshape(shape)


def after(x, other):
    return lax.optimization_barrier((x, other))[0]


def on_device(matrix_tiles):
    tile_shape = matrix_tiles.shape
    blocks, tile, wide = tile_shape[0], tile_shape[2], tile_shape[3]
    band = 2 * tile
    rows, cols = lax.axis_size(ROW), lax.axis_size(COL)
    r, c, core = lax.axis_index(ROW), lax.axis_index(COL), lax.axis_index(CORE)
    a = untiled(matrix_tiles)
    slab = blocks * tile // cols
    part = band // cols
    lane = jnp.arange(band, dtype=jnp.int32)

    def places(count, peers, me):
        at = jnp.arange(count, dtype=jnp.int32)
        return (at // tile * peers + me) * tile + at % tile

    def pair(source, first):
        return jnp.concatenate([source[first], source[first + 1]], 1)

    def cleared(x, at, below):
        return jnp.where((at >= below)[:, None], x, 0.0)

    row_of, col_of = places(blocks * tile, rows, r), places(wide * tile, cols, c)

    source = swap(cut_rows(a[:, :tile], blocks, cols), COL)
    p_own, next_own = pair(source, 0), pair(source, 2)
    def flag(x):
        return jnp.broadcast_to(x.astype(jnp.float32), (1, band))

    far, near, held = lax.axis_size("x_lo"), lax.axis_size("z"), tile // cols
    packs = (cols, band // 2 + STEP, band)
    mirrored = to_mirror(p_own)
    arrived = gathered(p_own, COL)
    p_rows, sent = call(
        functools.partial(rows_kernel, (blocks, held, tile)),
        [(blocks * tile, band), (cols, slab + packs[1], band)],
        arrived, mirrored, flag(r >= band // tile), flops=10**9,
    )
    arrived = swap(sent, PAIR)
    gram = arrived[:, slab:].sum(0)
    mine = arrived[:, :slab]
    parts = jnp.stack([gram, other_core(gram)])
    (p_cols,) = call(
        functools.partial(columns_kernel, (far, near, blocks, held, tile)),
        [(wide * tile, band)], mine, other_core(mine), flag(core == 0), flag(c >= band // tile), flops=10**9,
    )
    square = (band, band)
    third = band // STEP // 3 + 1
    for panel in range(PANELS):
        below = (panel + 1) * band
        first = below // tile
        if panel:
            (parts,) = call(gram_kernel, [packs], p_cols, flops=10**9)
            late_z, x_cols, u_rows, tft = after((half_z, x_cols, u_rows, tft), parts)
            x_rows = mm_nt(u_rows, tft)
            left = jnp.concatenate([y_rows, x_rows - mm(y_rows, late_z)], 1)
            a = a - update(left, jnp.concatenate([x_cols - mm(y_cols, late_z), y_cols], 1))
            parts = swap(parts, COL)
        (inverse,) = call(whole_kernel, [square], parts)
        if panel:
            x_rows, side = after((x_rows, side), inverse)
            p_rows = cleared(more[0] - mm_nt(x_rows, y_top) + mm(y_rows, side), row_of, below)

        if panel:
            edge = cut_rows(a[:, :tile], blocks, cols)
            sent = jnp.concatenate([
                cut_rows(mm(a, p_cols), blocks, cols),
                jnp.broadcast_to(p_cols[None, :tile], (cols, tile, band)),
                jnp.concatenate([edge[:, :slab // 2], edge[:, slab // 2:]], 2),
            ], 1)
        else:
            (sent,) = call(
                functools.partial(product_kernel, held), [(cols, slab + tile, band)], a, p_cols, flops=10**9,
            )
        arrived = swap(sent, COL)
        arrived, inverse = after((arrived, inverse), inverse)
        sign, turned, top, u_parts, u_own = call(
            functools.partial(reflect_kernel, first, slab, panel > 0),
            [(1, band), square, square, (cols, slab if panel else 2 * slab, band), (slab, band if panel else 2 * band)],
            arrived, inverse, next_own, flops=10**9,
        )
        def signs_at(at):
            return jnp.where(at[:, None] - below == lane[None, :], sign, 0.0)

        y_rows = mm_nt(p_rows, inverse) - signs_at(row_of)
        y_cols = mm_nt(p_cols, inverse) - signs_at(col_of)
        if panel == 0:
            y_rows, turned = after((y_rows, turned), y_rows)
        mirrored = to_mirror(u_own)
        arrived = swap(u_parts, COL)
        (m1,) = call(functools.partial(outer_first_kernel, (0, third)), [square], turned)
        arrived, m1 = after((arrived, m1), m1)
        mirrored, m1 = after((mirrored, m1), arrived)
        inner, u_rows, *more = call(
            functools.partial(inner_kernel, (blocks, held, tile)),
            [packs if panel else (cols, packs[1] + tile, band)] + [(blocks * tile, band)] * (1 if panel else 2),
            y_rows, arrived, flops=10**9,
        )
        if panel == 0:
            mirrored = jnp.concatenate([mirrored[:, :band], mirrored[:, band:]], 0)
        arrived = gathered(after(mirrored, m1), PAIR)
        m1 = after(m1, (inner, y_cols) if panel else inner)
        (m2,) = call(functools.partial(middle_kernel, (third, 2 * third)), [square], m1)
        arrived, m2 = after((arrived, m2), m2)
        inner = swap(after(inner, arrived), PAIR)
        (tft,) = call(functools.partial(outer_last_kernel, (2 * third, band // STEP)), [square], after(m2, arrived), turned, sign, flops=10**6)
        u_cols = mirror_rows(arrived[:, :slab], core, blocks)
        x_cols = mm_nt(u_cols, tft)
        if panel == 0:
            next_cols = mirror_rows(arrived[:, slab:], core, blocks)
            y_top = mm_nt(top, inverse) - jnp.where(jnp.eye(band, dtype=bool), sign, 0.0)
            p_cols = next_cols - mm_nt(x_cols, y_top)
            inner, p_cols = after((inner, p_cols), p_cols)
        else:
            x_rows = mm_nt(u_rows, tft)
            a = a - update(jnp.concatenate([y_rows, x_rows], 1), jnp.concatenate([x_cols, y_cols], 1))
            inner, a = after((inner, a), a)
        mine = inner[:, :packs[1]].sum(0)
        theirs = other_core(mine)
        if panel == 0:
            u_top = inner[first // 2, packs[1]:]
            half_z, side = call(
                top_z_kernel, [square, square], mine, theirs, tft, y_top, u_top, other_core(u_top), flag(core == 0),
                flops=10**9,
            )
            p_cols = cleared(p_cols + mm(y_cols, side), col_of, below + band)
        else:
            (z,) = call(whole_z_kernel, [square], mine, theirs, tft, flops=10**9)
            a = a + update(mm(y_rows, z), y_cols)
    return tiled(a, tile_shape)


def solution(mesh):
    finer = Mesh(mesh.devices.reshape(2, 4, 2, 2, 4), ("x_lo", "z", "core", "x_hi", "y"))
    spec = P(None, ROW, None, None, COL, None)
    return jax.shard_map(on_device, mesh=finer, in_specs=(spec,), out_specs=spec, check_vma=False)
```
